128 devices in a mesh: pb: 16 (over y, x), ga: 8 (over z, core).
Axes of the slice: x: 4, y: 4, z: 4, core: 2. Of those that a mesh axis runs over, the one named last changes fastest.
Arguments:
- irr_vectors: bfloat16 [8, 16384, 2048], P(None, ('pb', 'ga')), may hold values from -0.046875 to 0.046875
- inv_dielectric: bfloat16 [16, 2048, 2048], P('pb', 'ga'), may hold values from -0.125 to 0.125
- pair_density: bfloat16 [16, 16384, 512], P('pb', 'ga'), may hold values from -6 to 6
- minus_q: int32 [16], replicated, may hold values from 0 to 15, as said below
- sym_op: int32 [16], replicated, may hold values from 0 to 47
- rot_blocks: int32 [48, 128], replicated, may hold values from 0 to 127, as said below
- rot_rows: int32 [48, 128, 128], replicated, may hold values from 0 to 127, each once within a row
- phase_bits: int32 [48, 16384], replicated, may hold values 0 or 1
Outputs:
- screened_density: bfloat16 [16, 16384, 512], P('pb', 'ga')
The draws below stay inside these ranges and needn't reach their ends.
Inputs may be any that keep to these rules, and one draw needn't show every extreme that they name: minus_q pairs the q-points: minus_q[minus_q[q]] = q and minus_q[q] != q. Each row rot_blocks[o] is a permutation of the 128 blocks; among the 16 destination blocks a * 16 to a * 16 + 15 of any slab a, at most 3 have source blocks with one value of the source block index mod 8, and every slab of every operation reaches 3 for some value.
All inputs are finite; a program needn't handle non-finite values.
Results may differ from the reference program's by a relative error of at most 0.0056.
Values may be sent and summed in bfloat16 or wider, within the bound.
A program may use at most 128 MiB of HBM per device.

```python
import math
import jax
import jax.numpy as jnp
from jax import lax

NB = 2048
RB = 128
NP = 512
NIRR = 8
NOPS = 48
NQ = 16
NBLK = 128
NG = 16384
N_PB = 16
N_GA = 8


def draw_minus_q(key, part):
    key = jax.random.fold_in(key, 37)
    first_key, second_key = jax.random.split(key, 2)
    order = jax.random.permutation(first_key, NQ).astype(jnp.int32)
    order = jax.random.permutation(second_key, order).astype(jnp.int32)
    pairs = order.reshape(NQ // 2, 2)
    mates = jnp.zeros((NQ,), jnp.int32)
    mates = mates.at[pairs[:, 0]].set(pairs[:, 1])
    mates = mates.at[pairs[:, 1]].set(pairs[:, 0])
    return mates


def draw_rot_blocks(key, part):
    key = jax.random.fold_in(key, 23)

    def one_operation(subkey):
        first_key, second_key, third_key = jax.random.split(subkey, 3)
        picked = jax.random.permutation(first_key, N_GA)
        counts = jnp.arange(N_PB, dtype=jnp.int32) % N_GA
        counts = counts.at[picked[1]].set(picked[0])
        shifts = jax.random.permutation(second_key, counts)
        places = jnp.arange(NBLK, dtype=jnp.int32)
        source_ga = (places // N_PB + shifts[places % N_PB]) % N_GA
        earlier = (places[None, :] < places[:, None]) & (source_ga[None, :] == source_ga[:, None])
        ranks = jnp.sum(earlier.astype(jnp.int32), axis=1)
        pb_orders = jax.vmap(lambda sub: jax.random.permutation(sub, N_PB))(jax.random.split(third_key, N_GA))
        source_pb = pb_orders[source_ga, ranks]
        return (source_pb * N_GA + source_ga).astype(jnp.int32)
    return jax.vmap(one_operation)(jax.random.split(key, NOPS))


def set_ends(values, key, low, top_value):
    index_at = [jax.random.randint(jax.random.fold_in(key, axis), (), 0, length) for axis, length in enumerate(values.shape)]
    widest = values.shape.index(max(values.shape))
    beside = index_at[:widest] + [(index_at[widest] + 1) % values.shape[widest]] + index_at[widest + 1:]
    return values.at[tuple(index_at)].set(low).at[tuple(beside)].set(top_value)


def levels(stream_key, extent, shards, low, largest):
    loudness = 1.0
    for position, parts in shards:
        steps = jax.random.uniform(jax.random.fold_in(jax.random.fold_in(stream_key, 6), position), (parts,), jnp.float32, low / len(shards), largest / len(shards))
        loudness = loudness * jnp.repeat(jnp.exp(steps), extent[position] // parts).reshape((-1,) + (1,) * (len(extent) - 1 - position))
    return loudness


def noise(stream_key, shape, scale, reach, pieces=(), kind=jnp.bfloat16):
    entries = jax.random.normal(stream_key, shape, jnp.float32) * scale
    if len(pieces) > 0:
        entries = levels(stream_key, shape, pieces, -0.22, 0.18) * entries
    return jnp.clip(entries, min=-reach, max=reach).astype(kind)


def setup_inputs(seed: int = 0) -> dict:
    splits = jax.random.split(jax.random.key(seed), 9)
    irr_vectors = noise(splits[0], (NIRR, NG, NB), NG ** -0.5, 0.046875, ((1, 128),))
    inv_dielectric = noise(splits[1], (NQ, NB, NB), NB ** -0.5, 0.125, ((0, 16), (1, 8)))
    pair_density = noise(splits[2], (NQ, NG, NP), 1.0, 6.0, ((0, 16), (1, 8)))
    minus_q = draw_minus_q(jax.random.fold_in(splits[8], 71), 0)
    sym_op = set_ends(jax.random.randint(splits[4], (NQ,), 0, NOPS), jax.random.fold_in(splits[4], 1), 0, NOPS - 1).astype(jnp.int32)
    rot_blocks = draw_rot_blocks(jax.random.fold_in(splits[8], 71), 0)
    rot_rows = jax.vmap(lambda own: jax.random.permutation(own, RB))(jax.random.split(splits[6], NOPS * NBLK)).reshape((NOPS, NBLK, RB)).astype(jnp.int32)
    phase_bits = set_ends((jax.random.randint(splits[7], (NOPS, NG), 0, 2) < 1).astype(jnp.int32), jax.random.fold_in(splits[7], 1), 0, 1)
    return dict(irr_vectors=irr_vectors, inv_dielectric=inv_dielectric, pair_density=pair_density, minus_q=minus_q, sym_op=sym_op, rot_blocks=rot_blocks, rot_rows=rot_rows, phase_bits=phase_bits)


def reference(irr_vectors, inv_dielectric, pair_density, minus_q, sym_op, rot_blocks, rot_rows, phase_bits):
    ratio = math.sqrt(NG / NB)

    def one_point(qpoint):
        operation = sym_op[qpoint]
        which_irr = qpoint % NIRR
        source = (rot_blocks[operation][:, None] * RB + rot_rows[operation]).reshape(-1).astype(jnp.int32)
        signs = (1 - 2 * phase_bits[operation]).astype(irr_vectors.dtype)
        vectors = jnp.take(irr_vectors[which_irr], source, axis=0) * signs[:, None]
        coef = jnp.dot(vectors.T, pair_density[qpoint], preferred_element_type=jnp.float32).astype(jnp.bfloat16)
        own_term = jnp.dot(inv_dielectric[qpoint], coef, preferred_element_type=jnp.float32)
        other_term = jnp.dot(inv_dielectric[minus_q[qpoint]].T, coef, preferred_element_type=jnp.float32)
        screened = (0.5 * (own_term + other_term) - coef.astype(jnp.float32)).astype(jnp.bfloat16)
        return (jnp.dot(vectors, screened, preferred_element_type=jnp.float32) * ratio).astype(jnp.bfloat16)
    return lax.map(one_point, jnp.arange(NQ, dtype=jnp.int32))
```

```python
import math

import jax
import jax.numpy as jnp
from jax import lax
from jax.experimental import pallas as pl
from jax.experimental.pallas import tpu as pltpu
from jax.sharding import PartitionSpec as P

MESH = pl.DeviceIdType.MESH
NX = 4
NC = 2
SEMS = 200
CAP = 3
BF16 = jnp.bfloat16
F32 = jnp.float32


def dot_nt(a, b):
    return lax.dot_general(a, b, (((1,), (1,)), ((), ())), preferred_element_type=F32)


def kernel(
    ratio,
    irr,
    dmat,
    drows,
    density,
    row_table,
    bits,
    minus_q,
    block_of_slot,
    held_slot,
    held_of_slot,
    send_slot,
    out,
    held,
    fwd,
    via_x,
    rho_tx,
    rho_rx_low,
    rho_rx_high,
    rho_group,
    part_tx,
    part_rx,
    acc,
    acc2,
    core_rx,
    core_rx2,
    sum_tx,
    sum_tx2,
    sum_rx,
    sum_rx2,
    mate_sum,
    coef,
    slab_sum,
    own_d,
    spread,
    chosen,
    mate_rows,
    mate_cols,
    screened,
    mate_scr,
    res_low,
    res_high,
    mate_res,
    back_low,
    back_high,
    turn_back,
    local_sem,
    send_sem,
    recv_sem,
):
    q_count = lax.axis_size("pb")
    g_count = lax.axis_size("ga")
    pb = lax.axis_index("pb")
    ga = lax.axis_index("ga")
    y, x = pb // NX, pb % NX
    z, c = ga // NC, ga % NC
    z_count = g_count // NC
    sibling = z * NC + (1 - c)
    basis = own_d.shape[0]
    rows = row_table.shape[1]
    plus, minus, beyond = (lambda v: (v + 1) % NX), (lambda v: (v + 3) % NX), (lambda v: (v + 2) % NX)
    ahead, behind = (lambda v: (v + 1 + 2 * c) % NX), (lambda v: (v + 3 - 2 * c) % NX)
    up, down, across = plus(y), minus(y), beyond(y)
    parts = range(2)
    res = (res_low, res_high)
    rho_rx = (rho_rx_low, rho_rx_high)
    back = (back_low, back_high)
    wide = res_low.shape[1]
    started = []
    taken = [0]

    def sems(count):
        first = taken[0]
        taken[0] += count
        assert taken[0] <= SEMS
        return first

    def copy(src, dst, i, to):
        return pltpu.make_async_remote_copy(
            src_ref=src,
            dst_ref=dst,
            send_sem=send_sem.at[i],
            recv_sem=recv_sem.at[i],
            device_id=to,
            device_id_type=MESH,
        )

    def send(src, dst, i, to):
        one = copy(src, dst, i, to)
        one.start()
        started.append(one)

    def arrive(dst, i):
        copy(dst, dst, i, (pb, ga)).wait_recv()

    def on_x(t):
        return (y * NX + t, ga)

    def on_y(t):
        return (t * NX + x, ga)

    class Exchange:
        def __init__(self, me, to, src, dst, via):
            self.me, self.to, self.src, self.dst, self.via = me, to, src, dst, via
            self.i = sems(4)

        def start(self):
            me = self.me
            send(self.src(plus(me)), self.dst(me), self.i, self.to(plus(me)))
            send(self.src(minus(me)), self.dst(me), self.i + 1, self.to(minus(me)))
            send(self.src(beyond(me)), self.via, self.i + 2, self.to(ahead(me)))

        def forward(self):
            arrive(self.via, self.i + 2)
            send(self.via, self.dst(behind(self.me)), self.i + 3, self.to(ahead(self.me)))

        def from_minus(self):
            arrive(self.dst(minus(self.me)), self.i)

        def from_plus(self):
            arrive(self.dst(plus(self.me)), self.i + 1)

        def from_beyond(self):
            arrive(self.dst(beyond(self.me)), self.i + 3)

        def finish(self):
            self.from_minus()
            self.from_plus()
            self.from_beyond()

    load_rho = pltpu.make_async_copy(density, out, local_sem.at[0])
    load_rho.start()

    barrier = pltpu.get_barrier_semaphore()

    def greet_pb(d, carry):
        pl.semaphore_signal(
            barrier, inc=1, device_id=((pb + d) % q_count, ga), device_id_type=MESH
        )
        return carry

    def greet_ga(d, carry):
        pl.semaphore_signal(
            barrier, inc=1, device_id=(pb, (ga + d) % g_count), device_id_type=MESH
        )
        return carry

    lax.fori_loop(1, q_count, greet_pb, 0)
    lax.fori_loop(1, g_count, greet_ga, 0)
    pl.semaphore_wait(barrier, q_count + g_count - 2)

    own_irr = NX * (y % 2)
    next_irr = NX * ((y + 1) % 2)
    next_x = Exchange(x, on_x, lambda t: irr.at[next_irr + t], lambda s: fwd.at[s], via_x.at[0])
    own_x = Exchange(x, on_x, lambda t: irr.at[own_irr + t], lambda s: held.at[y, s], via_x.at[1])
    next_x.start()
    keep = pltpu.make_async_copy(irr.at[own_irr + x], held.at[y, x], local_sem.at[1])
    keep.start()
    y_sem = sems(8)

    def to_neighbours(k, source, src):
        there = held.at[y, source]
        send(src, there, y_sem + k, on_y(up))
        send(src, there, y_sem + 4 + k, on_y(down))

    to_neighbours(0, x, irr.at[next_irr + x])

    def turn_of(j):
        sources = lax.broadcasted_iota(jnp.int32, (rows, rows), 0)
        sign = (1 - 2 * bits[pl.ds(j, 1), :]).astype(F32)
        return jnp.where(row_table[pl.ds(j, 1), :] == sources, sign, 0.0)

    load_rho.wait()
    rho_sem = sems(2 * g_count)

    def rho_copy(h, d):
        to = (ga + d) % g_count
        return copy(
            rho_tx.at[h, pl.ds(to * CAP, CAP)],
            rho_rx[h].at[pl.ds(ga * CAP, CAP)],
            rho_sem + h * g_count + d,
            (pb, to),
        )

    for h in parts:

        def make_turned(j, carry):
            value = jnp.dot(
                turn_of(j).astype(BF16),
                out[j, :, h * wide : (h + 1) * wide],
                preferred_element_type=F32,
            )
            res[h][j] = value.astype(BF16).T
            return carry

        def rho_start(k, carry):
            d = (k + 2) % (g_count - 1) + 1
            to = (ga + d) % g_count
            for i in range(CAP):
                rho_tx[h, to * CAP + i] = res[h][block_of_slot[to * CAP + i]]
            rho_copy(h, d).start()
            return carry

        lax.fori_loop(0, q_count, make_turned, 0)
        lax.fori_loop(0, g_count - 1, rho_start, 0)
        for i in range(CAP):
            rho_rx[h][ga * CAP + i] = res[h][block_of_slot[ga * CAP + i]]

    load_d = pltpu.make_async_copy(drows, own_d, local_sem.at[3])
    load_d.start()

    next_x.from_minus()
    to_neighbours(1, minus(x), fwd.at[minus(x)])
    next_x.from_plus()
    to_neighbours(2, plus(x), fwd.at[plus(x)])
    next_x.forward()
    own_x.start()

    d1_sem, d2_sem = sems(q_count), sems(q_count)

    def spread_copy(d):
        to = (pb + d) % q_count
        return copy(dmat.at[to], spread.at[pb], d1_sem + d, (to, ga))

    def spread_start(d, carry):
        spread_copy(d).start()
        return carry

    lax.fori_loop(1, q_count, spread_start, 0)
    keep_d1 = pltpu.make_async_copy(dmat.at[pb], spread.at[pb], local_sem.at[2])
    keep_d1.start()

    def make_turn_back(j, carry):
        turn_back[j] = turn_of(j).T.astype(BF16)
        return carry

    lax.fori_loop(0, q_count, make_turn_back, 0)
    next_x.from_beyond()
    to_neighbours(3, beyond(x), fwd.at[beyond(x)])
    own_x.forward()

    def group(h, row):
        return jnp.concatenate([rho_rx[h][held_slot[row * NX + i]] for i in range(NX)], axis=1)

    def project(row, values, total, first):
        def one(n, carry):
            columns = pl.ds(pl.multiple_of(n * basis, basis), basis)
            block = held[row, :, :, columns].reshape(-1, basis)
            part = jnp.dot(values[...], block, preferred_element_type=F32)
            total[n] = part if first else total[n] + part
            return carry

        lax.fori_loop(0, g_count, one, 0)

    part_sem = sems(4)
    for h in parts:

        def rho_wait(d, carry):
            source = (ga + g_count - d) % g_count
            arrive(rho_rx[h].at[pl.ds(source * CAP, CAP)], rho_sem + h * g_count + d)
            return carry

        lax.fori_loop(1, g_count, rho_wait, 0)
        part_tx[h] = group(h, across)
        send(part_tx.at[h], part_rx.at[h], part_sem + h, on_y(across))

    def spread_wait(d, carry):
        arrive(spread.at[(pb + q_count - d) % q_count], d1_sem + d)
        return carry

    lax.fori_loop(1, q_count, spread_wait, 0)
    keep_d1.wait()

    def choose(q, carry):
        chosen[q] = spread[minus_q[q]]
        return carry

    lax.fori_loop(0, q_count, choose, 0)

    def mate_copy(d):
        to = (pb + d) % q_count
        return copy(chosen.at[to], mate_rows.at[pb], d2_sem + d, (to, ga))

    def mate_start(d, carry):
        mate_copy(d).start()
        return carry

    lax.fori_loop(1, q_count, mate_start, 0)
    keep_d2 = pltpu.make_async_copy(chosen.at[pb], mate_rows.at[pb], local_sem.at[2])
    keep_d2.start()

    class Reduce:
        def __init__(self, total, landing, outgoing, incoming):
            self.total, self.landing = total, landing
            self.outgoing, self.incoming = outgoing, incoming
            self.i = sems(2 * z_count)

        def to_core(self, k):
            return copy(
                self.total.at[k * NC + (1 - c)], self.landing.at[k], self.i + k, (pb, sibling)
            )

        def start(self):
            for k in range(z_count):
                self.to_core(k).start()

        def sent(self):
            for k in range(z_count):
                self.to_core(k).wait_send()

        def along_z(self):
            for d in (2, 1, 3):
                k = (z + d) % z_count
                arrive(self.landing.at[k], self.i + k)
                self.outgoing[d] = (self.total[k * NC + c] + self.landing[k]).astype(BF16)
                send(
                    self.outgoing.at[d],
                    self.incoming.at[d],
                    self.i + z_count + d,
                    (pb, k * NC + c),
                )
            arrive(self.landing.at[z], self.i + z)

        def finish(self):
            value = self.total[ga] + self.landing[z]
            for d in (1, 3, 2):
                arrive(self.incoming.at[d], self.i + z_count + d)
                value = value + self.incoming[d].astype(F32)
            return value

    reduce1 = [Reduce(acc.at[h], core_rx.at[h], sum_tx.at[h], sum_rx.at[h]) for h in parts]
    reduce2 = [Reduce(acc2.at[h], core_rx2.at[h], sum_tx2.at[h], sum_rx2.at[h]) for h in parts]

    own_x.finish()
    keep.wait()
    for h in parts:
        arrive(part_rx.at[h], part_sem + h)
        project(y, part_rx.at[h], acc2.at[h], True)
        reduce2[h].start()
    for h in parts:
        rho_group[...] = group(h, y)
        project(y, rho_group, acc.at[h], True)
        reduce2[h].along_z()
    for k, s in enumerate((x, minus(x), plus(x), beyond(x))):
        arrive(held.at[down, s], y_sem + k)
        arrive(held.at[up, s], y_sem + 4 + k)
    for h in parts:
        for row in (down, up):
            rho_group[...] = group(h, row)
            project(row, rho_group, acc.at[h], False)
        reduce1[h].start()
    for h in parts:
        mate_sum[h, 0] = reduce2[h].finish().astype(BF16)
        send(mate_sum.at[h, 0], mate_sum.at[h, 1], part_sem + 2 + h, on_y(across))
        reduce1[h].along_z()

    def mate_wait(d, carry):
        arrive(mate_rows.at[(pb + q_count - d) % q_count], d2_sem + d)
        return carry

    lax.fori_loop(1, q_count, mate_wait, 0)
    keep_d2.wait()

    column_sem = sems(g_count)

    def column_copy(d):
        to = (ga + d) % g_count
        columns = pl.ds(pl.multiple_of(to * basis, basis), basis)
        return copy(mate_rows.at[:, :, columns], mate_cols.at[ga], column_sem + d, (pb, to))

    def column_start(d, carry):
        column_copy(d).start()
        return carry

    lax.fori_loop(1, g_count, column_start, 0)
    own_columns = pl.ds(pl.multiple_of(ga * basis, basis), basis)
    keep_cols = pltpu.make_async_copy(
        mate_rows.at[:, :, own_columns], mate_cols.at[ga], local_sem.at[4]
    )
    keep_cols.start()

    class Gather:
        def __init__(self, ref, use):
            self.ref, self.use = ref, use
            self.i = sems(8)

        def start(self):
            mine = self.ref.at[ga]
            for d in (2, 1, 3):
                send(mine, mine, self.i + d, (pb, (z + d) % z_count * NC + c))
            send(mine, mine, self.i, (pb, sibling))

        def own(self):
            self.use(ga)

        def beside(self):
            arrive(self.ref.at[sibling], self.i)
            self.use(sibling)

        def along_z(self):
            for d in (1, 3, 2):
                source = (z + z_count - d) % z_count * NC + c
                there = self.ref.at[source]
                arrive(there, self.i + d)
                send(there, there, self.i + 4 + d, (pb, sibling))
                self.use(source)

        def rest(self):
            for d in (1, 3, 2):
                source = (z + z_count - d) % z_count * NC + (1 - c)
                arrive(self.ref.at[source], self.i + 4 + d)
                self.use(source)

    def column_wait(d, carry):
        arrive(mate_cols.at[(ga + g_count - d) % g_count], column_sem + d)
        return carry

    def apply(h):
        def use(n):
            columns = pl.ds(pl.multiple_of(n * basis, basis), basis)
            other = jnp.dot(
                coef[h, n], mate_cols[n].reshape(basis, basis), preferred_element_type=F32
            )
            slab_sum[h] += dot_nt(coef[h, n], own_d[:, columns]) + other

        return use

    gather_coef = [Gather(coef.at[h], apply(h)) for h in parts]
    for h in parts:
        value = reduce1[h].finish()
        arrive(mate_sum.at[h, 1], part_sem + 2 + h)
        coef[h, ga] = (value + mate_sum[h, 1].astype(F32)).astype(BF16)
        gather_coef[h].start()
    lax.fori_loop(1, g_count, column_wait, 0)
    keep_cols.wait()
    load_d.wait()
    slab_sum[...] = jnp.zeros_like(slab_sum)

    half = NX // 2

    def part_of(k):
        return (y + NX - 1 + k // 2) % NX, k % 2

    def expand(values, total, first_part, count):
        first = [True]

        def use(n):
            columns = pl.ds(pl.multiple_of(n * basis, basis), basis)
            fresh = first.pop() if first else False

            def one(k, carry):
                row, side = part_of(first_part + k)
                block = held[row, pl.ds(side * half, half), :, columns].reshape(-1, basis)
                value = dot_nt(values[n], block)
                total[k] = value if fresh else total[k] + value
                return carry

            lax.fori_loop(0, count, one, 0)

        return use

    mate_sem = sems(4)
    gather_own, gather_mate = [], []
    for h in parts:
        gather_own.append(
            Gather(screened.at[h], expand(screened.at[h], acc2.at[h], 0, 2 * (NX - 1)))
        )
        gather_mate.append(Gather(mate_scr.at[h], expand(mate_scr.at[h], acc.at[h], 2, 2)))
    for h in parts:
        gather_coef[h].own()
        gather_coef[h].beside()
    for h in parts:
        gather_coef[h].along_z()
        gather_coef[h].rest()
        screened[h, ga] = (0.5 * slab_sum[h] - coef[h, ga].astype(F32)).astype(BF16)
        send(screened.at[h, ga], mate_scr.at[h, ga], mate_sem + h, on_y(across))
        gather_own[h].start()
    for h in parts:
        reduce1[h].sent()
        reduce2[h].sent()
    for h in parts:
        gather_own[h].own()
        arrive(mate_scr.at[h, ga], mate_sem + h)
        gather_mate[h].start()

    def rho_sent(d, carry):
        for h in parts:
            rho_copy(h, d).wait_send()
        return carry

    lax.fori_loop(1, g_count, rho_sent, 0)
    back_sem = sems(2 * g_count)

    def back_copy(h, d):
        to = (ga + d) % g_count
        return copy(
            rho_tx.at[h, pl.ds(to * CAP, CAP)],
            back[h].at[pl.ds(ga * CAP, CAP)],
            back_sem + h * g_count + d,
            (pb, to),
        )

    for h in parts:
        gather_own[h].beside()
        gather_own[h].along_z()
        gather_mate[h].own()
        gather_mate[h].beside()
        gather_mate[h].along_z()
        gather_mate[h].rest()
        for k in range(2):
            value = (acc[h, k] * ratio).astype(BF16)
            for i in range(half):
                mate_res[h, k * half + i] = value[:, i * rows : (i + 1) * rows]
        send(mate_res.at[h], res[h].at[pl.ds(y * NX, NX)], mate_sem + 2 + h, on_y(across))
        gather_own[h].rest()

        def finish_rows(k, carry):
            row, side = part_of(k)
            value = (acc2[h, k] * ratio).astype(BF16)
            for i in range(half):
                res[h][row * NX + side * half + i] = value[:, i * rows : (i + 1) * rows]
            return carry

        lax.fori_loop(0, 2 * (NX - 1), finish_rows, 0)
        arrive(res[h].at[pl.ds(across * NX, NX)], mate_sem + 2 + h)

        def back_start(k, carry):
            d = (k + 2) % (g_count - 1) + 1
            to = (ga + d) % g_count
            for i in range(CAP):
                rho_tx[h, to * CAP + i] = res[h][held_of_slot[to * CAP + i]]
            back_copy(h, d).start()
            return carry

        lax.fori_loop(0, g_count - 1, back_start, 0)
        for i in range(CAP):
            back[h][ga * CAP + i] = res[h][held_of_slot[ga * CAP + i]]

    for h in parts:

        def back_wait(d, carry):
            source = (ga + g_count - d) % g_count
            arrive(back[h].at[pl.ds(source * CAP, CAP)], back_sem + h * g_count + d)
            return carry

        def unturn(j, carry):
            value = dot_nt(turn_back[j], back[h][send_slot[j]])
            out[j, :, h * wide : (h + 1) * wide] = value.astype(BF16)
            return carry

        lax.fori_loop(1, g_count, back_wait, 0)
        lax.fori_loop(0, q_count, unturn, 0)

    for one in started:
        one.wait_send()

    def drain_pb(d, carry):
        spread_copy(d).wait_send()
        mate_copy(d).wait_send()
        return carry

    def drain_ga(d, carry):
        column_copy(d).wait_send()
        for h in parts:
            back_copy(h, d).wait_send()
        return carry

    lax.fori_loop(1, q_count, drain_pb, 0)
    lax.fori_loop(1, g_count, drain_ga, 0)


def on_device(
    irr_vectors, inv_dielectric, pair_density, minus_q, sym_op, rot_blocks, rot_rows, phase_bits
):
    q_count = lax.axis_size("pb")
    g_count = lax.axis_size("ga")
    owner = lax.axis_index("pb")
    slab_index = lax.axis_index("ga")
    irr_count, block_rows, width = irr_vectors.shape
    density_width = pair_density.shape[2]
    blocks_all = q_count * g_count
    slab_rows = q_count * block_rows
    basis_rows = width // g_count
    slot_count = g_count * CAP
    ratio = math.sqrt(slab_rows * g_count / width)

    operation = lax.dynamic_index_in_dim(sym_op, owner, 0, keepdims=False)
    table = lax.dynamic_index_in_dim(rot_blocks, operation, 0, keepdims=False)
    places = jnp.arange(blocks_all, dtype=jnp.int32)
    source_ga = table % g_count
    earlier = (places[None, :] < places[:, None]) & (
        places[None, :] // q_count == places[:, None] // q_count
    )
    ranks = jnp.sum(
        (earlier & (source_ga[None, :] == source_ga[:, None])).astype(jnp.int32), axis=1
    )
    mine_source = lax.dynamic_slice_in_dim(table, slab_index * q_count, q_count)
    mine_rank = lax.dynamic_slice_in_dim(ranks, slab_index * q_count, q_count)
    send_slot = mine_source % g_count * CAP + mine_rank
    slots = jnp.arange(slot_count, dtype=jnp.int32)
    local = jnp.arange(q_count, dtype=jnp.int32)
    block_of_slot = jnp.sum(
        jnp.where(slots[:, None] == send_slot[None, :], local[None, :], 0), axis=1
    )
    senders = local * g_count + slab_index
    match = table[None, :] == senders[:, None]
    dest_block = jnp.sum(jnp.where(match, places[None, :], 0), axis=1)
    dest_rank = jnp.sum(jnp.where(match, ranks[None, :], 0), axis=1)
    held_slot = dest_block // q_count * CAP + dest_rank
    held_of_slot = jnp.sum(
        jnp.where(slots[:, None] == held_slot[None, :], local[None, :], 0), axis=1
    )

    row_table = lax.dynamic_slice_in_dim(
        lax.dynamic_index_in_dim(rot_rows, operation, 0, keepdims=False),
        slab_index * q_count,
        q_count,
    )
    bits = lax.dynamic_slice_in_dim(
        lax.dynamic_index_in_dim(phase_bits, operation, 0, keepdims=False),
        slab_index * slab_rows,
        slab_rows,
    ).reshape(q_count, block_rows)

    vmem = pltpu.VMEM
    dma = pltpu.SemaphoreType.DMA
    wide = density_width // 2
    slab = (wide, basis_rows)
    slots = (slot_count, wide, block_rows)
    chunk = basis_rows // q_count
    any_spec = pl.BlockSpec(memory_space=pl.ANY)
    smem_spec = pl.BlockSpec(memory_space=pltpu.SMEM)
    vmem_spec = pl.BlockSpec(memory_space=pltpu.VMEM)

    def run(*operands):
        return pl.pallas_call(
            lambda *refs: kernel(ratio, *refs),
            out_shape=jax.ShapeDtypeStruct((q_count, block_rows, density_width), BF16),
            in_specs=[any_spec] * 4 + [vmem_spec] * 2 + [smem_spec] * 5,
            out_specs=vmem_spec,
            scratch_shapes=[
                vmem((NX, NX, block_rows, width), BF16),
                vmem((NX, block_rows, width), BF16),
                vmem((2, block_rows, width), BF16),
                vmem((2, *slots), BF16),
                vmem(slots, BF16),
                vmem(slots, BF16),
                vmem((wide, NX * block_rows), BF16),
                vmem((2, wide, NX * block_rows), BF16),
                vmem((2, wide, NX * block_rows), BF16),
                vmem((2, g_count, *slab), F32),
                vmem((2, g_count, *slab), F32),
                vmem((2, g_count // NC, *slab), F32),
                vmem((2, g_count // NC, *slab), F32),
                vmem((2, g_count // NC, *slab), BF16),
                vmem((2, g_count // NC, *slab), BF16),
                vmem((2, g_count // NC, *slab), BF16),
                vmem((2, g_count // NC, *slab), BF16),
                vmem((2, 2, *slab), BF16),
                vmem((2, g_count, *slab), BF16),
                vmem((2, *slab), F32),
                vmem((basis_rows, width), BF16),
                vmem((q_count, chunk, width), BF16),
                vmem((q_count, chunk, width), BF16),
                vmem((q_count, chunk, width), BF16),
                vmem((g_count, q_count, chunk, basis_rows), BF16),
                vmem((2, g_count, *slab), BF16),
                vmem((2, g_count, *slab), BF16),
                vmem((q_count, wide, block_rows), BF16),
                vmem((q_count, wide, block_rows), BF16),
                vmem((2, NX, wide, block_rows), BF16),
                vmem(slots, BF16),
                vmem(slots, BF16),
                vmem((q_count, block_rows, block_rows), BF16),
                dma((5,)),
                dma((SEMS,)),
                dma((SEMS,)),
            ],
            compiler_params=pltpu.CompilerParams(
                collective_id=0, has_side_effects=True, vmem_limit_bytes=62 * 1024 * 1024
            ),
        )(*operands)

    out = run(
        irr_vectors,
        inv_dielectric[0].reshape(q_count, chunk, width),
        inv_dielectric[0],
        pair_density[0].reshape(q_count, block_rows, density_width),
        row_table,
        bits,
        minus_q,
        block_of_slot,
        held_slot,
        held_of_slot,
        send_slot,
    )
    return out.reshape(1, slab_rows, density_width)


def solution(mesh):
    in_specs = (
        P(None, ("pb", "ga"), None),
        P("pb", "ga", None),
        P("pb", "ga", None),
        P(),
        P(),
        P(),
        P(),
        P(),
    )
    out_specs = P("pb", "ga", None)
    return jax.shard_map(
        on_device, mesh=mesh, in_specs=in_specs, out_specs=out_specs, check_vma=False
    )
```

```python
import math

import jax
import jax.numpy as jnp
from jax import lax
from jax.experimental import pallas as pl
from jax.experimental.pallas import tpu as pltpu
from jax.sharding import PartitionSpec as P

MESH = pl.DeviceIdType.MESH
NX = 4
NC = 2
SEMS = 200
CAP = 3
BF16 = jnp.bfloat16
F32 = jnp.float32


def kernel(
    ratio,
    irr,
    dmat,
    drows,
    density,
    row_table,
    bits,
    minus_q,
    block_of_slot,
    held_slot,
    held_of_slot,
    send_slot,
    out,
    held,
    fwd,
    via_x,
    rho_tx,
    rho_rx_low,
    rho_rx_high,
    rho_group,
    part_tx,
    part_rx,
    acc,
    acc2,
    core_rx,
    core_rx2,
    sum_tx,
    sum_tx2,
    sum_rx,
    sum_rx2,
    mate_sum,
    coef,
    slab_sum,
    own_d,
    spread,
    chosen,
    mate_rows,
    mate_cols,
    mate_t,
    screened,
    mate_scr,
    res_low,
    res_high,
    mate_res,
    back_low,
    back_high,
    turn_back,
    local_sem,
    send_sem,
    recv_sem,
):
    q_count = lax.axis_size("pb")
    g_count = lax.axis_size("ga")
    pb = lax.axis_index("pb")
    ga = lax.axis_index("ga")
    y, x = pb // NX, pb % NX
    z, c = ga // NC, ga % NC
    z_count = g_count // NC
    sibling = z * NC + (1 - c)
    basis = own_d.shape[0]
    rows = row_table.shape[1]
    plus, minus, beyond = (lambda v: (v + 1) % NX), (lambda v: (v + 3) % NX), (lambda v: (v + 2) % NX)
    ahead, behind = (lambda v: (v + 1 + 2 * c) % NX), (lambda v: (v + 3 - 2 * c) % NX)
    up, down, across = plus(y), minus(y), beyond(y)
    parts = range(2)
    res = (res_low, res_high)
    rho_rx = (rho_rx_low, rho_rx_high)
    back = (back_low, back_high)
    wide = res_low.shape[2]
    started = []
    taken = [0]

    def sems(count):
        first = taken[0]
        taken[0] += count
        assert taken[0] <= SEMS
        return first

    def copy(src, dst, i, to):
        return pltpu.make_async_remote_copy(
            src_ref=src,
            dst_ref=dst,
            send_sem=send_sem.at[i],
            recv_sem=recv_sem.at[i],
            device_id=to,
            device_id_type=MESH,
        )

    def send(src, dst, i, to):
        one = copy(src, dst, i, to)
        one.start()
        started.append(one)

    def arrive(dst, i):
        copy(dst, dst, i, (pb, ga)).wait_recv()

    def on_x(t):
        return (y * NX + t, ga)

    def on_y(t):
        return (t * NX + x, ga)

    class Exchange:
        def __init__(self, me, to, src, dst, via):
            self.me, self.to, self.src, self.dst, self.via = me, to, src, dst, via
            self.i = sems(4)

        def start(self):
            me = self.me
            send(self.src(plus(me)), self.dst(me), self.i, self.to(plus(me)))
            send(self.src(minus(me)), self.dst(me), self.i + 1, self.to(minus(me)))
            send(self.src(beyond(me)), self.via, self.i + 2, self.to(ahead(me)))

        def forward(self):
            arrive(self.via, self.i + 2)
            send(self.via, self.dst(behind(self.me)), self.i + 3, self.to(ahead(self.me)))

        def from_minus(self):
            arrive(self.dst(minus(self.me)), self.i)

        def from_plus(self):
            arrive(self.dst(plus(self.me)), self.i + 1)

        def from_beyond(self):
            arrive(self.dst(beyond(self.me)), self.i + 3)

        def finish(self):
            self.from_minus()
            self.from_plus()
            self.from_beyond()

    load_rho = pltpu.make_async_copy(density, out, local_sem.at[0])
    load_rho.start()

    barrier = pltpu.get_barrier_semaphore()

    def greet_pb(d, carry):
        pl.semaphore_signal(
            barrier, inc=1, device_id=((pb + d) % q_count, ga), device_id_type=MESH
        )
        return carry

    def greet_ga(d, carry):
        pl.semaphore_signal(
            barrier, inc=1, device_id=(pb, (ga + d) % g_count), device_id_type=MESH
        )
        return carry

    lax.fori_loop(1, q_count, greet_pb, 0)
    lax.fori_loop(1, g_count, greet_ga, 0)
    pl.semaphore_wait(barrier, q_count + g_count - 2)

    own_irr = NX * (y % 2)
    next_irr = NX * ((y + 1) % 2)
    next_x = Exchange(x, on_x, lambda t: irr.at[next_irr + t], lambda s: fwd.at[s], via_x.at[0])
    own_x = Exchange(x, on_x, lambda t: irr.at[own_irr + t], lambda s: held.at[y, s], via_x.at[1])
    next_x.start()
    keep = pltpu.make_async_copy(irr.at[own_irr + x], held.at[y, x], local_sem.at[1])
    keep.start()
    y_sem = sems(8)

    def to_neighbours(k, source, src):
        there = held.at[y, source]
        send(src, there, y_sem + k, on_y(up))
        send(src, there, y_sem + 4 + k, on_y(down))

    to_neighbours(0, x, irr.at[next_irr + x])

    def turn_of(j):
        sources = lax.broadcasted_iota(jnp.int32, (rows, rows), 0)
        sign = (1 - 2 * bits[pl.ds(j, 1), :]).astype(F32)
        return jnp.where(row_table[pl.ds(j, 1), :] == sources, sign, 0.0)

    load_rho.wait()
    rho_sem = sems(2 * g_count)

    def rho_copy(h, d):
        to = (ga + d) % g_count
        return copy(
            rho_tx.at[h, pl.ds(to * CAP, CAP)],
            rho_rx[h].at[pl.ds(ga * CAP, CAP)],
            rho_sem + h * g_count + d,
            (pb, to),
        )

    for h in parts:

        def make_turned(j, carry):
            value = jnp.dot(
                turn_of(j).astype(BF16),
                out[j, :, h * wide : (h + 1) * wide],
                preferred_element_type=F32,
            )
            res[h][j] = value.astype(BF16)
            return carry

        def rho_start(k, carry):
            d = (k + 2) % (g_count - 1) + 1
            to = (ga + d) % g_count
            for i in range(CAP):
                rho_tx[h, to * CAP + i] = res[h][block_of_slot[to * CAP + i]]
            rho_copy(h, d).start()
            return carry

        lax.fori_loop(0, q_count, make_turned, 0)
        lax.fori_loop(0, g_count - 1, rho_start, 0)
        for i in range(CAP):
            rho_rx[h][ga * CAP + i] = res[h][block_of_slot[ga * CAP + i]]

    load_d = pltpu.make_async_copy(drows, own_d, local_sem.at[3])
    load_d.start()

    next_x.from_minus()
    to_neighbours(1, minus(x), fwd.at[minus(x)])
    next_x.from_plus()
    to_neighbours(2, plus(x), fwd.at[plus(x)])
    next_x.forward()
    own_x.start()

    def make_turn_back(j, carry):
        turn_back[j] = turn_of(j).T.astype(BF16)
        return carry

    lax.fori_loop(0, q_count, make_turn_back, 0)
    next_x.from_beyond()
    to_neighbours(3, beyond(x), fwd.at[beyond(x)])
    own_x.forward()

    def group(h, row):
        return jnp.concatenate([rho_rx[h][held_slot[row * NX + i]] for i in range(NX)], axis=0).T

    def project(row, values, total, first):
        def one(n, carry):
            columns = pl.ds(pl.multiple_of(n * basis, basis), basis)
            block = held[row, :, :, columns].reshape(-1, basis)
            part = jnp.dot(values[...], block, preferred_element_type=F32)
            total[n] = part if first else total[n] + part
            return carry

        lax.fori_loop(0, g_count, one, 0)

    part_sem = sems(4)
    for h in parts:

        def rho_wait(d, carry):
            source = (ga + g_count - d) % g_count
            arrive(rho_rx[h].at[pl.ds(source * CAP, CAP)], rho_sem + h * g_count + d)
            return carry

        lax.fori_loop(1, g_count, rho_wait, 0)
        part_tx[h] = group(h, across)
        send(part_tx.at[h], part_rx.at[h], part_sem + h, on_y(across))

    class Reduce:
        def __init__(self, total, landing, outgoing, incoming):
            self.total, self.landing = total, landing
            self.outgoing, self.incoming = outgoing, incoming
            self.i = sems(2 * z_count)

        def to_core(self, k):
            return copy(
                self.total.at[k * NC + (1 - c)], self.landing.at[k], self.i + k, (pb, sibling)
            )

        def start(self):
            for k in range(z_count):
                self.to_core(k).start()

        def sent(self):
            for k in range(z_count):
                self.to_core(k).wait_send()

        def along_z(self):
            for d in (2, 1, 3):
                k = (z + d) % z_count
                arrive(self.landing.at[k], self.i + k)
                self.outgoing[d] = (self.total[k * NC + c] + self.landing[k]).astype(BF16)
                send(
                    self.outgoing.at[d],
                    self.incoming.at[d],
                    self.i + z_count + d,
                    (pb, k * NC + c),
                )
            arrive(self.landing.at[z], self.i + z)

        def finish(self):
            value = self.total[ga] + self.landing[z]
            for d in (1, 3, 2):
                arrive(self.incoming.at[d], self.i + z_count + d)
                value = value + self.incoming[d].astype(F32)
            return value

    reduce1 = [Reduce(acc.at[h], core_rx.at[h], sum_tx.at[h], sum_rx.at[h]) for h in parts]
    reduce2 = [Reduce(acc2.at[h], core_rx2.at[h], sum_tx2.at[h], sum_rx2.at[h]) for h in parts]

    own_x.finish()
    keep.wait()
    d1_sem, d2_sem = sems(q_count), sems(q_count)

    def spread_copy(d):
        to = (pb + d) % q_count
        return copy(dmat.at[to], spread.at[pb], d1_sem + d, (to, ga))

    def spread_start(d, carry):
        spread_copy(d).start()
        return carry

    lax.fori_loop(1, q_count, spread_start, 0)
    keep_d1 = pltpu.make_async_copy(dmat.at[pb], spread.at[pb], local_sem.at[2])
    keep_d1.start()

    for h in parts:
        arrive(part_rx.at[h], part_sem + h)
        project(y, part_rx.at[h], acc2.at[h], True)
        reduce2[h].start()
    for h in parts:
        rho_group[...] = group(h, y)
        project(y, rho_group, acc.at[h], True)
        reduce2[h].along_z()
    for k, s in enumerate((x, minus(x), plus(x), beyond(x))):
        arrive(held.at[down, s], y_sem + k)
        arrive(held.at[up, s], y_sem + 4 + k)
    def spread_wait(d, carry):
        arrive(spread.at[(pb + q_count - d) % q_count], d1_sem + d)
        return carry

    lax.fori_loop(1, q_count, spread_wait, 0)
    keep_d1.wait()

    def choose(q, carry):
        chosen[q] = spread[minus_q[q]]
        return carry

    lax.fori_loop(0, q_count, choose, 0)

    def mate_copy(d):
        to = (pb + d) % q_count
        return copy(chosen.at[to], mate_rows.at[pb], d2_sem + d, (to, ga))

    def mate_start(d, carry):
        mate_copy(d).start()
        return carry

    lax.fori_loop(1, q_count, mate_start, 0)
    keep_d2 = pltpu.make_async_copy(chosen.at[pb], mate_rows.at[pb], local_sem.at[2])
    keep_d2.start()

    for h in parts:
        for row in (down, up):
            rho_group[...] = group(h, row)
            project(row, rho_group, acc.at[h], False)
        reduce1[h].start()
    for h in parts:
        mate_sum[h, 0] = reduce2[h].finish().astype(BF16)
        send(mate_sum.at[h, 0], mate_sum.at[h, 1], part_sem + 2 + h, on_y(across))
        reduce1[h].along_z()

    def mate_wait(d, carry):
        arrive(mate_rows.at[(pb + q_count - d) % q_count], d2_sem + d)
        return carry

    lax.fori_loop(1, q_count, mate_wait, 0)
    keep_d2.wait()

    column_sem = sems(g_count)

    def column_copy(d):
        to = (ga + d) % g_count
        columns = pl.ds(pl.multiple_of(to * basis, basis), basis)
        return copy(mate_rows.at[:, :, columns], mate_cols.at[ga], column_sem + d, (pb, to))

    def column_start(d, carry):
        column_copy(d).start()
        return carry

    lax.fori_loop(1, g_count, column_start, 0)
    own_columns = pl.ds(pl.multiple_of(ga * basis, basis), basis)
    keep_cols = pltpu.make_async_copy(
        mate_rows.at[:, :, own_columns], mate_cols.at[ga], local_sem.at[4]
    )
    keep_cols.start()

    class Gather:
        def __init__(self, ref, use):
            self.ref, self.use = ref, use
            self.i = sems(8)

        def start(self):
            mine = self.ref.at[ga]
            for d in (2, 1, 3):
                send(mine, mine, self.i + d, (pb, (z + d) % z_count * NC + c))
            send(mine, mine, self.i, (pb, sibling))

        def own(self):
            self.use(ga)

        def beside(self):
            arrive(self.ref.at[sibling], self.i)
            self.use(sibling)

        def along_z(self):
            for d in (1, 3, 2):
                source = (z + z_count - d) % z_count * NC + c
                there = self.ref.at[source]
                arrive(there, self.i + d)
                send(there, there, self.i + 4 + d, (pb, sibling))
                self.use(source)

        def rest(self):
            for d in (1, 3, 2):
                source = (z + z_count - d) % z_count * NC + (1 - c)
                arrive(self.ref.at[source], self.i + 4 + d)
                self.use(source)

    def column_wait(d, carry):
        arrive(mate_cols.at[(ga + g_count - d) % g_count], column_sem + d)
        return carry

    def apply(h):
        def use(n):
            columns = pl.ds(pl.multiple_of(n * basis, basis), basis)
            slab_sum[h] += jnp.dot(
                own_d[:, columns], coef[h, n], preferred_element_type=F32
            ) + jnp.dot(mate_t[:, columns], coef[h, n], preferred_element_type=F32)

        return use

    gather_coef = [Gather(coef.at[h], apply(h)) for h in parts]
    for h in parts:
        value = reduce1[h].finish()
        arrive(mate_sum.at[h, 1], part_sem + 2 + h)
        coef[h, ga] = (value + mate_sum[h, 1].astype(F32)).astype(BF16).T
        gather_coef[h].start()
    lax.fori_loop(1, g_count, column_wait, 0)
    keep_cols.wait()
    load_d.wait()

    def turn_columns(n, carry):
        columns = pl.ds(pl.multiple_of(n * basis, basis), basis)
        mate_t[:, columns] = mate_cols[n].reshape(basis, basis).T
        return carry

    lax.fori_loop(0, g_count, turn_columns, 0)
    slab_sum[...] = jnp.zeros_like(slab_sum)

    half = NX // 2

    def row_of(k):
        return (y + NX - 1 + k) % NX

    def expand(values, total, first_row, count):
        first = [True]

        def use(n):
            columns = pl.ds(pl.multiple_of(n * basis, basis), basis)
            fresh = first.pop() if first else False

            def one(k, carry):
                block = held[row_of(first_row + k), :, :, columns].reshape(-1, basis)
                value = jnp.dot(block, values[n], preferred_element_type=F32)
                value = value.reshape(half, -1, wide)
                place = pl.ds(k * half, half)
                total[place] = value if fresh else total[place] + value
                return carry

            lax.fori_loop(0, count, one, 0)

        return use

    mate_sem = sems(4)
    gather_own, gather_mate = [], []
    for h in parts:
        gather_own.append(
            Gather(screened.at[h], expand(screened.at[h], acc2.at[h], 0, NX - 1))
        )
        gather_mate.append(Gather(mate_scr.at[h], expand(mate_scr.at[h], acc.at[h], 1, 1)))
    for h in parts:
        gather_coef[h].own()
        gather_coef[h].beside()
    for h in parts:
        gather_coef[h].along_z()
        gather_coef[h].rest()
        screened[h, ga] = (0.5 * slab_sum[h] - coef[h, ga].astype(F32)).astype(BF16)
        send(screened.at[h, ga], mate_scr.at[h, ga], mate_sem + h, on_y(across))
        gather_own[h].start()
    for h in parts:
        reduce1[h].sent()
        reduce2[h].sent()
    for h in parts:
        gather_own[h].own()
        arrive(mate_scr.at[h, ga], mate_sem + h)
        gather_mate[h].start()

    def rho_sent(d, carry):
        for h in parts:
            rho_copy(h, d).wait_send()
        return carry

    lax.fori_loop(1, g_count, rho_sent, 0)
    back_sem = sems(2 * g_count)

    def back_copy(h, d):
        to = (ga + d) % g_count
        return copy(
            rho_tx.at[h, pl.ds(to * CAP, CAP)],
            back[h].at[pl.ds(ga * CAP, CAP)],
            back_sem + h * g_count + d,
            (pb, to),
        )

    for h in parts:
        gather_own[h].beside()
        gather_own[h].along_z()
        gather_mate[h].own()
        gather_mate[h].beside()
        gather_mate[h].along_z()
        gather_mate[h].rest()
        mate_res[h] = (acc[h, :half] * ratio).astype(BF16).reshape(NX, rows, wide)
        send(mate_res.at[h], res[h].at[pl.ds(y * NX, NX)], mate_sem + 2 + h, on_y(across))
        gather_own[h].rest()

        def finish_rows(k, carry):
            value = (acc2[h, pl.ds(k * half, half)] * ratio).astype(BF16)
            res[h][pl.ds(row_of(k) * NX, NX)] = value.reshape(NX, rows, wide)
            return carry

        lax.fori_loop(0, NX - 1, finish_rows, 0)
        arrive(res[h].at[pl.ds(across * NX, NX)], mate_sem + 2 + h)

        def back_start(k, carry):
            d = (k + 2) % (g_count - 1) + 1
            to = (ga + d) % g_count
            for i in range(CAP):
                rho_tx[h, to * CAP + i] = res[h][held_of_slot[to * CAP + i]]
            back_copy(h, d).start()
            return carry

        lax.fori_loop(0, g_count - 1, back_start, 0)
        for i in range(CAP):
            back[h][ga * CAP + i] = res[h][held_of_slot[ga * CAP + i]]

    for h in parts:

        def back_wait(d, carry):
            source = (ga + g_count - d) % g_count
            arrive(back[h].at[pl.ds(source * CAP, CAP)], back_sem + h * g_count + d)
            return carry

        def unturn(j, carry):
            value = jnp.dot(turn_back[j], back[h][send_slot[j]], preferred_element_type=F32)
            out[j, :, h * wide : (h + 1) * wide] = value.astype(BF16)
            return carry

        lax.fori_loop(1, g_count, back_wait, 0)
        lax.fori_loop(0, q_count, unturn, 0)

    for one in started:
        one.wait_send()

    def drain_pb(d, carry):
        spread_copy(d).wait_send()
        mate_copy(d).wait_send()
        return carry

    def drain_ga(d, carry):
        column_copy(d).wait_send()
        for h in parts:
            back_copy(h, d).wait_send()
        return carry

    lax.fori_loop(1, q_count, drain_pb, 0)
    lax.fori_loop(1, g_count, drain_ga, 0)


def on_device(
    irr_vectors, inv_dielectric, pair_density, minus_q, sym_op, rot_blocks, rot_rows, phase_bits
):
    q_count = lax.axis_size("pb")
    g_count = lax.axis_size("ga")
    owner = lax.axis_index("pb")
    slab_index = lax.axis_index("ga")
    irr_count, block_rows, width = irr_vectors.shape
    density_width = pair_density.shape[2]
    blocks_all = q_count * g_count
    slab_rows = q_count * block_rows
    basis_rows = width // g_count
    slot_count = g_count * CAP
    ratio = math.sqrt(slab_rows * g_count / width)

    operation = lax.dynamic_index_in_dim(sym_op, owner, 0, keepdims=False)
    table = lax.dynamic_index_in_dim(rot_blocks, operation, 0, keepdims=False)
    places = jnp.arange(blocks_all, dtype=jnp.int32)
    source_ga = table % g_count
    earlier = (places[None, :] < places[:, None]) & (
        places[None, :] // q_count == places[:, None] // q_count
    )
    ranks = jnp.sum(
        (earlier & (source_ga[None, :] == source_ga[:, None])).astype(jnp.int32), axis=1
    )
    mine_source = lax.dynamic_slice_in_dim(table, slab_index * q_count, q_count)
    mine_rank = lax.dynamic_slice_in_dim(ranks, slab_index * q_count, q_count)
    send_slot = mine_source % g_count * CAP + mine_rank
    slots = jnp.arange(slot_count, dtype=jnp.int32)
    local = jnp.arange(q_count, dtype=jnp.int32)
    block_of_slot = jnp.sum(
        jnp.where(slots[:, None] == send_slot[None, :], local[None, :], 0), axis=1
    )
    senders = local * g_count + slab_index
    match = table[None, :] == senders[:, None]
    dest_block = jnp.sum(jnp.where(match, places[None, :], 0), axis=1)
    dest_rank = jnp.sum(jnp.where(match, ranks[None, :], 0), axis=1)
    held_slot = dest_block // q_count * CAP + dest_rank
    held_of_slot = jnp.sum(
        jnp.where(slots[:, None] == held_slot[None, :], local[None, :], 0), axis=1
    )

    row_table = lax.dynamic_slice_in_dim(
        lax.dynamic_index_in_dim(rot_rows, operation, 0, keepdims=False),
        slab_index * q_count,
        q_count,
    )
    bits = lax.dynamic_slice_in_dim(
        lax.dynamic_index_in_dim(phase_bits, operation, 0, keepdims=False),
        slab_index * slab_rows,
        slab_rows,
    ).reshape(q_count, block_rows)

    vmem = pltpu.VMEM
    dma = pltpu.SemaphoreType.DMA
    wide = density_width // 2
    slab = (wide, basis_rows)
    square = (basis_rows, wide)
    slots = (slot_count, block_rows, wide)
    chunk = basis_rows // q_count
    any_spec = pl.BlockSpec(memory_space=pl.ANY)
    smem_spec = pl.BlockSpec(memory_space=pltpu.SMEM)
    vmem_spec = pl.BlockSpec(memory_space=pltpu.VMEM)

    def run(*operands):
        return pl.pallas_call(
            lambda *refs: kernel(ratio, *refs),
            out_shape=jax.ShapeDtypeStruct((q_count, block_rows, density_width), BF16),
            in_specs=[any_spec] * 4 + [vmem_spec] * 2 + [smem_spec] * 5,
            out_specs=vmem_spec,
            scratch_shapes=[
                vmem((NX, NX, block_rows, width), BF16),
                vmem((NX, block_rows, width), BF16),
                vmem((2, block_rows, width), BF16),
                vmem((2, *slots), BF16),
                vmem(slots, BF16),
                vmem(slots, BF16),
                vmem((wide, NX * block_rows), BF16),
                vmem((2, wide, NX * block_rows), BF16),
                vmem((2, wide, NX * block_rows), BF16),
                vmem((2, g_count, *slab), F32),
                vmem((2, g_count, *slab), F32),
                vmem((2, g_count // NC, *slab), F32),
                vmem((2, g_count // NC, *slab), F32),
                vmem((2, g_count // NC, *slab), BF16),
                vmem((2, g_count // NC, *slab), BF16),
                vmem((2, g_count // NC, *slab), BF16),
                vmem((2, g_count // NC, *slab), BF16),
                vmem((2, 2, *slab), BF16),
                vmem((2, g_count, *square), BF16),
                vmem((2, *square), F32),
                vmem((basis_rows, width), BF16),
                vmem((q_count, chunk, width), BF16),
                vmem((q_count, chunk, width), BF16),
                vmem((q_count, chunk, width), BF16),
                vmem((g_count, q_count, chunk, basis_rows), BF16),
                vmem((basis_rows, width), BF16),
                vmem((2, g_count, *square), BF16),
                vmem((2, g_count, *square), BF16),
                vmem((q_count, block_rows, wide), BF16),
                vmem((q_count, block_rows, wide), BF16),
                vmem((2, NX, block_rows, wide), BF16),
                vmem(slots, BF16),
                vmem(slots, BF16),
                vmem((q_count, block_rows, block_rows), BF16),
                dma((5,)),
                dma((SEMS,)),
                dma((SEMS,)),
            ],
            compiler_params=pltpu.CompilerParams(
                collective_id=0, has_side_effects=True, vmem_limit_bytes=62 * 1024 * 1024
            ),
        )(*operands)

    out = run(
        irr_vectors,
        inv_dielectric[0].reshape(q_count, chunk, width),
        inv_dielectric[0],
        pair_density[0].reshape(q_count, block_rows, density_width),
        row_table,
        bits,
        minus_q,
        block_of_slot,
        held_slot,
        held_of_slot,
        send_slot,
    )
    return out.reshape(1, slab_rows, density_width)


def solution(mesh):
    in_specs = (
        P(None, ("pb", "ga"), None),
        P("pb", "ga", None),
        P("pb", "ga", None),
        P(),
        P(),
        P(),
        P(),
        P(),
    )
    out_specs = P("pb", "ga", None)
    return jax.shard_map(
        on_device, mesh=mesh, in_specs=in_specs, out_specs=out_specs, check_vma=False
    )
```

```python
import math

import jax
import jax.numpy as jnp
from jax import lax
from jax.experimental import pallas as pl
from jax.experimental.pallas import tpu as pltpu
from jax.sharding import PartitionSpec as P

MESH = pl.DeviceIdType.MESH
NX = 4
NC = 2
SEMS = 200
CAP = 3
BF16 = jnp.bfloat16
F32 = jnp.float32


def kernel(
    ratio,
    irr,
    dmat,
    drows,
    density,
    row_table,
    bits,
    minus_q,
    block_of_slot,
    held_slot,
    held_of_slot,
    send_slot,
    out,
    held,
    fwd,
    via_x,
    rho_tx,
    rho_rx_low,
    rho_rx_high,
    rho_group,
    part_tx,
    part_rx,
    acc,
    acc2,
    core_rx,
    core_rx2,
    sum_tx,
    sum_tx2,
    sum_rx,
    sum_rx2,
    mate_sum,
    coef,
    slab_sum,
    own_d,
    spread,
    chosen,
    mate_rows,
    mate_cols,
    mate_t,
    screened,
    mate_scr,
    res_low,
    res_high,
    mate_res,
    back_low,
    back_high,
    turn_back,
    local_sem,
    send_sem,
    recv_sem,
):
    q_count = lax.axis_size("pb")
    g_count = lax.axis_size("ga")
    pb = lax.axis_index("pb")
    ga = lax.axis_index("ga")
    y, x = pb // NX, pb % NX
    z, c = ga // NC, ga % NC
    z_count = g_count // NC
    sibling = z * NC + (1 - c)
    basis = own_d.shape[0]
    rows = row_table.shape[1]
    plus, minus, beyond = (lambda v: (v + 1) % NX), (lambda v: (v + 3) % NX), (lambda v: (v + 2) % NX)
    ahead, behind = (lambda v: (v + 1 + 2 * c) % NX), (lambda v: (v + 3 - 2 * c) % NX)
    up, down, across = plus(y), minus(y), beyond(y)
    parts = range(2)
    res = (res_low, res_high)
    rho_rx = (rho_rx_low, rho_rx_high)
    back = (back_low, back_high)
    wide = res_low.shape[2]
    started = []
    taken = [0]

    def sems(count):
        first = taken[0]
        taken[0] += count
        assert taken[0] <= SEMS
        return first

    def copy(src, dst, i, to):
        return pltpu.make_async_remote_copy(
            src_ref=src,
            dst_ref=dst,
            send_sem=send_sem.at[i],
            recv_sem=recv_sem.at[i],
            device_id=to,
            device_id_type=MESH,
        )

    def send(src, dst, i, to):
        one = copy(src, dst, i, to)
        one.start()
        started.append(one)

    def arrive(dst, i):
        copy(dst, dst, i, (pb, ga)).wait_recv()

    def on_x(t):
        return (y * NX + t, ga)

    def on_y(t):
        return (t * NX + x, ga)

    class Exchange:
        def __init__(self, me, to, src, dst, via):
            self.me, self.to, self.src, self.dst, self.via = me, to, src, dst, via
            self.i = sems(4)

        def start(self):
            me = self.me
            send(self.src(plus(me)), self.dst(me), self.i, self.to(plus(me)))
            send(self.src(minus(me)), self.dst(me), self.i + 1, self.to(minus(me)))
            send(self.src(beyond(me)), self.via, self.i + 2, self.to(ahead(me)))

        def forward(self):
            arrive(self.via, self.i + 2)
            send(self.via, self.dst(behind(self.me)), self.i + 3, self.to(ahead(self.me)))

        def from_minus(self):
            arrive(self.dst(minus(self.me)), self.i)

        def from_plus(self):
            arrive(self.dst(plus(self.me)), self.i + 1)

        def from_beyond(self):
            arrive(self.dst(beyond(self.me)), self.i + 3)

        def finish(self):
            self.from_minus()
            self.from_plus()
            self.from_beyond()

    load_rho = pltpu.make_async_copy(density, out, local_sem.at[0])
    load_rho.start()

    barrier = pltpu.get_barrier_semaphore()

    def greet_pb(d, carry):
        pl.semaphore_signal(
            barrier, inc=1, device_id=((pb + d) % q_count, ga), device_id_type=MESH
        )
        return carry

    def greet_ga(d, carry):
        pl.semaphore_signal(
            barrier, inc=1, device_id=(pb, (ga + d) % g_count), device_id_type=MESH
        )
        return carry

    lax.fori_loop(1, q_count, greet_pb, 0)
    lax.fori_loop(1, g_count, greet_ga, 0)
    pl.semaphore_wait(barrier, q_count + g_count - 2)

    own_irr = NX * (y % 2)
    next_irr = NX * ((y + 1) % 2)
    next_x = Exchange(x, on_x, lambda t: irr.at[next_irr + t], lambda s: fwd.at[s], via_x.at[0])
    own_x = Exchange(x, on_x, lambda t: irr.at[own_irr + t], lambda s: held.at[y, s], via_x.at[1])
    next_x.start()
    keep = pltpu.make_async_copy(irr.at[own_irr + x], held.at[y, x], local_sem.at[1])
    keep.start()
    y_sem = sems(8)

    def to_neighbours(k, source, src):
        there = held.at[y, source]
        send(src, there, y_sem + k, on_y(up))
        send(src, there, y_sem + 4 + k, on_y(down))

    to_neighbours(0, x, irr.at[next_irr + x])

    def turn_of(j):
        sources = lax.broadcasted_iota(jnp.int32, (rows, rows), 0)
        sign = (1 - 2 * bits[pl.ds(j, 1), :]).astype(F32)
        return jnp.where(row_table[pl.ds(j, 1), :] == sources, sign, 0.0)

    load_rho.wait()
    rho_sem = sems(2 * g_count)

    def rho_copy(h, d):
        to = (ga + d) % g_count
        return copy(
            rho_tx.at[h, pl.ds(to * CAP, CAP)],
            rho_rx[h].at[pl.ds(ga * CAP, CAP)],
            rho_sem + h * g_count + d,
            (pb, to),
        )

    for h in parts:

        def make_turned(j, carry):
            value = jnp.dot(
                turn_of(j).astype(BF16),
                out[j, :, h * wide : (h + 1) * wide],
                preferred_element_type=F32,
            )
            res[h][j] = value.astype(BF16)
            return carry

        def rho_start(k, carry):
            d = (k + 2) % (g_count - 1) + 1
            to = (ga + d) % g_count
            for i in range(CAP):
                rho_tx[h, to * CAP + i] = res[h][block_of_slot[to * CAP + i]]
            rho_copy(h, d).start()
            return carry

        lax.fori_loop(0, q_count, make_turned, 0)
        lax.fori_loop(0, g_count - 1, rho_start, 0)
        if h == 0:
            own_x.start()
        for i in range(CAP):
            rho_rx[h][ga * CAP + i] = res[h][block_of_slot[ga * CAP + i]]

    load_d = pltpu.make_async_copy(drows, own_d, local_sem.at[3])
    load_d.start()

    next_x.from_minus()
    to_neighbours(1, minus(x), fwd.at[minus(x)])
    next_x.from_plus()
    to_neighbours(2, plus(x), fwd.at[plus(x)])
    next_x.forward()

    def make_turn_back(j, carry):
        turn_back[j] = turn_of(j).T.astype(BF16)
        return carry

    lax.fori_loop(0, q_count, make_turn_back, 0)
    next_x.from_beyond()
    to_neighbours(3, beyond(x), fwd.at[beyond(x)])
    own_x.forward()

    def group(h, row):
        return jnp.concatenate([rho_rx[h][held_slot[row * NX + i]] for i in range(NX)], axis=0).T

    def project(row, values, total, first):
        def one(n, carry):
            columns = pl.ds(pl.multiple_of(n * basis, basis), basis)
            block = held[row, :, :, columns].reshape(-1, basis)
            part = jnp.dot(values[...], block, preferred_element_type=F32)
            total[n] = part if first else total[n] + part
            return carry

        lax.fori_loop(0, g_count, one, 0)

    part_sem = sems(4)
    for h in parts:

        def rho_wait(d, carry):
            source = (ga + g_count - d) % g_count
            arrive(rho_rx[h].at[pl.ds(source * CAP, CAP)], rho_sem + h * g_count + d)
            return carry

        lax.fori_loop(1, g_count, rho_wait, 0)
        part_tx[h] = group(h, across)
        send(part_tx.at[h], part_rx.at[h], part_sem + h, on_y(across))

    class Reduce:
        def __init__(self, total, landing, outgoing, incoming):
            self.total, self.landing = total, landing
            self.outgoing, self.incoming = outgoing, incoming
            self.i = sems(2 * z_count)

        def to_core(self, k):
            return copy(
                self.total.at[k * NC + (1 - c)], self.landing.at[k], self.i + k, (pb, sibling)
            )

        def start(self):
            for k in range(z_count):
                self.to_core(k).start()

        def sent(self):
            for k in range(z_count):
                self.to_core(k).wait_send()

        def along_z(self):
            for d in (2, 1, 3):
                k = (z + d) % z_count
                arrive(self.landing.at[k], self.i + k)
                self.outgoing[d] = (self.total[k * NC + c] + self.landing[k]).astype(BF16)
                send(
                    self.outgoing.at[d],
                    self.incoming.at[d],
                    self.i + z_count + d,
                    (pb, k * NC + c),
                )
            arrive(self.landing.at[z], self.i + z)

        def finish(self):
            value = self.total[ga] + self.landing[z]
            for d in (1, 3, 2):
                arrive(self.incoming.at[d], self.i + z_count + d)
                value = value + self.incoming[d].astype(F32)
            return value

    reduce1 = [Reduce(acc.at[h], core_rx.at[h], sum_tx.at[h], sum_rx.at[h]) for h in parts]
    reduce2 = [Reduce(acc2.at[h], core_rx2.at[h], sum_tx2.at[h], sum_rx2.at[h]) for h in parts]

    own_x.finish()
    keep.wait()
    for h in parts:
        arrive(part_rx.at[h], part_sem + h)
        project(y, part_rx.at[h], acc2.at[h], True)
        reduce2[h].start()
    for h in parts:
        rho_group[...] = group(h, y)
        project(y, rho_group, acc.at[h], True)
        reduce2[h].along_z()
    for k, s in enumerate((x, minus(x), plus(x), beyond(x))):
        arrive(held.at[down, s], y_sem + k)
        arrive(held.at[up, s], y_sem + 4 + k)
    d1_sem, d2_sem = sems(q_count), sems(q_count)

    def spread_copy(d):
        to = (pb + d) % q_count
        return copy(dmat.at[to], spread.at[pb], d1_sem + d, (to, ga))

    def spread_start(d, carry):
        spread_copy(d).start()
        return carry

    lax.fori_loop(1, q_count, spread_start, 0)
    keep_d1 = pltpu.make_async_copy(dmat.at[pb], spread.at[pb], local_sem.at[2])
    keep_d1.start()

    for h in parts:
        for row in (down, up):
            rho_group[...] = group(h, row)
            project(row, rho_group, acc.at[h], False)
        reduce1[h].start()
    def spread_wait(d, carry):
        arrive(spread.at[(pb + q_count - d) % q_count], d1_sem + d)
        return carry

    lax.fori_loop(1, q_count, spread_wait, 0)
    keep_d1.wait()

    def choose(q, carry):
        chosen[q] = spread[minus_q[q]]
        return carry

    lax.fori_loop(0, q_count, choose, 0)

    def mate_copy(d):
        to = (pb + d) % q_count
        return copy(chosen.at[to], mate_rows.at[pb], d2_sem + d, (to, ga))

    def mate_start(d, carry):
        mate_copy(d).start()
        return carry

    lax.fori_loop(1, q_count, mate_start, 0)
    keep_d2 = pltpu.make_async_copy(chosen.at[pb], mate_rows.at[pb], local_sem.at[2])
    keep_d2.start()

    for h in parts:
        mate_sum[h, 0] = reduce2[h].finish().astype(BF16)
        send(mate_sum.at[h, 0], mate_sum.at[h, 1], part_sem + 2 + h, on_y(across))
        reduce1[h].along_z()

    def mate_wait(d, carry):
        arrive(mate_rows.at[(pb + q_count - d) % q_count], d2_sem + d)
        return carry

    lax.fori_loop(1, q_count, mate_wait, 0)
    keep_d2.wait()

    column_sem = sems(g_count)

    def column_copy(d):
        to = (ga + d) % g_count
        columns = pl.ds(pl.multiple_of(to * basis, basis), basis)
        return copy(mate_rows.at[:, :, columns], mate_cols.at[ga], column_sem + d, (pb, to))

    def column_start(d, carry):
        column_copy(d).start()
        return carry

    lax.fori_loop(1, g_count, column_start, 0)
    own_columns = pl.ds(pl.multiple_of(ga * basis, basis), basis)
    keep_cols = pltpu.make_async_copy(
        mate_rows.at[:, :, own_columns], mate_cols.at[ga], local_sem.at[4]
    )
    keep_cols.start()

    class Gather:
        def __init__(self, ref, use):
            self.ref, self.use = ref, use
            self.i = sems(8)

        def start(self):
            mine = self.ref.at[ga]
            for d in (2, 1, 3):
                send(mine, mine, self.i + d, (pb, (z + d) % z_count * NC + c))
            send(mine, mine, self.i, (pb, sibling))

        def own(self):
            self.use(ga)

        def beside(self):
            arrive(self.ref.at[sibling], self.i)
            self.use(sibling)

        def along_z(self):
            for d in (1, 3, 2):
                source = (z + z_count - d) % z_count * NC + c
                there = self.ref.at[source]
                arrive(there, self.i + d)
                send(there, there, self.i + 4 + d, (pb, sibling))
                self.use(source)

        def rest(self):
            for d in (1, 3, 2):
                source = (z + z_count - d) % z_count * NC + (1 - c)
                arrive(self.ref.at[source], self.i + 4 + d)
                self.use(source)

    def column_wait(d, carry):
        arrive(mate_cols.at[(ga + g_count - d) % g_count], column_sem + d)
        return carry

    def apply(h):
        def use(n):
            columns = pl.ds(pl.multiple_of(n * basis, basis), basis)
            slab_sum[h] += jnp.dot(
                own_d[:, columns], coef[h, n], preferred_element_type=F32
            ) + jnp.dot(mate_t[:, columns], coef[h, n], preferred_element_type=F32)

        return use

    gather_coef = [Gather(coef.at[h], apply(h)) for h in parts]
    for h in parts:
        value = reduce1[h].finish()
        arrive(mate_sum.at[h, 1], part_sem + 2 + h)
        coef[h, ga] = (value + mate_sum[h, 1].astype(F32)).astype(BF16).T
        gather_coef[h].start()
    lax.fori_loop(1, g_count, column_wait, 0)
    keep_cols.wait()
    load_d.wait()

    def turn_columns(n, carry):
        columns = pl.ds(pl.multiple_of(n * basis, basis), basis)
        mate_t[:, columns] = mate_cols[n].reshape(basis, basis).T
        return carry

    lax.fori_loop(0, g_count, turn_columns, 0)
    slab_sum[...] = jnp.zeros_like(slab_sum)

    half = NX // 2

    def row_of(k):
        return (y + NX - 1 + k) % NX

    def expand(values, total, first_row, count):
        first = [True]

        def use(n):
            columns = pl.ds(pl.multiple_of(n * basis, basis), basis)
            fresh = first.pop() if first else False

            def one(k, carry):
                block = held[row_of(first_row + k), :, :, columns].reshape(-1, basis)
                value = jnp.dot(block, values[n], preferred_element_type=F32)
                value = value.reshape(half, -1, wide)
                place = pl.ds(k * half, half)
                total[place] = value if fresh else total[place] + value
                return carry

            lax.fori_loop(0, count, one, 0)

        return use

    mate_sem = sems(4)
    gather_own, gather_mate = [], []
    for h in parts:
        gather_own.append(
            Gather(screened.at[h], expand(screened.at[h], acc2.at[h], 0, NX - 1))
        )
        gather_mate.append(Gather(mate_scr.at[h], expand(mate_scr.at[h], acc.at[h], 1, 1)))
    for h in parts:
        gather_coef[h].own()
        gather_coef[h].beside()
    for h in parts:
        gather_coef[h].along_z()
        gather_coef[h].rest()
        screened[h, ga] = (0.5 * slab_sum[h] - coef[h, ga].astype(F32)).astype(BF16)
        send(screened.at[h, ga], mate_scr.at[h, ga], mate_sem + h, on_y(across))
        gather_own[h].start()
    for h in parts:
        reduce1[h].sent()
        reduce2[h].sent()
    for h in parts:
        gather_own[h].own()
        arrive(mate_scr.at[h, ga], mate_sem + h)
        gather_mate[h].start()

    def rho_sent(d, carry):
        for h in parts:
            rho_copy(h, d).wait_send()
        return carry

    lax.fori_loop(1, g_count, rho_sent, 0)
    back_sem = sems(2 * g_count)

    def back_copy(h, d):
        to = (ga + d) % g_count
        return copy(
            rho_tx.at[h, pl.ds(to * CAP, CAP)],
            back[h].at[pl.ds(ga * CAP, CAP)],
            back_sem + h * g_count + d,
            (pb, to),
        )

    for h in parts:
        gather_own[h].beside()
        gather_own[h].along_z()
        gather_mate[h].own()
        gather_mate[h].beside()
        gather_mate[h].along_z()
        gather_mate[h].rest()
        mate_res[h] = (acc[h, :half] * ratio).astype(BF16).reshape(NX, rows, wide)
        send(mate_res.at[h], res[h].at[pl.ds(y * NX, NX)], mate_sem + 2 + h, on_y(across))
        gather_own[h].rest()

        def finish_rows(k, carry):
            value = (acc2[h, pl.ds(k * half, half)] * ratio).astype(BF16)
            res[h][pl.ds(row_of(k) * NX, NX)] = value.reshape(NX, rows, wide)
            return carry

        lax.fori_loop(0, NX - 1, finish_rows, 0)
        arrive(res[h].at[pl.ds(across * NX, NX)], mate_sem + 2 + h)

        def back_start(k, carry):
            d = (k + 2) % (g_count - 1) + 1
            to = (ga + d) % g_count
            for i in range(CAP):
                rho_tx[h, to * CAP + i] = res[h][held_of_slot[to * CAP + i]]
            back_copy(h, d).start()
            return carry

        lax.fori_loop(0, g_count - 1, back_start, 0)
        for i in range(CAP):
            back[h][ga * CAP + i] = res[h][held_of_slot[ga * CAP + i]]

    for h in parts:

        def back_wait(d, carry):
            source = (ga + g_count - d) % g_count
            arrive(back[h].at[pl.ds(source * CAP, CAP)], back_sem + h * g_count + d)
            return carry

        def unturn(j, carry):
            value = jnp.dot(turn_back[j], back[h][send_slot[j]], preferred_element_type=F32)
            out[j, :, h * wide : (h + 1) * wide] = value.astype(BF16)
            return carry

        lax.fori_loop(1, g_count, back_wait, 0)
        lax.fori_loop(0, q_count, unturn, 0)

    for one in started:
        one.wait_send()

    def drain_pb(d, carry):
        spread_copy(d).wait_send()
        mate_copy(d).wait_send()
        return carry

    def drain_ga(d, carry):
        column_copy(d).wait_send()
        for h in parts:
            back_copy(h, d).wait_send()
        return carry

    lax.fori_loop(1, q_count, drain_pb, 0)
    lax.fori_loop(1, g_count, drain_ga, 0)


def on_device(
    irr_vectors, inv_dielectric, pair_density, minus_q, sym_op, rot_blocks, rot_rows, phase_bits
):
    q_count = lax.axis_size("pb")
    g_count = lax.axis_size("ga")
    owner = lax.axis_index("pb")
    slab_index = lax.axis_index("ga")
    irr_count, block_rows, width = irr_vectors.shape
    density_width = pair_density.shape[2]
    blocks_all = q_count * g_count
    slab_rows = q_count * block_rows
    basis_rows = width // g_count
    slot_count = g_count * CAP
    ratio = math.sqrt(slab_rows * g_count / width)

    operation = lax.dynamic_index_in_dim(sym_op, owner, 0, keepdims=False)
    table = lax.dynamic_index_in_dim(rot_blocks, operation, 0, keepdims=False)
    places = jnp.arange(blocks_all, dtype=jnp.int32)
    source_ga = table % g_count
    earlier = (places[None, :] < places[:, None]) & (
        places[None, :] // q_count == places[:, None] // q_count
    )
    ranks = jnp.sum(
        (earlier & (source_ga[None, :] == source_ga[:, None])).astype(jnp.int32), axis=1
    )
    mine_source = lax.dynamic_slice_in_dim(table, slab_index * q_count, q_count)
    mine_rank = lax.dynamic_slice_in_dim(ranks, slab_index * q_count, q_count)
    send_slot = mine_source % g_count * CAP + mine_rank
    slots = jnp.arange(slot_count, dtype=jnp.int32)
    local = jnp.arange(q_count, dtype=jnp.int32)
    block_of_slot = jnp.sum(
        jnp.where(slots[:, None] == send_slot[None, :], local[None, :], 0), axis=1
    )
    senders = local * g_count + slab_index
    match = table[None, :] == senders[:, None]
    dest_block = jnp.sum(jnp.where(match, places[None, :], 0), axis=1)
    dest_rank = jnp.sum(jnp.where(match, ranks[None, :], 0), axis=1)
    held_slot = dest_block // q_count * CAP + dest_rank
    held_of_slot = jnp.sum(
        jnp.where(slots[:, None] == held_slot[None, :], local[None, :], 0), axis=1
    )

    row_table = lax.dynamic_slice_in_dim(
        lax.dynamic_index_in_dim(rot_rows, operation, 0, keepdims=False),
        slab_index * q_count,
        q_count,
    )
    bits = lax.dynamic_slice_in_dim(
        lax.dynamic_index_in_dim(phase_bits, operation, 0, keepdims=False),
        slab_index * slab_rows,
        slab_rows,
    ).reshape(q_count, block_rows)

    vmem = pltpu.VMEM
    dma = pltpu.SemaphoreType.DMA
    wide = density_width // 2
    slab = (wide, basis_rows)
    square = (basis_rows, wide)
    slots = (slot_count, block_rows, wide)
    chunk = basis_rows // q_count
    any_spec = pl.BlockSpec(memory_space=pl.ANY)
    smem_spec = pl.BlockSpec(memory_space=pltpu.SMEM)
    vmem_spec = pl.BlockSpec(memory_space=pltpu.VMEM)

    def run(*operands):
        return pl.pallas_call(
            lambda *refs: kernel(ratio, *refs),
            out_shape=jax.ShapeDtypeStruct((q_count, block_rows, density_width), BF16),
            in_specs=[any_spec] * 4 + [vmem_spec] * 2 + [smem_spec] * 5,
            out_specs=vmem_spec,
            scratch_shapes=[
                vmem((NX, NX, block_rows, width), BF16),
                vmem((NX, block_rows, width), BF16),
                vmem((2, block_rows, width), BF16),
                vmem((2, *slots), BF16),
                vmem(slots, BF16),
                vmem(slots, BF16),
                vmem((wide, NX * block_rows), BF16),
                vmem((2, wide, NX * block_rows), BF16),
                vmem((2, wide, NX * block_rows), BF16),
                vmem((2, g_count, *slab), F32),
                vmem((2, g_count, *slab), F32),
                vmem((2, g_count // NC, *slab), F32),
                vmem((2, g_count // NC, *slab), F32),
                vmem((2, g_count // NC, *slab), BF16),
                vmem((2, g_count // NC, *slab), BF16),
                vmem((2, g_count // NC, *slab), BF16),
                vmem((2, g_count // NC, *slab), BF16),
                vmem((2, 2, *slab), BF16),
                vmem((2, g_count, *square), BF16),
                vmem((2, *square), F32),
                vmem((basis_rows, width), BF16),
                vmem((q_count, chunk, width), BF16),
                vmem((q_count, chunk, width), BF16),
                vmem((q_count, chunk, width), BF16),
                vmem((g_count, q_count, chunk, basis_rows), BF16),
                vmem((basis_rows, width), BF16),
                vmem((2, g_count, *square), BF16),
                vmem((2, g_count, *square), BF16),
                vmem((q_count, block_rows, wide), BF16),
                vmem((q_count, block_rows, wide), BF16),
                vmem((2, NX, block_rows, wide), BF16),
                vmem(slots, BF16),
                vmem(slots, BF16),
                vmem((q_count, block_rows, block_rows), BF16),
                dma((5,)),
                dma((SEMS,)),
                dma((SEMS,)),
            ],
            compiler_params=pltpu.CompilerParams(
                collective_id=0, has_side_effects=True, vmem_limit_bytes=62 * 1024 * 1024
            ),
        )(*operands)

    out = run(
        irr_vectors,
        inv_dielectric[0].reshape(q_count, chunk, width),
        inv_dielectric[0],
        pair_density[0].reshape(q_count, block_rows, density_width),
        row_table,
        bits,
        minus_q,
        block_of_slot,
        held_slot,
        held_of_slot,
        send_slot,
    )
    return out.reshape(1, slab_rows, density_width)


def solution(mesh):
    in_specs = (
        P(None, ("pb", "ga"), None),
        P("pb", "ga", None),
        P("pb", "ga", None),
        P(),
        P(),
        P(),
        P(),
        P(),
    )
    out_specs = P("pb", "ga", None)
    return jax.shard_map(
        on_device, mesh=mesh, in_specs=in_specs, out_specs=out_specs, check_vma=False
    )
```

```python
import math

import jax
import jax.numpy as jnp
from jax import lax
from jax.experimental import pallas as pl
from jax.experimental.pallas import tpu as pltpu
from jax.sharding import PartitionSpec as P

MESH = pl.DeviceIdType.MESH
NX = 4
NC = 2
SEMS = 200
CAP = 3
BF16 = jnp.bfloat16
F32 = jnp.float32


def kernel(
    ratio,
    irr,
    dmat,
    drows,
    density,
    row_table,
    bits,
    minus_q,
    block_of_slot,
    held_slot,
    held_of_slot,
    send_slot,
    out,
    held,
    fwd,
    via_x,
    rho_tx,
    rho_rx_low,
    rho_rx_high,
    rho_group,
    part_tx,
    part_rx,
    acc,
    acc2,
    core_rx,
    core_rx2,
    sum_tx,
    sum_tx2,
    sum_rx,
    sum_rx2,
    mate_sum,
    coef,
    slab_sum,
    own_d,
    spread,
    chosen,
    dcols,
    mate_cols,
    mate_t,
    screened,
    mate_scr,
    res_low,
    res_high,
    mate_res,
    back_low,
    back_high,
    turn_back,
    local_sem,
    send_sem,
    recv_sem,
):
    q_count = lax.axis_size("pb")
    g_count = lax.axis_size("ga")
    pb = lax.axis_index("pb")
    ga = lax.axis_index("ga")
    y, x = pb // NX, pb % NX
    z, c = ga // NC, ga % NC
    z_count = g_count // NC
    sibling = z * NC + (1 - c)
    basis = own_d.shape[0]
    rows = row_table.shape[1]
    plus, minus, beyond = (lambda v: (v + 1) % NX), (lambda v: (v + 3) % NX), (lambda v: (v + 2) % NX)
    ahead, behind = (lambda v: (v + 1 + 2 * c) % NX), (lambda v: (v + 3 - 2 * c) % NX)
    up, down, across = plus(y), minus(y), beyond(y)
    parts = range(2)
    res = (res_low, res_high)
    rho_rx = (rho_rx_low, rho_rx_high)
    back = (back_low, back_high)
    wide = res_low.shape[2]
    started = []
    taken = [0]

    def sems(count):
        first = taken[0]
        taken[0] += count
        assert taken[0] <= SEMS
        return first

    def copy(src, dst, i, to):
        return pltpu.make_async_remote_copy(
            src_ref=src,
            dst_ref=dst,
            send_sem=send_sem.at[i],
            recv_sem=recv_sem.at[i],
            device_id=to,
            device_id_type=MESH,
        )

    def send(src, dst, i, to):
        one = copy(src, dst, i, to)
        one.start()
        started.append(one)

    def arrive(dst, i):
        copy(dst, dst, i, (pb, ga)).wait_recv()

    def on_x(t):
        return (y * NX + t, ga)

    def on_y(t):
        return (t * NX + x, ga)

    class Exchange:
        def __init__(self, me, to, src, dst, via):
            self.me, self.to, self.src, self.dst, self.via = me, to, src, dst, via
            self.i = sems(4)

        def start(self):
            me = self.me
            send(self.src(plus(me)), self.dst(me), self.i, self.to(plus(me)))
            send(self.src(minus(me)), self.dst(me), self.i + 1, self.to(minus(me)))
            send(self.src(beyond(me)), self.via, self.i + 2, self.to(ahead(me)))

        def forward(self):
            arrive(self.via, self.i + 2)
            send(self.via, self.dst(behind(self.me)), self.i + 3, self.to(ahead(self.me)))

        def from_minus(self):
            arrive(self.dst(minus(self.me)), self.i)

        def from_plus(self):
            arrive(self.dst(plus(self.me)), self.i + 1)

        def from_beyond(self):
            arrive(self.dst(beyond(self.me)), self.i + 3)

        def finish(self):
            self.from_minus()
            self.from_plus()
            self.from_beyond()

    load_rho = pltpu.make_async_copy(density, out, local_sem.at[0])
    load_rho.start()

    barrier = pltpu.get_barrier_semaphore()

    def greet_pb(d, carry):
        pl.semaphore_signal(
            barrier, inc=1, device_id=((pb + d) % q_count, ga), device_id_type=MESH
        )
        return carry

    def greet_ga(d, carry):
        pl.semaphore_signal(
            barrier, inc=1, device_id=(pb, (ga + d) % g_count), device_id_type=MESH
        )
        return carry

    lax.fori_loop(1, q_count, greet_pb, 0)
    lax.fori_loop(1, g_count, greet_ga, 0)
    pl.semaphore_wait(barrier, q_count + g_count - 2)

    own_irr = NX * (y % 2)
    next_irr = NX * ((y + 1) % 2)
    next_x = Exchange(x, on_x, lambda t: irr.at[next_irr + t], lambda s: fwd.at[s], via_x.at[0])
    own_x = Exchange(x, on_x, lambda t: irr.at[own_irr + t], lambda s: held.at[y, s], via_x.at[1])
    next_x.start()
    keep = pltpu.make_async_copy(irr.at[own_irr + x], held.at[y, x], local_sem.at[1])
    keep.start()
    y_sem = sems(8)

    def to_neighbours(k, source, src):
        there = held.at[y, source]
        send(src, there, y_sem + k, on_y(up))
        send(src, there, y_sem + 4 + k, on_y(down))

    to_neighbours(0, x, irr.at[next_irr + x])

    def turn_of(j):
        sources = lax.broadcasted_iota(jnp.int32, (rows, rows), 0)
        sign = (1 - 2 * bits[pl.ds(j, 1), :]).astype(F32)
        return jnp.where(row_table[pl.ds(j, 1), :] == sources, sign, 0.0)

    load_rho.wait()
    rho_sem = sems(2 * g_count)

    def rho_copy(h, d):
        to = (ga + d) % g_count
        return copy(
            rho_tx.at[h, pl.ds(to * CAP, CAP)],
            rho_rx[h].at[pl.ds(ga * CAP, CAP)],
            rho_sem + h * g_count + d,
            (pb, to),
        )

    for h in parts:

        def make_turned(j, carry):
            value = jnp.dot(
                turn_of(j).astype(BF16),
                out[j, :, h * wide : (h + 1) * wide],
                preferred_element_type=F32,
            )
            res[h][j] = value.astype(BF16)
            return carry

        def rho_start(k, carry):
            d = (k + 2) % (g_count - 1) + 1
            to = (ga + d) % g_count
            for i in range(CAP):
                rho_tx[h, to * CAP + i] = res[h][block_of_slot[to * CAP + i]]
            rho_copy(h, d).start()
            return carry

        lax.fori_loop(0, q_count, make_turned, 0)
        lax.fori_loop(0, g_count - 1, rho_start, 0)
        for i in range(CAP):
            rho_rx[h][ga * CAP + i] = res[h][block_of_slot[ga * CAP + i]]

    load_d = pltpu.make_async_copy(drows, own_d, local_sem.at[3])
    load_d.start()

    next_x.from_minus()
    to_neighbours(1, minus(x), fwd.at[minus(x)])
    next_x.from_plus()
    to_neighbours(2, plus(x), fwd.at[plus(x)])
    next_x.forward()
    own_x.start()

    def make_turn_back(j, carry):
        turn_back[j] = turn_of(j).T.astype(BF16)
        return carry

    lax.fori_loop(0, q_count, make_turn_back, 0)
    next_x.from_beyond()
    to_neighbours(3, beyond(x), fwd.at[beyond(x)])
    own_x.forward()

    def group(h, row):
        return jnp.concatenate([rho_rx[h][held_slot[row * NX + i]] for i in range(NX)], axis=0).T

    def project(row, values, total, first):
        def one(n, carry):
            columns = pl.ds(pl.multiple_of(n * basis, basis), basis)
            block = held[row, :, :, columns].reshape(-1, basis)
            part = jnp.dot(values[...], block, preferred_element_type=F32)
            total[n] = part if first else total[n] + part
            return carry

        lax.fori_loop(0, g_count, one, 0)

    part_sem = sems(4)
    column_sem = sems(g_count)

    def column_copy(d):
        to = (ga + d) % g_count
        columns = pl.ds(pl.multiple_of(to * basis, basis), basis)
        return copy(dmat.at[:, :, columns], dcols.at[ga], column_sem + d, (pb, to))

    def column_start(d, carry):
        column_copy(d).start()
        return carry

    own_columns = pl.ds(pl.multiple_of(ga * basis, basis), basis)
    keep_cols = pltpu.make_async_copy(
        dmat.at[:, :, own_columns], dcols.at[ga], local_sem.at[4]
    )

    for h in parts:
        if h:
            lax.fori_loop(1, g_count, column_start, 0)
            keep_cols.start()

        def rho_wait(d, carry):
            source = (ga + g_count - d) % g_count
            arrive(rho_rx[h].at[pl.ds(source * CAP, CAP)], rho_sem + h * g_count + d)
            return carry

        lax.fori_loop(1, g_count, rho_wait, 0)
        part_tx[h] = group(h, across)
        send(part_tx.at[h], part_rx.at[h], part_sem + h, on_y(across))

    class Reduce:
        def __init__(self, total, landing, outgoing, incoming):
            self.total, self.landing = total, landing
            self.outgoing, self.incoming = outgoing, incoming
            self.i = sems(2 * z_count)

        def to_core(self, k):
            return copy(
                self.total.at[k * NC + (1 - c)], self.landing.at[k], self.i + k, (pb, sibling)
            )

        def start(self):
            for k in range(z_count):
                self.to_core(k).start()

        def sent(self):
            for k in range(z_count):
                self.to_core(k).wait_send()

        def along_z(self):
            for d in (2, 1, 3):
                k = (z + d) % z_count
                arrive(self.landing.at[k], self.i + k)
                self.outgoing[d] = (self.total[k * NC + c] + self.landing[k]).astype(BF16)
                send(
                    self.outgoing.at[d],
                    self.incoming.at[d],
                    self.i + z_count + d,
                    (pb, k * NC + c),
                )
            arrive(self.landing.at[z], self.i + z)

        def finish(self):
            value = self.total[ga] + self.landing[z]
            for d in (1, 3, 2):
                arrive(self.incoming.at[d], self.i + z_count + d)
                value = value + self.incoming[d].astype(F32)
            return value

    reduce1 = [Reduce(acc.at[h], core_rx.at[h], sum_tx.at[h], sum_rx.at[h]) for h in parts]
    reduce2 = [Reduce(acc2.at[h], core_rx2.at[h], sum_tx2.at[h], sum_rx2.at[h]) for h in parts]

    own_x.finish()
    keep.wait()
    def column_wait(d, carry):
        arrive(dcols.at[(ga + g_count - d) % g_count], column_sem + d)
        return carry

    lax.fori_loop(1, g_count, column_wait, 0)
    keep_cols.wait()
    d1_sem, d2_sem = sems(q_count), sems(q_count)

    def spread_copy(d):
        to = (pb + d) % q_count
        return copy(dcols.at[to // 2, to % 2], spread.at[pb], d1_sem + d, (to, ga))

    def spread_start(d, carry):
        spread_copy(d).start()
        return carry

    lax.fori_loop(1, q_count, spread_start, 0)
    keep_d1 = pltpu.make_async_copy(dcols.at[pb // 2, pb % 2], spread.at[pb], local_sem.at[2])
    keep_d1.start()

    for h in parts:
        arrive(part_rx.at[h], part_sem + h)
        project(y, part_rx.at[h], acc2.at[h], True)
        reduce2[h].start()
    for h in parts:
        rho_group[...] = group(h, y)
        project(y, rho_group, acc.at[h], True)
        reduce2[h].along_z()
    for k, s in enumerate((x, minus(x), plus(x), beyond(x))):
        arrive(held.at[down, s], y_sem + k)
        arrive(held.at[up, s], y_sem + 4 + k)
    def spread_wait(d, carry):
        arrive(spread.at[(pb + q_count - d) % q_count], d1_sem + d)
        return carry

    lax.fori_loop(1, q_count, spread_wait, 0)
    keep_d1.wait()

    def choose(q, carry):
        chosen[q] = spread[minus_q[q]]
        return carry

    lax.fori_loop(0, q_count, choose, 0)

    def mate_copy(d):
        to = (pb + d) % q_count
        return copy(chosen.at[to], mate_cols.at[pb], d2_sem + d, (to, ga))

    def mate_start(d, carry):
        mate_copy(d).start()
        return carry

    lax.fori_loop(1, q_count, mate_start, 0)
    keep_d2 = pltpu.make_async_copy(chosen.at[pb], mate_cols.at[pb], local_sem.at[2])
    keep_d2.start()

    for h in parts:
        for row in (down, up):
            rho_group[...] = group(h, row)
            project(row, rho_group, acc.at[h], False)
        reduce1[h].start()
    for h in parts:
        mate_sum[h, 0] = reduce2[h].finish().astype(BF16)
        send(mate_sum.at[h, 0], mate_sum.at[h, 1], part_sem + 2 + h, on_y(across))
        reduce1[h].along_z()

    class Gather:
        def __init__(self, ref, use):
            self.ref, self.use = ref, use
            self.i = sems(8)

        def start(self):
            mine = self.ref.at[ga]
            for d in (2, 1, 3):
                send(mine, mine, self.i + d, (pb, (z + d) % z_count * NC + c))
            send(mine, mine, self.i, (pb, sibling))

        def own(self):
            self.use(ga)

        def beside(self):
            arrive(self.ref.at[sibling], self.i)
            self.use(sibling)

        def along_z(self):
            for d in (1, 3, 2):
                source = (z + z_count - d) % z_count * NC + c
                there = self.ref.at[source]
                arrive(there, self.i + d)
                send(there, there, self.i + 4 + d, (pb, sibling))
                self.use(source)

        def rest(self):
            for d in (1, 3, 2):
                source = (z + z_count - d) % z_count * NC + (1 - c)
                arrive(self.ref.at[source], self.i + 4 + d)
                self.use(source)

    def apply(h):
        def use(n):
            columns = pl.ds(pl.multiple_of(n * basis, basis), basis)
            slab_sum[h] += jnp.dot(
                own_d[:, columns], coef[h, n], preferred_element_type=F32
            ) + jnp.dot(mate_t[:, columns], coef[h, n], preferred_element_type=F32)

        return use

    gather_coef = [Gather(coef.at[h], apply(h)) for h in parts]
    for h in parts:
        value = reduce1[h].finish()
        arrive(mate_sum.at[h, 1], part_sem + 2 + h)
        coef[h, ga] = (value + mate_sum[h, 1].astype(F32)).astype(BF16).T
        gather_coef[h].start()

    def mate_wait(d, carry):
        arrive(mate_cols.at[(pb + q_count - d) % q_count], d2_sem + d)
        return carry

    lax.fori_loop(1, q_count, mate_wait, 0)
    keep_d2.wait()
    load_d.wait()
    chunk = mate_cols.shape[1]

    def turn_columns(k, carry):
        mate_t[:, pl.ds(pl.multiple_of(k * chunk, chunk), chunk)] = mate_cols[k].T
        return carry

    lax.fori_loop(0, q_count, turn_columns, 0)
    slab_sum[...] = jnp.zeros_like(slab_sum)

    half = NX // 2

    def row_of(k):
        return (y + NX - 1 + k) % NX

    def expand(values, total, first_row, count):
        first = [True]

        def use(n):
            columns = pl.ds(pl.multiple_of(n * basis, basis), basis)
            fresh = first.pop() if first else False

            def one(k, carry):
                block = held[row_of(first_row + k), :, :, columns].reshape(-1, basis)
                value = jnp.dot(block, values[n], preferred_element_type=F32)
                value = value.reshape(half, -1, wide)
                place = pl.ds(k * half, half)
                total[place] = value if fresh else total[place] + value
                return carry

            lax.fori_loop(0, count, one, 0)

        return use

    mate_sem = sems(4)
    gather_own, gather_mate = [], []
    for h in parts:
        gather_own.append(
            Gather(screened.at[h], expand(screened.at[h], acc2.at[h], 0, NX - 1))
        )
        gather_mate.append(Gather(mate_scr.at[h], expand(mate_scr.at[h], acc.at[h], 1, 1)))
    for h in parts:
        gather_coef[h].own()
        gather_coef[h].beside()
    for h in parts:
        gather_coef[h].along_z()
        gather_coef[h].rest()
        screened[h, ga] = (0.5 * slab_sum[h] - coef[h, ga].astype(F32)).astype(BF16)
        send(screened.at[h, ga], mate_scr.at[h, ga], mate_sem + h, on_y(across))
        gather_own[h].start()
    for h in parts:
        reduce1[h].sent()
        reduce2[h].sent()
    for h in parts:
        gather_own[h].own()
        arrive(mate_scr.at[h, ga], mate_sem + h)
        gather_mate[h].start()

    def rho_sent(d, carry):
        for h in parts:
            rho_copy(h, d).wait_send()
        return carry

    lax.fori_loop(1, g_count, rho_sent, 0)
    back_sem = sems(2 * g_count)

    def back_copy(h, d):
        to = (ga + d) % g_count
        return copy(
            rho_tx.at[h, pl.ds(to * CAP, CAP)],
            back[h].at[pl.ds(ga * CAP, CAP)],
            back_sem + h * g_count + d,
            (pb, to),
        )

    for h in parts:
        gather_own[h].beside()
        gather_own[h].along_z()
        gather_mate[h].own()
        gather_mate[h].beside()
        gather_mate[h].along_z()
        gather_mate[h].rest()
        mate_res[h] = (acc[h, :half] * ratio).astype(BF16).reshape(NX, rows, wide)
        send(mate_res.at[h], res[h].at[pl.ds(y * NX, NX)], mate_sem + 2 + h, on_y(across))
        gather_own[h].rest()

        def finish_rows(k, carry):
            value = (acc2[h, pl.ds(k * half, half)] * ratio).astype(BF16)
            res[h][pl.ds(row_of(k) * NX, NX)] = value.reshape(NX, rows, wide)
            return carry

        lax.fori_loop(0, NX - 1, finish_rows, 0)
        arrive(res[h].at[pl.ds(across * NX, NX)], mate_sem + 2 + h)

        def back_start(k, carry):
            d = (k + 2) % (g_count - 1) + 1
            to = (ga + d) % g_count
            for i in range(CAP):
                rho_tx[h, to * CAP + i] = res[h][held_of_slot[to * CAP + i]]
            back_copy(h, d).start()
            return carry

        lax.fori_loop(0, g_count - 1, back_start, 0)
        for i in range(CAP):
            back[h][ga * CAP + i] = res[h][held_of_slot[ga * CAP + i]]

    for h in parts:

        def back_wait(d, carry):
            source = (ga + g_count - d) % g_count
            arrive(back[h].at[pl.ds(source * CAP, CAP)], back_sem + h * g_count + d)
            return carry

        def unturn(j, carry):
            value = jnp.dot(turn_back[j], back[h][send_slot[j]], preferred_element_type=F32)
            out[j, :, h * wide : (h + 1) * wide] = value.astype(BF16)
            return carry

        lax.fori_loop(1, g_count, back_wait, 0)
        lax.fori_loop(0, q_count, unturn, 0)

    for one in started:
        one.wait_send()

    def drain_pb(d, carry):
        spread_copy(d).wait_send()
        mate_copy(d).wait_send()
        return carry

    def drain_ga(d, carry):
        column_copy(d).wait_send()
        for h in parts:
            back_copy(h, d).wait_send()
        return carry

    lax.fori_loop(1, q_count, drain_pb, 0)
    lax.fori_loop(1, g_count, drain_ga, 0)


def on_device(
    irr_vectors, inv_dielectric, pair_density, minus_q, sym_op, rot_blocks, rot_rows, phase_bits
):
    q_count = lax.axis_size("pb")
    g_count = lax.axis_size("ga")
    owner = lax.axis_index("pb")
    slab_index = lax.axis_index("ga")
    irr_count, block_rows, width = irr_vectors.shape
    density_width = pair_density.shape[2]
    blocks_all = q_count * g_count
    slab_rows = q_count * block_rows
    basis_rows = width // g_count
    slot_count = g_count * CAP
    ratio = math.sqrt(slab_rows * g_count / width)

    operation = lax.dynamic_index_in_dim(sym_op, owner, 0, keepdims=False)
    table = lax.dynamic_index_in_dim(rot_blocks, operation, 0, keepdims=False)
    places = jnp.arange(blocks_all, dtype=jnp.int32)
    source_ga = table % g_count
    earlier = (places[None, :] < places[:, None]) & (
        places[None, :] // q_count == places[:, None] // q_count
    )
    ranks = jnp.sum(
        (earlier & (source_ga[None, :] == source_ga[:, None])).astype(jnp.int32), axis=1
    )
    mine_source = lax.dynamic_slice_in_dim(table, slab_index * q_count, q_count)
    mine_rank = lax.dynamic_slice_in_dim(ranks, slab_index * q_count, q_count)
    send_slot = mine_source % g_count * CAP + mine_rank
    slots = jnp.arange(slot_count, dtype=jnp.int32)
    local = jnp.arange(q_count, dtype=jnp.int32)
    block_of_slot = jnp.sum(
        jnp.where(slots[:, None] == send_slot[None, :], local[None, :], 0), axis=1
    )
    senders = local * g_count + slab_index
    match = table[None, :] == senders[:, None]
    dest_block = jnp.sum(jnp.where(match, places[None, :], 0), axis=1)
    dest_rank = jnp.sum(jnp.where(match, ranks[None, :], 0), axis=1)
    held_slot = dest_block // q_count * CAP + dest_rank
    held_of_slot = jnp.sum(
        jnp.where(slots[:, None] == held_slot[None, :], local[None, :], 0), axis=1
    )

    row_table = lax.dynamic_slice_in_dim(
        lax.dynamic_index_in_dim(rot_rows, operation, 0, keepdims=False),
        slab_index * q_count,
        q_count,
    )
    bits = lax.dynamic_slice_in_dim(
        lax.dynamic_index_in_dim(phase_bits, operation, 0, keepdims=False),
        slab_index * slab_rows,
        slab_rows,
    ).reshape(q_count, block_rows)

    vmem = pltpu.VMEM
    dma = pltpu.SemaphoreType.DMA
    wide = density_width // 2
    slab = (wide, basis_rows)
    square = (basis_rows, wide)
    slots = (slot_count, block_rows, wide)
    chunk = width // q_count
    any_spec = pl.BlockSpec(memory_space=pl.ANY)
    smem_spec = pl.BlockSpec(memory_space=pltpu.SMEM)
    vmem_spec = pl.BlockSpec(memory_space=pltpu.VMEM)

    def run(*operands):
        return pl.pallas_call(
            lambda *refs: kernel(ratio, *refs),
            out_shape=jax.ShapeDtypeStruct((q_count, block_rows, density_width), BF16),
            in_specs=[any_spec] * 4 + [vmem_spec] * 2 + [smem_spec] * 5,
            out_specs=vmem_spec,
            scratch_shapes=[
                vmem((NX, NX, block_rows, width), BF16),
                vmem((NX, block_rows, width), BF16),
                vmem((2, block_rows, width), BF16),
                vmem((2, *slots), BF16),
                vmem(slots, BF16),
                vmem(slots, BF16),
                vmem((wide, NX * block_rows), BF16),
                vmem((2, wide, NX * block_rows), BF16),
                vmem((2, wide, NX * block_rows), BF16),
                vmem((2, g_count, *slab), F32),
                vmem((2, g_count, *slab), F32),
                vmem((2, g_count // NC, *slab), F32),
                vmem((2, g_count // NC, *slab), F32),
                vmem((2, g_count // NC, *slab), BF16),
                vmem((2, g_count // NC, *slab), BF16),
                vmem((2, g_count // NC, *slab), BF16),
                vmem((2, g_count // NC, *slab), BF16),
                vmem((2, 2, *slab), BF16),
                vmem((2, g_count, *square), BF16),
                vmem((2, *square), F32),
                vmem((basis_rows, width), BF16),
                vmem((q_count, chunk, basis_rows), BF16),
                vmem((q_count, chunk, basis_rows), BF16),
                vmem((g_count, 2, chunk, basis_rows), BF16),
                vmem((q_count, chunk, basis_rows), BF16),
                vmem((basis_rows, width), BF16),
                vmem((2, g_count, *square), BF16),
                vmem((2, g_count, *square), BF16),
                vmem((q_count, block_rows, wide), BF16),
                vmem((q_count, block_rows, wide), BF16),
                vmem((2, NX, block_rows, wide), BF16),
                vmem(slots, BF16),
                vmem(slots, BF16),
                vmem((q_count, block_rows, block_rows), BF16),
                dma((5,)),
                dma((SEMS,)),
                dma((SEMS,)),
            ],
            compiler_params=pltpu.CompilerParams(
                collective_id=0, has_side_effects=True, vmem_limit_bytes=62 * 1024 * 1024
            ),
        )(*operands)

    out = run(
        irr_vectors,
        inv_dielectric[0].reshape(2, chunk, width),
        inv_dielectric[0],
        pair_density[0].reshape(q_count, block_rows, density_width),
        row_table,
        bits,
        minus_q,
        block_of_slot,
        held_slot,
        held_of_slot,
        send_slot,
    )
    return out.reshape(1, slab_rows, density_width)


def solution(mesh):
    in_specs = (
        P(None, ("pb", "ga"), None),
        P("pb", "ga", None),
        P("pb", "ga", None),
        P(),
        P(),
        P(),
        P(),
        P(),
    )
    out_specs = P("pb", "ga", None)
    return jax.shard_map(
        on_device, mesh=mesh, in_specs=in_specs, out_specs=out_specs, check_vma=False
    )
```

```python
import math

import jax
import jax.numpy as jnp
from jax import lax
from jax.experimental import pallas as pl
from jax.experimental.pallas import tpu as pltpu
from jax.sharding import PartitionSpec as P

MESH = pl.DeviceIdType.MESH
NX = 4
NC = 2
SEMS = 200
CAP = 3
BF16 = jnp.bfloat16
F32 = jnp.float32


def kernel(
    ratio,
    irr,
    dmat,
    drows,
    density,
    row_table,
    bits,
    minus_q,
    block_of_slot,
    held_slot,
    held_of_slot,
    send_slot,
    out,
    held,
    fwd,
    via_x,
    rho_tx,
    rho_rx_low,
    rho_rx_high,
    rho_group,
    part_tx,
    part_rx,
    acc,
    acc2,
    core_rx,
    core_rx2,
    sum_tx,
    sum_tx2,
    sum_rx,
    sum_rx2,
    mate_sum,
    coef,
    slab_sum,
    own_d,
    spread,
    chosen,
    dcols,
    mate_cols,
    mate_t,
    screened,
    mate_scr,
    res_low,
    res_high,
    mate_res,
    back_low,
    back_high,
    turn_back,
    local_sem,
    send_sem,
    recv_sem,
):
    q_count = lax.axis_size("pb")
    g_count = lax.axis_size("ga")
    pb = lax.axis_index("pb")
    ga = lax.axis_index("ga")
    y, x = pb // NX, pb % NX
    z, c = ga // NC, ga % NC
    z_count = g_count // NC
    sibling = z * NC + (1 - c)
    basis = own_d.shape[0]
    rows = row_table.shape[1]
    plus, minus, beyond = (lambda v: (v + 1) % NX), (lambda v: (v + 3) % NX), (lambda v: (v + 2) % NX)
    ahead, behind = (lambda v: (v + 1 + 2 * c) % NX), (lambda v: (v + 3 - 2 * c) % NX)
    up, down, across = plus(y), minus(y), beyond(y)
    parts = range(2)
    res = (res_low, res_high)
    rho_rx = (rho_rx_low, rho_rx_high)
    back = (back_low, back_high)
    wide = res_low.shape[2]
    started = []
    taken = [0]

    def sems(count):
        first = taken[0]
        taken[0] += count
        assert taken[0] <= SEMS
        return first

    def copy(src, dst, i, to):
        return pltpu.make_async_remote_copy(
            src_ref=src,
            dst_ref=dst,
            send_sem=send_sem.at[i],
            recv_sem=recv_sem.at[i],
            device_id=to,
            device_id_type=MESH,
        )

    def send(src, dst, i, to):
        one = copy(src, dst, i, to)
        one.start()
        started.append(one)

    def arrive(dst, i):
        copy(dst, dst, i, (pb, ga)).wait_recv()

    def on_x(t):
        return (y * NX + t, ga)

    def on_y(t):
        return (t * NX + x, ga)

    class Exchange:
        def __init__(self, me, to, src, dst, via):
            self.me, self.to, self.src, self.dst, self.via = me, to, src, dst, via
            self.i = sems(4)

        def start(self):
            me = self.me
            send(self.src(plus(me)), self.dst(me), self.i, self.to(plus(me)))
            send(self.src(minus(me)), self.dst(me), self.i + 1, self.to(minus(me)))
            send(self.src(beyond(me)), self.via, self.i + 2, self.to(ahead(me)))

        def forward(self):
            arrive(self.via, self.i + 2)
            send(self.via, self.dst(behind(self.me)), self.i + 3, self.to(ahead(self.me)))

        def from_minus(self):
            arrive(self.dst(minus(self.me)), self.i)

        def from_plus(self):
            arrive(self.dst(plus(self.me)), self.i + 1)

        def from_beyond(self):
            arrive(self.dst(beyond(self.me)), self.i + 3)

        def finish(self):
            self.from_minus()
            self.from_plus()
            self.from_beyond()

    load_rho = pltpu.make_async_copy(density, out, local_sem.at[0])
    load_rho.start()

    barrier = pltpu.get_barrier_semaphore()

    def greet_pb(d, carry):
        pl.semaphore_signal(
            barrier, inc=1, device_id=((pb + d) % q_count, ga), device_id_type=MESH
        )
        return carry

    def greet_ga(d, carry):
        pl.semaphore_signal(
            barrier, inc=1, device_id=(pb, (ga + d) % g_count), device_id_type=MESH
        )
        return carry

    lax.fori_loop(1, q_count, greet_pb, 0)
    lax.fori_loop(1, g_count, greet_ga, 0)
    pl.semaphore_wait(barrier, q_count + g_count - 2)

    own_irr = NX * (y % 2)
    next_irr = NX * ((y + 1) % 2)
    next_x = Exchange(x, on_x, lambda t: irr.at[next_irr + t], lambda s: fwd.at[s], via_x.at[0])
    own_x = Exchange(x, on_x, lambda t: irr.at[own_irr + t], lambda s: held.at[y, s], via_x.at[1])
    next_x.start()
    keep = pltpu.make_async_copy(irr.at[own_irr + x], held.at[y, x], local_sem.at[1])
    keep.start()
    y_sem = sems(8)

    def to_neighbours(k, source, src):
        there = held.at[y, source]
        send(src, there, y_sem + k, on_y(up))
        send(src, there, y_sem + 4 + k, on_y(down))

    to_neighbours(0, x, irr.at[next_irr + x])

    def turn_of(j):
        sources = lax.broadcasted_iota(jnp.int32, (rows, rows), 0)
        sign = (1 - 2 * bits[pl.ds(j, 1), :]).astype(F32)
        return jnp.where(row_table[pl.ds(j, 1), :] == sources, sign, 0.0)

    load_rho.wait()
    rho_sem = sems(2 * g_count)

    def rho_copy(h, d):
        to = (ga + d) % g_count
        return copy(
            rho_tx.at[h, pl.ds(to * CAP, CAP)],
            rho_rx[h].at[pl.ds(ga * CAP, CAP)],
            rho_sem + h * g_count + d,
            (pb, to),
        )

    for h in parts:

        def make_turned(j, carry):
            value = jnp.dot(
                turn_of(j).astype(BF16),
                out[j, :, h * wide : (h + 1) * wide],
                preferred_element_type=F32,
            )
            res[h][j] = value.astype(BF16)
            return carry

        def rho_start(k, carry):
            d = (k + 2) % (g_count - 1) + 1
            to = (ga + d) % g_count
            for i in range(CAP):
                rho_tx[h, to * CAP + i] = res[h][block_of_slot[to * CAP + i]]
            rho_copy(h, d).start()
            return carry

        lax.fori_loop(0, q_count, make_turned, 0)
        lax.fori_loop(0, g_count - 1, rho_start, 0)
        for i in range(CAP):
            rho_rx[h][ga * CAP + i] = res[h][block_of_slot[ga * CAP + i]]

    load_d = pltpu.make_async_copy(drows, own_d, local_sem.at[3])
    load_d.start()

    next_x.from_minus()
    to_neighbours(1, minus(x), fwd.at[minus(x)])
    next_x.from_plus()
    to_neighbours(2, plus(x), fwd.at[plus(x)])
    next_x.forward()
    own_x.start()

    def make_turn_back(j, carry):
        turn_back[j] = turn_of(j).T.astype(BF16)
        return carry

    lax.fori_loop(0, q_count, make_turn_back, 0)
    next_x.from_beyond()
    to_neighbours(3, beyond(x), fwd.at[beyond(x)])
    own_x.forward()

    def group(h, row):
        return jnp.concatenate([rho_rx[h][held_slot[row * NX + i]] for i in range(NX)], axis=0).T

    def project(row, values, total, first):
        def one(n, carry):
            columns = pl.ds(pl.multiple_of(n * basis, basis), basis)
            block = held[row, :, :, columns].reshape(-1, basis)
            part = jnp.dot(values[...], block, preferred_element_type=F32)
            total[n] = part if first else total[n] + part
            return carry

        lax.fori_loop(0, g_count, one, 0)

    part_sem = sems(4)
    column_sem = sems(g_count)

    def column_copy(d):
        to = (ga + d) % g_count
        columns = pl.ds(pl.multiple_of(to * basis, basis), basis)
        return copy(dmat.at[:, :, columns], dcols.at[ga], column_sem + d, (pb, to))

    def column_start(d, carry):
        column_copy(d).start()
        return carry

    own_columns = pl.ds(pl.multiple_of(ga * basis, basis), basis)
    keep_cols = pltpu.make_async_copy(
        dmat.at[:, :, own_columns], dcols.at[ga], local_sem.at[4]
    )

    for h in parts:
        if h:
            lax.fori_loop(1, g_count, column_start, 0)
            keep_cols.start()

        def rho_wait(d, carry):
            source = (ga + g_count - d) % g_count
            arrive(rho_rx[h].at[pl.ds(source * CAP, CAP)], rho_sem + h * g_count + d)
            return carry

        lax.fori_loop(1, g_count, rho_wait, 0)
        part_tx[h] = group(h, across)
        send(part_tx.at[h], part_rx.at[h], part_sem + h, on_y(across))

    class Reduce:
        def __init__(self, total, landing, outgoing, incoming):
            self.total, self.landing = total, landing
            self.outgoing, self.incoming = outgoing, incoming
            self.i = sems(2 * z_count)

        def to_core(self, k):
            return copy(
                self.total.at[k * NC + (1 - c)], self.landing.at[k], self.i + k, (pb, sibling)
            )

        def start(self):
            for k in range(z_count):
                self.to_core(k).start()

        def sent(self):
            for k in range(z_count):
                self.to_core(k).wait_send()

        def along_z(self):
            for d in (2, 1, 3):
                k = (z + d) % z_count
                arrive(self.landing.at[k], self.i + k)
                self.outgoing[d] = (self.total[k * NC + c] + self.landing[k]).astype(BF16)
                send(
                    self.outgoing.at[d],
                    self.incoming.at[d],
                    self.i + z_count + d,
                    (pb, k * NC + c),
                )
            arrive(self.landing.at[z], self.i + z)

        def finish(self):
            value = self.total[ga] + self.landing[z]
            for d in (1, 3, 2):
                arrive(self.incoming.at[d], self.i + z_count + d)
                value = value + self.incoming[d].astype(F32)
            return value

    reduce1 = [Reduce(acc.at[h], core_rx.at[h], sum_tx.at[h], sum_rx.at[h]) for h in parts]
    reduce2 = [Reduce(acc2.at[h], core_rx2.at[h], sum_tx2.at[h], sum_rx2.at[h]) for h in parts]

    own_x.finish()
    keep.wait()
    for h in parts:
        arrive(part_rx.at[h], part_sem + h)
        project(y, part_rx.at[h], acc2.at[h], True)
        reduce2[h].start()
    for h in parts:
        rho_group[...] = group(h, y)
        project(y, rho_group, acc.at[h], True)
        reduce2[h].along_z()
    for k, s in enumerate((x, minus(x), plus(x), beyond(x))):
        arrive(held.at[down, s], y_sem + k)
        arrive(held.at[up, s], y_sem + 4 + k)
    def column_wait(d, carry):
        arrive(dcols.at[(ga + g_count - d) % g_count], column_sem + d)
        return carry

    lax.fori_loop(1, g_count, column_wait, 0)
    keep_cols.wait()
    d1_sem, d2_sem = sems(q_count), sems(q_count)

    def spread_copy(d):
        to = (pb + d) % q_count
        return copy(dcols.at[to // 2, to % 2], spread.at[pb], d1_sem + d, (to, ga))

    def spread_start(d, carry):
        spread_copy(d).start()
        return carry

    lax.fori_loop(1, q_count, spread_start, 0)
    keep_d1 = pltpu.make_async_copy(dcols.at[pb // 2, pb % 2], spread.at[pb], local_sem.at[2])
    keep_d1.start()

    for h in parts:
        for row in (down, up):
            rho_group[...] = group(h, row)
            project(row, rho_group, acc.at[h], False)
        reduce1[h].start()
    def spread_wait(d, carry):
        arrive(spread.at[(pb + q_count - d) % q_count], d1_sem + d)
        return carry

    lax.fori_loop(1, q_count, spread_wait, 0)
    keep_d1.wait()

    def choose(q, carry):
        chosen[q] = spread[minus_q[q]]
        return carry

    lax.fori_loop(0, q_count, choose, 0)

    def mate_copy(d):
        to = (pb + d) % q_count
        return copy(chosen.at[to], mate_cols.at[pb], d2_sem + d, (to, ga))

    def mate_start(d, carry):
        mate_copy(d).start()
        return carry

    lax.fori_loop(1, q_count, mate_start, 0)
    keep_d2 = pltpu.make_async_copy(chosen.at[pb], mate_cols.at[pb], local_sem.at[2])
    keep_d2.start()

    for h in parts:
        mate_sum[h, 0] = reduce2[h].finish().astype(BF16)
        send(mate_sum.at[h, 0], mate_sum.at[h, 1], part_sem + 2 + h, on_y(across))
        reduce1[h].along_z()

    class Gather:
        def __init__(self, ref, use):
            self.ref, self.use = ref, use
            self.i = sems(8)

        def start(self):
            mine = self.ref.at[ga]
            for d in (2, 1, 3):
                send(mine, mine, self.i + d, (pb, (z + d) % z_count * NC + c))
            send(mine, mine, self.i, (pb, sibling))

        def own(self):
            self.use(ga)

        def beside(self):
            arrive(self.ref.at[sibling], self.i)
            self.use(sibling)

        def along_z(self):
            for d in (1, 3, 2):
                source = (z + z_count - d) % z_count * NC + c
                there = self.ref.at[source]
                arrive(there, self.i + d)
                send(there, there, self.i + 4 + d, (pb, sibling))
                self.use(source)

        def rest(self):
            for d in (1, 3, 2):
                source = (z + z_count - d) % z_count * NC + (1 - c)
                arrive(self.ref.at[source], self.i + 4 + d)
                self.use(source)

    def apply(h):
        def use(n):
            columns = pl.ds(pl.multiple_of(n * basis, basis), basis)
            slab_sum[h] += jnp.dot(
                own_d[:, columns], coef[h, n], preferred_element_type=F32
            ) + jnp.dot(mate_t[:, columns], coef[h, n], preferred_element_type=F32)

        return use

    gather_coef = [Gather(coef.at[h], apply(h)) for h in parts]
    for h in parts:
        value = reduce1[h].finish()
        arrive(mate_sum.at[h, 1], part_sem + 2 + h)
        coef[h, ga] = (value + mate_sum[h, 1].astype(F32)).astype(BF16).T
        gather_coef[h].start()

    def mate_wait(d, carry):
        arrive(mate_cols.at[(pb + q_count - d) % q_count], d2_sem + d)
        return carry

    lax.fori_loop(1, q_count, mate_wait, 0)
    keep_d2.wait()
    load_d.wait()
    chunk = mate_cols.shape[1]

    def turn_columns(k, carry):
        mate_t[:, pl.ds(pl.multiple_of(k * chunk, chunk), chunk)] = mate_cols[k].T
        return carry

    lax.fori_loop(0, q_count, turn_columns, 0)
    slab_sum[...] = jnp.zeros_like(slab_sum)

    half = NX // 2

    def row_of(k):
        return (y + NX - 1 + k) % NX

    def expand(values, total, first_row, count):
        first = [True]

        def use(n):
            columns = pl.ds(pl.multiple_of(n * basis, basis), basis)
            fresh = first.pop() if first else False

            def one(k, carry):
                block = held[row_of(first_row + k), :, :, columns].reshape(-1, basis)
                value = jnp.dot(block, values[n], preferred_element_type=F32)
                value = value.reshape(half, -1, wide)
                place = pl.ds(k * half, half)
                total[place] = value if fresh else total[place] + value
                return carry

            lax.fori_loop(0, count, one, 0)

        return use

    mate_sem = sems(4)
    gather_own, gather_mate = [], []
    for h in parts:
        gather_own.append(
            Gather(screened.at[h], expand(screened.at[h], acc2.at[h], 0, NX - 1))
        )
        gather_mate.append(Gather(mate_scr.at[h], expand(mate_scr.at[h], acc.at[h], 1, 1)))
    for h in parts:
        gather_coef[h].own()
        gather_coef[h].beside()
    for h in parts:
        gather_coef[h].along_z()
        gather_coef[h].rest()
        screened[h, ga] = (0.5 * slab_sum[h] - coef[h, ga].astype(F32)).astype(BF16)
        send(screened.at[h, ga], mate_scr.at[h, ga], mate_sem + h, on_y(across))
        gather_own[h].start()
    for h in parts:
        reduce1[h].sent()
        reduce2[h].sent()
    for h in parts:
        gather_own[h].own()
        arrive(mate_scr.at[h, ga], mate_sem + h)
        gather_mate[h].start()

    def rho_sent(d, carry):
        for h in parts:
            rho_copy(h, d).wait_send()
        return carry

    lax.fori_loop(1, g_count, rho_sent, 0)
    back_sem = sems(2 * g_count)

    def back_copy(h, d):
        to = (ga + d) % g_count
        return copy(
            rho_tx.at[h, pl.ds(to * CAP, CAP)],
            back[h].at[pl.ds(ga * CAP, CAP)],
            back_sem + h * g_count + d,
            (pb, to),
        )

    for h in parts:
        gather_own[h].beside()
        gather_own[h].along_z()
        gather_mate[h].own()
        gather_mate[h].beside()
        gather_mate[h].along_z()
        gather_mate[h].rest()
        mate_res[h] = (acc[h, :half] * ratio).astype(BF16).reshape(NX, rows, wide)
        send(mate_res.at[h], res[h].at[pl.ds(y * NX, NX)], mate_sem + 2 + h, on_y(across))
        gather_own[h].rest()

        def finish_rows(k, carry):
            value = (acc2[h, pl.ds(k * half, half)] * ratio).astype(BF16)
            res[h][pl.ds(row_of(k) * NX, NX)] = value.reshape(NX, rows, wide)
            return carry

        lax.fori_loop(0, NX - 1, finish_rows, 0)
        arrive(res[h].at[pl.ds(across * NX, NX)], mate_sem + 2 + h)

        def back_start(k, carry):
            d = (k + 2) % (g_count - 1) + 1
            to = (ga + d) % g_count
            for i in range(CAP):
                rho_tx[h, to * CAP + i] = res[h][held_of_slot[to * CAP + i]]
            back_copy(h, d).start()
            return carry

        lax.fori_loop(0, g_count - 1, back_start, 0)
        for i in range(CAP):
            back[h][ga * CAP + i] = res[h][held_of_slot[ga * CAP + i]]

    for h in parts:

        def back_wait(d, carry):
            source = (ga + g_count - d) % g_count
            arrive(back[h].at[pl.ds(source * CAP, CAP)], back_sem + h * g_count + d)
            return carry

        def unturn(j, carry):
            value = jnp.dot(turn_back[j], back[h][send_slot[j]], preferred_element_type=F32)
            out[j, :, h * wide : (h + 1) * wide] = value.astype(BF16)
            return carry

        lax.fori_loop(1, g_count, back_wait, 0)
        lax.fori_loop(0, q_count, unturn, 0)

    for one in started:
        one.wait_send()

    def drain_pb(d, carry):
        spread_copy(d).wait_send()
        mate_copy(d).wait_send()
        return carry

    def drain_ga(d, carry):
        column_copy(d).wait_send()
        for h in parts:
            back_copy(h, d).wait_send()
        return carry

    lax.fori_loop(1, q_count, drain_pb, 0)
    lax.fori_loop(1, g_count, drain_ga, 0)


def on_device(
    irr_vectors, inv_dielectric, pair_density, minus_q, sym_op, rot_blocks, rot_rows, phase_bits
):
    q_count = lax.axis_size("pb")
    g_count = lax.axis_size("ga")
    owner = lax.axis_index("pb")
    slab_index = lax.axis_index("ga")
    irr_count, block_rows, width = irr_vectors.shape
    density_width = pair_density.shape[2]
    blocks_all = q_count * g_count
    slab_rows = q_count * block_rows
    basis_rows = width // g_count
    slot_count = g_count * CAP
    ratio = math.sqrt(slab_rows * g_count / width)

    operation = lax.dynamic_index_in_dim(sym_op, owner, 0, keepdims=False)
    table = lax.dynamic_index_in_dim(rot_blocks, operation, 0, keepdims=False)
    places = jnp.arange(blocks_all, dtype=jnp.int32)
    source_ga = table % g_count
    earlier = (places[None, :] < places[:, None]) & (
        places[None, :] // q_count == places[:, None] // q_count
    )
    ranks = jnp.sum(
        (earlier & (source_ga[None, :] == source_ga[:, None])).astype(jnp.int32), axis=1
    )
    mine_source = lax.dynamic_slice_in_dim(table, slab_index * q_count, q_count)
    mine_rank = lax.dynamic_slice_in_dim(ranks, slab_index * q_count, q_count)
    send_slot = mine_source % g_count * CAP + mine_rank
    slots = jnp.arange(slot_count, dtype=jnp.int32)
    local = jnp.arange(q_count, dtype=jnp.int32)
    block_of_slot = jnp.sum(
        jnp.where(slots[:, None] == send_slot[None, :], local[None, :], 0), axis=1
    )
    senders = local * g_count + slab_index
    match = table[None, :] == senders[:, None]
    dest_block = jnp.sum(jnp.where(match, places[None, :], 0), axis=1)
    dest_rank = jnp.sum(jnp.where(match, ranks[None, :], 0), axis=1)
    held_slot = dest_block // q_count * CAP + dest_rank
    held_of_slot = jnp.sum(
        jnp.where(slots[:, None] == held_slot[None, :], local[None, :], 0), axis=1
    )

    row_table = lax.dynamic_slice_in_dim(
        lax.dynamic_index_in_dim(rot_rows, operation, 0, keepdims=False),
        slab_index * q_count,
        q_count,
    )
    bits = lax.dynamic_slice_in_dim(
        lax.dynamic_index_in_dim(phase_bits, operation, 0, keepdims=False),
        slab_index * slab_rows,
        slab_rows,
    ).reshape(q_count, block_rows)

    vmem = pltpu.VMEM
    dma = pltpu.SemaphoreType.DMA
    wide = density_width // 2
    slab = (wide, basis_rows)
    square = (basis_rows, wide)
    slots = (slot_count, block_rows, wide)
    chunk = width // q_count
    any_spec = pl.BlockSpec(memory_space=pl.ANY)
    smem_spec = pl.BlockSpec(memory_space=pltpu.SMEM)
    vmem_spec = pl.BlockSpec(memory_space=pltpu.VMEM)

    def run(*operands):
        return pl.pallas_call(
            lambda *refs: kernel(ratio, *refs),
            out_shape=jax.ShapeDtypeStruct((q_count, block_rows, density_width), BF16),
            in_specs=[any_spec] * 4 + [vmem_spec] * 2 + [smem_spec] * 5,
            out_specs=vmem_spec,
            scratch_shapes=[
                vmem((NX, NX, block_rows, width), BF16),
                vmem((NX, block_rows, width), BF16),
                vmem((2, block_rows, width), BF16),
                vmem((2, *slots), BF16),
                vmem(slots, BF16),
                vmem(slots, BF16),
                vmem((wide, NX * block_rows), BF16),
                vmem((2, wide, NX * block_rows), BF16),
                vmem((2, wide, NX * block_rows), BF16),
                vmem((2, g_count, *slab), F32),
                vmem((2, g_count, *slab), F32),
                vmem((2, g_count // NC, *slab), F32),
                vmem((2, g_count // NC, *slab), F32),
                vmem((2, g_count // NC, *slab), BF16),
                vmem((2, g_count // NC, *slab), BF16),
                vmem((2, g_count // NC, *slab), BF16),
                vmem((2, g_count // NC, *slab), BF16),
                vmem((2, 2, *slab), BF16),
                vmem((2, g_count, *square), BF16),
                vmem((2, *square), F32),
                vmem((basis_rows, width), BF16),
                vmem((q_count, chunk, basis_rows), BF16),
                vmem((q_count, chunk, basis_rows), BF16),
                vmem((g_count, 2, chunk, basis_rows), BF16),
                vmem((q_count, chunk, basis_rows), BF16),
                vmem((basis_rows, width), BF16),
                vmem((2, g_count, *square), BF16),
                vmem((2, g_count, *square), BF16),
                vmem((q_count, block_rows, wide), BF16),
                vmem((q_count, block_rows, wide), BF16),
                vmem((2, NX, block_rows, wide), BF16),
                vmem(slots, BF16),
                vmem(slots, BF16),
                vmem((q_count, block_rows, block_rows), BF16),
                dma((5,)),
                dma((SEMS,)),
                dma((SEMS,)),
            ],
            compiler_params=pltpu.CompilerParams(
                collective_id=0, has_side_effects=True, vmem_limit_bytes=62 * 1024 * 1024
            ),
        )(*operands)

    out = run(
        irr_vectors,
        inv_dielectric[0].reshape(2, chunk, width),
        inv_dielectric[0],
        pair_density[0].reshape(q_count, block_rows, density_width),
        row_table,
        bits,
        minus_q,
        block_of_slot,
        held_slot,
        held_of_slot,
        send_slot,
    )
    return out.reshape(1, slab_rows, density_width)


def solution(mesh):
    in_specs = (
        P(None, ("pb", "ga"), None),
        P("pb", "ga", None),
        P("pb", "ga", None),
        P(),
        P(),
        P(),
        P(),
        P(),
    )
    out_specs = P("pb", "ga", None)
    return jax.shard_map(
        on_device, mesh=mesh, in_specs=in_specs, out_specs=out_specs, check_vma=False
    )
```

```python
import math

import jax
import jax.numpy as jnp
from jax import lax
from jax.experimental import pallas as pl
from jax.experimental.pallas import tpu as pltpu
from jax.sharding import PartitionSpec as P

MESH = pl.DeviceIdType.MESH
NX = 4
NC = 2
SEMS = 200
CAP = 3
BF16 = jnp.bfloat16
F32 = jnp.float32


def kernel(
    ratio,
    irr,
    dmat,
    drows,
    density,
    row_table,
    bits,
    minus_q,
    block_of_slot,
    held_slot,
    held_of_slot,
    send_slot,
    out,
    held,
    fwd,
    via_x,
    rho_tx,
    rho_rx_low,
    rho_rx_high,
    rho_group,
    part_tx,
    part_rx,
    acc,
    acc2,
    core_rx,
    core_rx2,
    sum_tx,
    sum_tx2,
    sum_rx,
    sum_rx2,
    mate_sum,
    coef,
    slab_sum,
    own_d,
    spread,
    chosen,
    dcols,
    mate_cols,
    mate_t,
    screened,
    mate_scr,
    res_low,
    res_high,
    mate_res,
    back_low,
    back_high,
    turn_back,
    local_sem,
    send_sem,
    recv_sem,
):
    q_count = lax.axis_size("pb")
    g_count = lax.axis_size("ga")
    pb = lax.axis_index("pb")
    ga = lax.axis_index("ga")
    y, x = pb // NX, pb % NX
    z, c = ga // NC, ga % NC
    z_count = g_count // NC
    sibling = z * NC + (1 - c)
    basis = own_d.shape[0]
    rows = row_table.shape[1]
    plus, minus, beyond = (lambda v: (v + 1) % NX), (lambda v: (v + 3) % NX), (lambda v: (v + 2) % NX)
    ahead, behind = (lambda v: (v + 1 + 2 * c) % NX), (lambda v: (v + 3 - 2 * c) % NX)
    up, down, across = plus(y), minus(y), beyond(y)
    parts = range(2)
    res = (res_low, res_high)
    rho_rx = (rho_rx_low, rho_rx_high)
    back = (back_low, back_high)
    wide = res_low.shape[2]
    started = []
    taken = [0]

    def sems(count):
        first = taken[0]
        taken[0] += count
        assert taken[0] <= SEMS
        return first

    def copy(src, dst, i, to):
        return pltpu.make_async_remote_copy(
            src_ref=src,
            dst_ref=dst,
            send_sem=send_sem.at[i],
            recv_sem=recv_sem.at[i],
            device_id=to,
            device_id_type=MESH,
        )

    def send(src, dst, i, to):
        one = copy(src, dst, i, to)
        one.start()
        started.append(one)

    def arrive(dst, i):
        copy(dst, dst, i, (pb, ga)).wait_recv()

    def on_x(t):
        return (y * NX + t, ga)

    def on_y(t):
        return (t * NX + x, ga)

    class Exchange:
        def __init__(self, me, to, src, dst, via):
            self.me, self.to, self.src, self.dst, self.via = me, to, src, dst, via
            self.i = sems(4)

        def start(self):
            me = self.me
            send(self.src(plus(me)), self.dst(me), self.i, self.to(plus(me)))
            send(self.src(minus(me)), self.dst(me), self.i + 1, self.to(minus(me)))
            send(self.src(beyond(me)), self.via, self.i + 2, self.to(ahead(me)))

        def forward(self):
            arrive(self.via, self.i + 2)
            send(self.via, self.dst(behind(self.me)), self.i + 3, self.to(ahead(self.me)))

        def from_minus(self):
            arrive(self.dst(minus(self.me)), self.i)

        def from_plus(self):
            arrive(self.dst(plus(self.me)), self.i + 1)

        def from_beyond(self):
            arrive(self.dst(beyond(self.me)), self.i + 3)

        def finish(self):
            self.from_minus()
            self.from_plus()
            self.from_beyond()

    load_rho = pltpu.make_async_copy(density, out, local_sem.at[0])
    load_rho.start()

    barrier = pltpu.get_barrier_semaphore()

    def greet_pb(d, carry):
        pl.semaphore_signal(
            barrier, inc=1, device_id=((pb + d) % q_count, ga), device_id_type=MESH
        )
        return carry

    def greet_ga(d, carry):
        pl.semaphore_signal(
            barrier, inc=1, device_id=(pb, (ga + d) % g_count), device_id_type=MESH
        )
        return carry

    lax.fori_loop(1, q_count, greet_pb, 0)
    lax.fori_loop(1, g_count, greet_ga, 0)
    pl.semaphore_wait(barrier, q_count + g_count - 2)

    own_irr = NX * (y % 2)
    next_irr = NX * ((y + 1) % 2)
    next_x = Exchange(x, on_x, lambda t: irr.at[next_irr + t], lambda s: fwd.at[s], via_x.at[0])
    own_x = Exchange(x, on_x, lambda t: irr.at[own_irr + t], lambda s: held.at[y, s], via_x.at[1])
    next_x.start()
    keep = pltpu.make_async_copy(irr.at[own_irr + x], held.at[y, x], local_sem.at[1])
    keep.start()
    y_sem = sems(8)

    def to_neighbours(k, source, src):
        there = held.at[y, source]
        send(src, there, y_sem + k, on_y(up))
        send(src, there, y_sem + 4 + k, on_y(down))

    to_neighbours(0, x, irr.at[next_irr + x])

    def turn_of(j):
        sources = lax.broadcasted_iota(jnp.int32, (rows, rows), 0)
        sign = (1 - 2 * bits[pl.ds(j, 1), :]).astype(F32)
        return jnp.where(row_table[pl.ds(j, 1), :] == sources, sign, 0.0)

    load_rho.wait()
    rho_sem = sems(2 * g_count)

    def rho_copy(h, d):
        to = (ga + d) % g_count
        return copy(
            rho_tx.at[h, pl.ds(to * CAP, CAP)],
            rho_rx[h].at[pl.ds(ga * CAP, CAP)],
            rho_sem + h * g_count + d,
            (pb, to),
        )

    for h in parts:

        def make_turned(j, carry):
            value = jnp.dot(
                turn_of(j).astype(BF16),
                out[j, :, h * wide : (h + 1) * wide],
                preferred_element_type=F32,
            )
            res[h][j] = value.astype(BF16)
            return carry

        def rho_start(k, carry):
            d = (k + 2) % (g_count - 1) + 1
            to = (ga + d) % g_count
            for i in range(CAP):
                rho_tx[h, to * CAP + i] = res[h][block_of_slot[to * CAP + i]]
            rho_copy(h, d).start()
            return carry

        lax.fori_loop(0, q_count, make_turned, 0)
        lax.fori_loop(0, g_count - 1, rho_start, 0)
        for i in range(CAP):
            rho_rx[h][ga * CAP + i] = res[h][block_of_slot[ga * CAP + i]]

    load_d = pltpu.make_async_copy(drows, own_d, local_sem.at[3])
    load_d.start()

    next_x.from_minus()
    to_neighbours(1, minus(x), fwd.at[minus(x)])
    next_x.from_plus()
    to_neighbours(2, plus(x), fwd.at[plus(x)])
    next_x.forward()
    own_x.start()

    def make_turn_back(j, carry):
        turn_back[j] = turn_of(j).T.astype(BF16)
        return carry

    lax.fori_loop(0, q_count, make_turn_back, 0)
    next_x.from_beyond()
    to_neighbours(3, beyond(x), fwd.at[beyond(x)])
    own_x.forward()

    def group(h, row):
        return jnp.concatenate([rho_rx[h][held_slot[row * NX + i]] for i in range(NX)], axis=0).T

    def project(row, values, total, first):
        def one(n, carry):
            columns = pl.ds(pl.multiple_of(n * basis, basis), basis)
            block = held[row, :, :, columns].reshape(-1, basis)
            part = jnp.dot(values[...], block, preferred_element_type=F32)
            total[n] = part if first else total[n] + part
            return carry

        lax.fori_loop(0, g_count, one, 0)

    part_sem = sems(4)
    column_sem = sems(g_count)

    def column_copy(d):
        to = (ga + d) % g_count
        columns = pl.ds(pl.multiple_of(to * basis, basis), basis)
        return copy(dmat.at[:, :, columns], dcols.at[ga], column_sem + d, (pb, to))

    def column_start(d, carry):
        column_copy(d).start()
        return carry

    own_columns = pl.ds(pl.multiple_of(ga * basis, basis), basis)
    keep_cols = pltpu.make_async_copy(
        dmat.at[:, :, own_columns], dcols.at[ga], local_sem.at[4]
    )

    for h in parts:
        if h:
            lax.fori_loop(1, g_count, column_start, 0)
            keep_cols.start()

        def rho_wait(d, carry):
            source = (ga + g_count - d) % g_count
            arrive(rho_rx[h].at[pl.ds(source * CAP, CAP)], rho_sem + h * g_count + d)
            return carry

        lax.fori_loop(1, g_count, rho_wait, 0)
        part_tx[h] = group(h, across)
        send(part_tx.at[h], part_rx.at[h], part_sem + h, on_y(across))

    class Reduce:
        def __init__(self, total, landing, outgoing, incoming):
            self.total, self.landing = total, landing
            self.outgoing, self.incoming = outgoing, incoming
            self.i = sems(2 * z_count)

        def to_core(self, k):
            return copy(
                self.total.at[k * NC + (1 - c)], self.landing.at[k], self.i + k, (pb, sibling)
            )

        def start(self):
            for k in range(z_count):
                self.to_core(k).start()

        def sent(self):
            for k in range(z_count):
                self.to_core(k).wait_send()

        def along_z(self):
            for d in (2, 1, 3):
                k = (z + d) % z_count
                arrive(self.landing.at[k], self.i + k)
                self.outgoing[d] = (self.total[k * NC + c] + self.landing[k]).astype(BF16)
                send(
                    self.outgoing.at[d],
                    self.incoming.at[d],
                    self.i + z_count + d,
                    (pb, k * NC + c),
                )
            arrive(self.landing.at[z], self.i + z)

        def finish(self):
            value = self.total[ga] + self.landing[z]
            for d in (1, 3, 2):
                arrive(self.incoming.at[d], self.i + z_count + d)
                value = value + self.incoming[d].astype(F32)
            return value

    reduce1 = [Reduce(acc.at[h], core_rx.at[h], sum_tx.at[h], sum_rx.at[h]) for h in parts]
    reduce2 = [Reduce(acc2.at[h], core_rx2.at[h], sum_tx2.at[h], sum_rx2.at[h]) for h in parts]

    own_x.finish()
    keep.wait()
    for h in parts:
        arrive(part_rx.at[h], part_sem + h)
        project(y, part_rx.at[h], acc2.at[h], True)
        reduce2[h].start()
    for h in parts:
        rho_group[...] = group(h, y)
        project(y, rho_group, acc.at[h], True)
        reduce2[h].along_z()
    for k, s in enumerate((x, minus(x), plus(x), beyond(x))):
        arrive(held.at[down, s], y_sem + k)
        arrive(held.at[up, s], y_sem + 4 + k)
    def column_wait(d, carry):
        arrive(dcols.at[(ga + g_count - d) % g_count], column_sem + d)
        return carry

    lax.fori_loop(1, g_count, column_wait, 0)
    keep_cols.wait()
    d1_sem, d2_sem = sems(q_count), sems(q_count)

    def spread_copy(d):
        to = (pb + d) % q_count
        return copy(dcols.at[to // 2, to % 2], spread.at[pb], d1_sem + d, (to, ga))

    def spread_start(d, carry):
        spread_copy(d).start()
        return carry

    lax.fori_loop(1, q_count, spread_start, 0)
    keep_d1 = pltpu.make_async_copy(dcols.at[pb // 2, pb % 2], spread.at[pb], local_sem.at[2])
    keep_d1.start()

    for h in parts:
        for row in (down, up):
            rho_group[...] = group(h, row)
            project(row, rho_group, acc.at[h], False)
        reduce1[h].start()
    def spread_wait(d, carry):
        arrive(spread.at[(pb + q_count - d) % q_count], d1_sem + d)
        return carry

    lax.fori_loop(1, q_count, spread_wait, 0)
    keep_d1.wait()

    def choose(q, carry):
        chosen[q] = spread[minus_q[q]]
        return carry

    lax.fori_loop(0, q_count, choose, 0)

    def mate_copy(d):
        to = (pb + d) % q_count
        return copy(chosen.at[to], mate_cols.at[pb], d2_sem + d, (to, ga))

    def mate_start(d, carry):
        mate_copy(d).start()
        return carry

    lax.fori_loop(1, q_count, mate_start, 0)
    keep_d2 = pltpu.make_async_copy(chosen.at[pb], mate_cols.at[pb], local_sem.at[2])
    keep_d2.start()

    for h in parts:
        mate_sum[h, 0] = reduce2[h].finish().astype(BF16)
        send(mate_sum.at[h, 0], mate_sum.at[h, 1], part_sem + 2 + h, on_y(across))
        reduce1[h].along_z()

    class Gather:
        def __init__(self, ref, use):
            self.ref, self.use = ref, use
            self.i = sems(8)

        def start(self):
            mine = self.ref.at[ga]
            for d in (2, 1, 3):
                send(mine, mine, self.i + d, (pb, (z + d) % z_count * NC + c))
            send(mine, mine, self.i, (pb, sibling))

        def own(self):
            self.use(ga)

        def beside(self):
            arrive(self.ref.at[sibling], self.i)
            self.use(sibling)

        def along_z(self):
            for d in (1, 3, 2):
                source = (z + z_count - d) % z_count * NC + c
                there = self.ref.at[source]
                arrive(there, self.i + d)
                send(there, there, self.i + 4 + d, (pb, sibling))
                self.use(source)

        def rest(self):
            for d in (1, 3, 2):
                source = (z + z_count - d) % z_count * NC + (1 - c)
                arrive(self.ref.at[source], self.i + 4 + d)
                self.use(source)

    def apply(h):
        def use(n):
            columns = pl.ds(pl.multiple_of(n * basis, basis), basis)
            slab_sum[h] += jnp.dot(
                own_d[:, columns], coef[h, n], preferred_element_type=F32
            ) + jnp.dot(mate_t[:, columns], coef[h, n], preferred_element_type=F32)

        return use

    gather_coef = [Gather(coef.at[h], apply(h)) for h in parts]
    for h in parts:
        value = reduce1[h].finish()
        arrive(mate_sum.at[h, 1], part_sem + 2 + h)
        coef[h, ga] = (value + mate_sum[h, 1].astype(F32)).astype(BF16).T
        gather_coef[h].start()

    def mate_wait(d, carry):
        arrive(mate_cols.at[(pb + q_count - d) % q_count], d2_sem + d)
        return carry

    lax.fori_loop(1, q_count, mate_wait, 0)
    keep_d2.wait()
    load_d.wait()
    chunk = mate_cols.shape[1]

    def turn_columns(k, carry):
        mate_t[:, pl.ds(pl.multiple_of(k * chunk, chunk), chunk)] = mate_cols[k].T
        return carry

    lax.fori_loop(0, q_count, turn_columns, 0)
    slab_sum[...] = jnp.zeros_like(slab_sum)

    half = NX // 2

    def row_of(k):
        return (y + NX - 1 + k) % NX

    def expand(values, total, first_row, count):
        first = [True]

        def use(n):
            columns = pl.ds(pl.multiple_of(n * basis, basis), basis)
            fresh = first.pop() if first else False

            def one(k, carry):
                block = held[row_of(first_row + k), :, :, columns].reshape(-1, basis)
                value = jnp.dot(block, values[n], preferred_element_type=F32)
                value = value.reshape(half, -1, wide)
                place = pl.ds(k * half, half)
                total[place] = value if fresh else total[place] + value
                return carry

            lax.fori_loop(0, count, one, 0)

        return use

    mate_sem = sems(4)
    gather_own, gather_mate = [], []
    for h in parts:
        gather_own.append(
            Gather(screened.at[h], expand(screened.at[h], acc2.at[h], 0, NX - 1))
        )
        gather_mate.append(Gather(mate_scr.at[h], expand(mate_scr.at[h], acc.at[h], 1, 1)))
    for h in parts:
        gather_coef[h].own()
        gather_coef[h].beside()
    for h in parts:
        gather_coef[h].along_z()
        gather_coef[h].rest()
        screened[h, ga] = (0.5 * slab_sum[h] - coef[h, ga].astype(F32)).astype(BF16)
        send(screened.at[h, ga], mate_scr.at[h, ga], mate_sem + h, on_y(across))
        if h == 0:
            gather_own[h].start()
    for h in parts:
        reduce1[h].sent()
        reduce2[h].sent()
    gather_own[0].own()
    arrive(mate_scr.at[0, ga], mate_sem)
    gather_mate[0].start()

    def rho_sent(d, carry):
        for h in parts:
            rho_copy(h, d).wait_send()
        return carry

    lax.fori_loop(1, g_count, rho_sent, 0)
    back_sem = sems(2 * g_count)

    def back_copy(h, d):
        to = (ga + d) % g_count
        return copy(
            rho_tx.at[h, pl.ds(to * CAP, CAP)],
            back[h].at[pl.ds(ga * CAP, CAP)],
            back_sem + h * g_count + d,
            (pb, to),
        )

    for h in parts:
        if h:
            gather_own[h].own()
        gather_own[h].beside()
        gather_own[h].along_z()
        gather_mate[h].own()
        gather_mate[h].beside()
        gather_mate[h].along_z()
        if h == 0:
            gather_own[1].start()
            arrive(mate_scr.at[1, ga], mate_sem + 1)
            gather_mate[1].start()
        gather_mate[h].rest()
        mate_res[h] = (acc[h, :half] * ratio).astype(BF16).reshape(NX, rows, wide)
        send(mate_res.at[h], res[h].at[pl.ds(y * NX, NX)], mate_sem + 2 + h, on_y(across))
        gather_own[h].rest()

        def finish_rows(k, carry):
            value = (acc2[h, pl.ds(k * half, half)] * ratio).astype(BF16)
            res[h][pl.ds(row_of(k) * NX, NX)] = value.reshape(NX, rows, wide)
            return carry

        lax.fori_loop(0, NX - 1, finish_rows, 0)
        arrive(res[h].at[pl.ds(across * NX, NX)], mate_sem + 2 + h)

        def back_start(k, carry):
            d = (k + 2) % (g_count - 1) + 1
            to = (ga + d) % g_count
            for i in range(CAP):
                rho_tx[h, to * CAP + i] = res[h][held_of_slot[to * CAP + i]]
            back_copy(h, d).start()
            return carry

        lax.fori_loop(0, g_count - 1, back_start, 0)
        for i in range(CAP):
            back[h][ga * CAP + i] = res[h][held_of_slot[ga * CAP + i]]

    for h in parts:

        def back_wait(d, carry):
            source = (ga + g_count - d) % g_count
            arrive(back[h].at[pl.ds(source * CAP, CAP)], back_sem + h * g_count + d)
            return carry

        def unturn(j, carry):
            value = jnp.dot(turn_back[j], back[h][send_slot[j]], preferred_element_type=F32)
            out[j, :, h * wide : (h + 1) * wide] = value.astype(BF16)
            return carry

        lax.fori_loop(1, g_count, back_wait, 0)
        lax.fori_loop(0, q_count, unturn, 0)

    for one in started:
        one.wait_send()

    def drain_pb(d, carry):
        spread_copy(d).wait_send()
        mate_copy(d).wait_send()
        return carry

    def drain_ga(d, carry):
        column_copy(d).wait_send()
        for h in parts:
            back_copy(h, d).wait_send()
        return carry

    lax.fori_loop(1, q_count, drain_pb, 0)
    lax.fori_loop(1, g_count, drain_ga, 0)


def on_device(
    irr_vectors, inv_dielectric, pair_density, minus_q, sym_op, rot_blocks, rot_rows, phase_bits
):
    q_count = lax.axis_size("pb")
    g_count = lax.axis_size("ga")
    owner = lax.axis_index("pb")
    slab_index = lax.axis_index("ga")
    irr_count, block_rows, width = irr_vectors.shape
    density_width = pair_density.shape[2]
    blocks_all = q_count * g_count
    slab_rows = q_count * block_rows
    basis_rows = width // g_count
    slot_count = g_count * CAP
    ratio = math.sqrt(slab_rows * g_count / width)

    operation = lax.dynamic_index_in_dim(sym_op, owner, 0, keepdims=False)
    table = lax.dynamic_index_in_dim(rot_blocks, operation, 0, keepdims=False)
    places = jnp.arange(blocks_all, dtype=jnp.int32)
    source_ga = table % g_count
    earlier = (places[None, :] < places[:, None]) & (
        places[None, :] // q_count == places[:, None] // q_count
    )
    ranks = jnp.sum(
        (earlier & (source_ga[None, :] == source_ga[:, None])).astype(jnp.int32), axis=1
    )
    mine_source = lax.dynamic_slice_in_dim(table, slab_index * q_count, q_count)
    mine_rank = lax.dynamic_slice_in_dim(ranks, slab_index * q_count, q_count)
    send_slot = mine_source % g_count * CAP + mine_rank
    slots = jnp.arange(slot_count, dtype=jnp.int32)
    local = jnp.arange(q_count, dtype=jnp.int32)
    block_of_slot = jnp.sum(
        jnp.where(slots[:, None] == send_slot[None, :], local[None, :], 0), axis=1
    )
    senders = local * g_count + slab_index
    match = table[None, :] == senders[:, None]
    dest_block = jnp.sum(jnp.where(match, places[None, :], 0), axis=1)
    dest_rank = jnp.sum(jnp.where(match, ranks[None, :], 0), axis=1)
    held_slot = dest_block // q_count * CAP + dest_rank
    held_of_slot = jnp.sum(
        jnp.where(slots[:, None] == held_slot[None, :], local[None, :], 0), axis=1
    )

    row_table = lax.dynamic_slice_in_dim(
        lax.dynamic_index_in_dim(rot_rows, operation, 0, keepdims=False),
        slab_index * q_count,
        q_count,
    )
    bits = lax.dynamic_slice_in_dim(
        lax.dynamic_index_in_dim(phase_bits, operation, 0, keepdims=False),
        slab_index * slab_rows,
        slab_rows,
    ).reshape(q_count, block_rows)

    vmem = pltpu.VMEM
    dma = pltpu.SemaphoreType.DMA
    wide = density_width // 2
    slab = (wide, basis_rows)
    square = (basis_rows, wide)
    slots = (slot_count, block_rows, wide)
    chunk = width // q_count
    any_spec = pl.BlockSpec(memory_space=pl.ANY)
    smem_spec = pl.BlockSpec(memory_space=pltpu.SMEM)
    vmem_spec = pl.BlockSpec(memory_space=pltpu.VMEM)

    def run(*operands):
        return pl.pallas_call(
            lambda *refs: kernel(ratio, *refs),
            out_shape=jax.ShapeDtypeStruct((q_count, block_rows, density_width), BF16),
            in_specs=[any_spec] * 4 + [vmem_spec] * 2 + [smem_spec] * 5,
            out_specs=vmem_spec,
            scratch_shapes=[
                vmem((NX, NX, block_rows, width), BF16),
                vmem((NX, block_rows, width), BF16),
                vmem((2, block_rows, width), BF16),
                vmem((2, *slots), BF16),
                vmem(slots, BF16),
                vmem(slots, BF16),
                vmem((wide, NX * block_rows), BF16),
                vmem((2, wide, NX * block_rows), BF16),
                vmem((2, wide, NX * block_rows), BF16),
                vmem((2, g_count, *slab), F32),
                vmem((2, g_count, *slab), F32),
                vmem((2, g_count // NC, *slab), F32),
                vmem((2, g_count // NC, *slab), F32),
                vmem((2, g_count // NC, *slab), BF16),
                vmem((2, g_count // NC, *slab), BF16),
                vmem((2, g_count // NC, *slab), BF16),
                vmem((2, g_count // NC, *slab), BF16),
                vmem((2, 2, *slab), BF16),
                vmem((2, g_count, *square), BF16),
                vmem((2, *square), F32),
                vmem((basis_rows, width), BF16),
                vmem((q_count, chunk, basis_rows), BF16),
                vmem((q_count, chunk, basis_rows), BF16),
                vmem((g_count, 2, chunk, basis_rows), BF16),
                vmem((q_count, chunk, basis_rows), BF16),
                vmem((basis_rows, width), BF16),
                vmem((2, g_count, *square), BF16),
                vmem((2, g_count, *square), BF16),
                vmem((q_count, block_rows, wide), BF16),
                vmem((q_count, block_rows, wide), BF16),
                vmem((2, NX, block_rows, wide), BF16),
                vmem(slots, BF16),
                vmem(slots, BF16),
                vmem((q_count, block_rows, block_rows), BF16),
                dma((5,)),
                dma((SEMS,)),
                dma((SEMS,)),
            ],
            compiler_params=pltpu.CompilerParams(
                collective_id=0, has_side_effects=True, vmem_limit_bytes=62 * 1024 * 1024
            ),
        )(*operands)

    out = run(
        irr_vectors,
        inv_dielectric[0].reshape(2, chunk, width),
        inv_dielectric[0],
        pair_density[0].reshape(q_count, block_rows, density_width),
        row_table,
        bits,
        minus_q,
        block_of_slot,
        held_slot,
        held_of_slot,
        send_slot,
    )
    return out.reshape(1, slab_rows, density_width)


def solution(mesh):
    in_specs = (
        P(None, ("pb", "ga"), None),
        P("pb", "ga", None),
        P("pb", "ga", None),
        P(),
        P(),
        P(),
        P(),
        P(),
    )
    out_specs = P("pb", "ga", None)
    return jax.shard_map(
        on_device, mesh=mesh, in_specs=in_specs, out_specs=out_specs, check_vma=False
    )
```

```python
import math

import jax
import jax.numpy as jnp
from jax import lax
from jax.experimental import pallas as pl
from jax.experimental.pallas import tpu as pltpu
from jax.sharding import PartitionSpec as P

MESH = pl.DeviceIdType.MESH
NX = 4
NC = 2
SEMS = 200
CAP = 3
BF16 = jnp.bfloat16
F32 = jnp.float32


def kernel(
    ratio,
    irr,
    dmat,
    drows,
    density,
    row_table,
    bits,
    minus_q,
    block_of_slot,
    held_slot,
    held_of_slot,
    send_slot,
    out,
    held,
    fwd,
    via_x,
    rho_tx,
    rho_rx_low,
    rho_rx_high,
    rho_group,
    part_tx,
    part_rx,
    acc,
    acc2,
    core_rx,
    core_rx2,
    sum_tx,
    sum_tx2,
    sum_rx,
    sum_rx2,
    mate_sum,
    coef,
    slab_sum,
    own_d,
    spread,
    chosen,
    dcols,
    mate_cols,
    mate_t,
    screened,
    mate_scr,
    res_low,
    res_high,
    mate_res,
    back_low,
    back_high,
    turn_back,
    local_sem,
    send_sem,
    recv_sem,
):
    q_count = lax.axis_size("pb")
    g_count = lax.axis_size("ga")
    pb = lax.axis_index("pb")
    ga = lax.axis_index("ga")
    y, x = pb // NX, pb % NX
    z, c = ga // NC, ga % NC
    z_count = g_count // NC
    sibling = z * NC + (1 - c)
    basis = own_d.shape[0]
    rows = row_table.shape[1]
    plus, minus, beyond = (lambda v: (v + 1) % NX), (lambda v: (v + 3) % NX), (lambda v: (v + 2) % NX)
    ahead, behind = (lambda v: (v + 1 + 2 * c) % NX), (lambda v: (v + 3 - 2 * c) % NX)
    up, down, across = plus(y), minus(y), beyond(y)
    parts = range(2)
    res = (res_low, res_high)
    rho_rx = (rho_rx_low, rho_rx_high)
    back = (back_low, back_high)
    wide = res_low.shape[2]
    started = []
    taken = [0]

    def sems(count):
        first = taken[0]
        taken[0] += count
        assert taken[0] <= SEMS
        return first

    def copy(src, dst, i, to):
        return pltpu.make_async_remote_copy(
            src_ref=src,
            dst_ref=dst,
            send_sem=send_sem.at[i],
            recv_sem=recv_sem.at[i],
            device_id=to,
            device_id_type=MESH,
        )

    def send(src, dst, i, to):
        one = copy(src, dst, i, to)
        one.start()
        started.append(one)

    def arrive(dst, i):
        copy(dst, dst, i, (pb, ga)).wait_recv()

    def on_x(t):
        return (y * NX + t, ga)

    def on_y(t):
        return (t * NX + x, ga)

    class Exchange:
        def __init__(self, me, to, src, dst, via):
            self.me, self.to, self.src, self.dst, self.via = me, to, src, dst, via
            self.i = sems(4)

        def start(self):
            me = self.me
            send(self.src(plus(me)), self.dst(me), self.i, self.to(plus(me)))
            send(self.src(minus(me)), self.dst(me), self.i + 1, self.to(minus(me)))
            send(self.src(beyond(me)), self.via, self.i + 2, self.to(ahead(me)))

        def forward(self):
            arrive(self.via, self.i + 2)
            send(self.via, self.dst(behind(self.me)), self.i + 3, self.to(ahead(self.me)))

        def from_minus(self):
            arrive(self.dst(minus(self.me)), self.i)

        def from_plus(self):
            arrive(self.dst(plus(self.me)), self.i + 1)

        def from_beyond(self):
            arrive(self.dst(beyond(self.me)), self.i + 3)

        def finish(self):
            self.from_minus()
            self.from_plus()
            self.from_beyond()

    load_rho = pltpu.make_async_copy(density, out, local_sem.at[0])
    load_rho.start()

    barrier = pltpu.get_barrier_semaphore()

    def greet_pb(d, carry):
        pl.semaphore_signal(
            barrier, inc=1, device_id=((pb + d) % q_count, ga), device_id_type=MESH
        )
        return carry

    def greet_ga(d, carry):
        pl.semaphore_signal(
            barrier, inc=1, device_id=(pb, (ga + d) % g_count), device_id_type=MESH
        )
        return carry

    lax.fori_loop(1, q_count, greet_pb, 0)
    lax.fori_loop(1, g_count, greet_ga, 0)
    pl.semaphore_wait(barrier, q_count + g_count - 2)

    own_irr = NX * (y % 2)
    next_irr = NX * ((y + 1) % 2)
    next_x = Exchange(x, on_x, lambda t: irr.at[next_irr + t], lambda s: fwd.at[s], via_x.at[0])
    own_x = Exchange(x, on_x, lambda t: irr.at[own_irr + t], lambda s: held.at[y, s], via_x.at[1])
    next_x.start()
    keep = pltpu.make_async_copy(irr.at[own_irr + x], held.at[y, x], local_sem.at[1])
    keep.start()
    y_sem = sems(8)

    def to_neighbours(k, source, src):
        there = held.at[y, source]
        send(src, there, y_sem + k, on_y(up))
        send(src, there, y_sem + 4 + k, on_y(down))

    to_neighbours(0, x, irr.at[next_irr + x])

    def turn_of(j):
        sources = lax.broadcasted_iota(jnp.int32, (rows, rows), 0)
        sign = (1 - 2 * bits[pl.ds(j, 1), :]).astype(F32)
        return jnp.where(row_table[pl.ds(j, 1), :] == sources, sign, 0.0)

    load_rho.wait()
    rho_sem = sems(2 * g_count)

    def rho_copy(h, d):
        to = (ga + d) % g_count
        return copy(
            rho_tx.at[h, pl.ds(to * CAP, CAP)],
            rho_rx[h].at[pl.ds(ga * CAP, CAP)],
            rho_sem + h * g_count + d,
            (pb, to),
        )

    for h in parts:

        def make_turned(j, carry):
            value = jnp.dot(
                turn_of(j).astype(BF16),
                out[j, :, h * wide : (h + 1) * wide],
                preferred_element_type=F32,
            )
            res[h][j] = value.astype(BF16)
            return carry

        def rho_start(k, carry):
            d = (k + 2) % (g_count - 1) + 1
            to = (ga + d) % g_count
            for i in range(CAP):
                rho_tx[h, to * CAP + i] = res[h][block_of_slot[to * CAP + i]]
            rho_copy(h, d).start()
            return carry

        lax.fori_loop(0, q_count, make_turned, 0)
        lax.fori_loop(0, g_count - 1, rho_start, 0)
        for i in range(CAP):
            rho_rx[h][ga * CAP + i] = res[h][block_of_slot[ga * CAP + i]]

    load_d = pltpu.make_async_copy(drows, own_d, local_sem.at[3])
    load_d.start()

    next_x.from_minus()
    to_neighbours(1, minus(x), fwd.at[minus(x)])
    next_x.from_plus()
    to_neighbours(2, plus(x), fwd.at[plus(x)])
    next_x.forward()
    own_x.start()

    def make_turn_back(j, carry):
        turn_back[j] = turn_of(j).T.astype(BF16)
        return carry

    lax.fori_loop(0, q_count, make_turn_back, 0)
    next_x.from_beyond()
    to_neighbours(3, beyond(x), fwd.at[beyond(x)])
    own_x.forward()

    def row_blocks(row):
        return [(row, i) for i in range(NX)]

    def group(h, blocks):
        found = [rho_rx[h][held_slot[row * NX + i]] for row, i in blocks]
        return jnp.concatenate(found, axis=0).T

    def project(blocks, values, total, first):
        def one(n, carry):
            columns = pl.ds(pl.multiple_of(n * basis, basis), basis)
            block = jnp.concatenate([held[row, i, :, columns] for row, i in blocks], axis=0)
            part = jnp.dot(values[...], block, preferred_element_type=F32)
            total[n] = part if first else total[n] + part
            return carry

        lax.fori_loop(0, g_count, one, 0)

    part_sem = sems(4)
    column_sem = sems(g_count)

    def column_copy(d):
        to = (ga + d) % g_count
        columns = pl.ds(pl.multiple_of(to * basis, basis), basis)
        return copy(dmat.at[:, :, columns], dcols.at[ga], column_sem + d, (pb, to))

    def column_start(d, carry):
        column_copy(d).start()
        return carry

    own_columns = pl.ds(pl.multiple_of(ga * basis, basis), basis)
    keep_cols = pltpu.make_async_copy(
        dmat.at[:, :, own_columns], dcols.at[ga], local_sem.at[4]
    )

    for h in parts:
        if h:
            lax.fori_loop(1, g_count, column_start, 0)
            keep_cols.start()

        def rho_wait(d, carry):
            source = (ga + g_count - d) % g_count
            arrive(rho_rx[h].at[pl.ds(source * CAP, CAP)], rho_sem + h * g_count + d)
            return carry

        lax.fori_loop(1, g_count, rho_wait, 0)
        part_tx[h] = group(h, row_blocks(across))
        send(part_tx.at[h], part_rx.at[h], part_sem + h, on_y(across))

    class Reduce:
        def __init__(self, total, landing, outgoing, incoming):
            self.total, self.landing = total, landing
            self.outgoing, self.incoming = outgoing, incoming
            self.i = sems(2 * z_count)

        def to_core(self, k):
            return copy(
                self.total.at[k * NC + (1 - c)], self.landing.at[k], self.i + k, (pb, sibling)
            )

        def start(self):
            for k in range(z_count):
                self.to_core(k).start()

        def sent(self):
            for k in range(z_count):
                self.to_core(k).wait_send()

        def along_z(self):
            for d in (2, 1, 3):
                k = (z + d) % z_count
                arrive(self.landing.at[k], self.i + k)
                self.outgoing[d] = (self.total[k * NC + c] + self.landing[k]).astype(BF16)
                send(
                    self.outgoing.at[d],
                    self.incoming.at[d],
                    self.i + z_count + d,
                    (pb, k * NC + c),
                )
            arrive(self.landing.at[z], self.i + z)

        def finish(self):
            value = self.total[ga] + self.landing[z]
            for d in (1, 3, 2):
                arrive(self.incoming.at[d], self.i + z_count + d)
                value = value + self.incoming[d].astype(F32)
            return value

    reduce1 = [Reduce(acc.at[h], core_rx.at[h], sum_tx.at[h], sum_rx.at[h]) for h in parts]
    reduce2 = [Reduce(acc2.at[h], core_rx2.at[h], sum_tx2.at[h], sum_rx2.at[h]) for h in parts]

    own_x.finish()
    keep.wait()
    for h in parts:
        arrive(part_rx.at[h], part_sem + h)
        project(row_blocks(y), part_rx.at[h], acc2.at[h], True)
        reduce2[h].start()
    for h in parts:
        rho_group[...] = group(h, row_blocks(y))
        project(row_blocks(y), rho_group, acc.at[h], True)
        reduce2[h].along_z()
    order = (x, minus(x), plus(x), beyond(x))
    batches = [[(row, s) for s in order[k : k + 2] for row in (down, up)] for k in (0, 2)]

    def batch_in(first):
        for k in (first, first + 1):
            arrive(held.at[down, order[k]], y_sem + k)
            arrive(held.at[up, order[k]], y_sem + 4 + k)

    batch_in(0)
    for h in parts:
        rho_group[...] = group(h, batches[0])
        project(batches[0], rho_group, acc.at[h], False)
    batch_in(2)
    def column_wait(d, carry):
        arrive(dcols.at[(ga + g_count - d) % g_count], column_sem + d)
        return carry

    lax.fori_loop(1, g_count, column_wait, 0)
    keep_cols.wait()
    d1_sem, d2_sem = sems(q_count), sems(q_count)

    def spread_copy(d):
        to = (pb + d) % q_count
        return copy(dcols.at[to // 2, to % 2], spread.at[pb], d1_sem + d, (to, ga))

    def spread_start(d, carry):
        spread_copy(d).start()
        return carry

    lax.fori_loop(1, q_count, spread_start, 0)
    keep_d1 = pltpu.make_async_copy(dcols.at[pb // 2, pb % 2], spread.at[pb], local_sem.at[2])
    keep_d1.start()

    for h in parts:
        rho_group[...] = group(h, batches[1])
        project(batches[1], rho_group, acc.at[h], False)
        reduce1[h].start()
    def spread_wait(d, carry):
        arrive(spread.at[(pb + q_count - d) % q_count], d1_sem + d)
        return carry

    lax.fori_loop(1, q_count, spread_wait, 0)
    keep_d1.wait()

    def choose(q, carry):
        chosen[q] = spread[minus_q[q]]
        return carry

    lax.fori_loop(0, q_count, choose, 0)

    def mate_copy(d):
        to = (pb + d) % q_count
        return copy(chosen.at[to], mate_cols.at[pb], d2_sem + d, (to, ga))

    def mate_start(d, carry):
        mate_copy(d).start()
        return carry

    lax.fori_loop(1, q_count, mate_start, 0)
    keep_d2 = pltpu.make_async_copy(chosen.at[pb], mate_cols.at[pb], local_sem.at[2])
    keep_d2.start()

    for h in parts:
        mate_sum[h, 0] = reduce2[h].finish().astype(BF16)
        send(mate_sum.at[h, 0], mate_sum.at[h, 1], part_sem + 2 + h, on_y(across))
        reduce1[h].along_z()

    class Gather:
        def __init__(self, ref, use):
            self.ref, self.use = ref, use
            self.i = sems(8)

        def start(self):
            mine = self.ref.at[ga]
            for d in (2, 1, 3):
                send(mine, mine, self.i + d, (pb, (z + d) % z_count * NC + c))
            send(mine, mine, self.i, (pb, sibling))

        def own(self):
            self.use(ga)

        def beside(self):
            arrive(self.ref.at[sibling], self.i)
            self.use(sibling)

        def along_z(self):
            for d in (1, 3, 2):
                source = (z + z_count - d) % z_count * NC + c
                there = self.ref.at[source]
                arrive(there, self.i + d)
                send(there, there, self.i + 4 + d, (pb, sibling))
                self.use(source)

        def rest(self):
            for d in (1, 3, 2):
                source = (z + z_count - d) % z_count * NC + (1 - c)
                arrive(self.ref.at[source], self.i + 4 + d)
                self.use(source)

    def apply(h):
        def use(n):
            columns = pl.ds(pl.multiple_of(n * basis, basis), basis)
            slab_sum[h] += jnp.dot(
                own_d[:, columns], coef[h, n], preferred_element_type=F32
            ) + jnp.dot(mate_t[:, columns], coef[h, n], preferred_element_type=F32)

        return use

    gather_coef = [Gather(coef.at[h], apply(h)) for h in parts]
    for h in parts:
        value = reduce1[h].finish()
        arrive(mate_sum.at[h, 1], part_sem + 2 + h)
        coef[h, ga] = (value + mate_sum[h, 1].astype(F32)).astype(BF16).T
        gather_coef[h].start()

    def mate_wait(d, carry):
        arrive(mate_cols.at[(pb + q_count - d) % q_count], d2_sem + d)
        return carry

    lax.fori_loop(1, q_count, mate_wait, 0)
    keep_d2.wait()
    load_d.wait()
    chunk = mate_cols.shape[1]

    def turn_columns(k, carry):
        mate_t[:, pl.ds(pl.multiple_of(k * chunk, chunk), chunk)] = mate_cols[k].T
        return carry

    lax.fori_loop(0, q_count, turn_columns, 0)
    slab_sum[...] = jnp.zeros_like(slab_sum)

    half = NX // 2

    def row_of(k):
        return (y + NX - 1 + k) % NX

    def expand(values, total, first_row, count):
        first = [True]

        def use(n):
            columns = pl.ds(pl.multiple_of(n * basis, basis), basis)
            fresh = first.pop() if first else False

            def one(k, carry):
                block = held[row_of(first_row + k), :, :, columns].reshape(-1, basis)
                value = jnp.dot(block, values[n], preferred_element_type=F32)
                value = value.reshape(half, -1, wide)
                place = pl.ds(k * half, half)
                total[place] = value if fresh else total[place] + value
                return carry

            lax.fori_loop(0, count, one, 0)

        return use

    mate_sem = sems(4)
    gather_own, gather_mate = [], []
    for h in parts:
        gather_own.append(
            Gather(screened.at[h], expand(screened.at[h], acc2.at[h], 0, NX - 1))
        )
        gather_mate.append(Gather(mate_scr.at[h], expand(mate_scr.at[h], acc.at[h], 1, 1)))
    for h in parts:
        gather_coef[h].own()
        gather_coef[h].beside()
    for h in parts:
        gather_coef[h].along_z()
        gather_coef[h].rest()
        screened[h, ga] = (0.5 * slab_sum[h] - coef[h, ga].astype(F32)).astype(BF16)
        send(screened.at[h, ga], mate_scr.at[h, ga], mate_sem + h, on_y(across))
        if h == 0:
            gather_own[h].start()
    for h in parts:
        reduce1[h].sent()
        reduce2[h].sent()
    gather_own[0].own()
    arrive(mate_scr.at[0, ga], mate_sem)
    gather_mate[0].start()

    def rho_sent(d, carry):
        for h in parts:
            rho_copy(h, d).wait_send()
        return carry

    lax.fori_loop(1, g_count, rho_sent, 0)
    back_sem = sems(2 * g_count)

    def back_copy(h, d):
        to = (ga + d) % g_count
        return copy(
            rho_tx.at[h, pl.ds(to * CAP, CAP)],
            back[h].at[pl.ds(ga * CAP, CAP)],
            back_sem + h * g_count + d,
            (pb, to),
        )

    for h in parts:
        if h:
            gather_own[h].own()
        gather_own[h].beside()
        gather_own[h].along_z()
        gather_mate[h].own()
        gather_mate[h].beside()
        gather_mate[h].along_z()
        if h == 0:
            gather_own[1].start()
            arrive(mate_scr.at[1, ga], mate_sem + 1)
            gather_mate[1].start()
        gather_mate[h].rest()
        mate_res[h] = (acc[h, :half] * ratio).astype(BF16).reshape(NX, rows, wide)
        send(mate_res.at[h], res[h].at[pl.ds(y * NX, NX)], mate_sem + 2 + h, on_y(across))
        gather_own[h].rest()

        def finish_rows(k, carry):
            value = (acc2[h, pl.ds(k * half, half)] * ratio).astype(BF16)
            res[h][pl.ds(row_of(k) * NX, NX)] = value.reshape(NX, rows, wide)
            return carry

        lax.fori_loop(0, NX - 1, finish_rows, 0)
        arrive(res[h].at[pl.ds(across * NX, NX)], mate_sem + 2 + h)

        def back_start(k, carry):
            d = (k + 2) % (g_count - 1) + 1
            to = (ga + d) % g_count
            for i in range(CAP):
                rho_tx[h, to * CAP + i] = res[h][held_of_slot[to * CAP + i]]
            back_copy(h, d).start()
            return carry

        lax.fori_loop(0, g_count - 1, back_start, 0)
        for i in range(CAP):
            back[h][ga * CAP + i] = res[h][held_of_slot[ga * CAP + i]]

    for h in parts:

        def back_wait(d, carry):
            source = (ga + g_count - d) % g_count
            arrive(back[h].at[pl.ds(source * CAP, CAP)], back_sem + h * g_count + d)
            return carry

        def unturn(j, carry):
            value = jnp.dot(turn_back[j], back[h][send_slot[j]], preferred_element_type=F32)
            out[j, :, h * wide : (h + 1) * wide] = value.astype(BF16)
            return carry

        lax.fori_loop(1, g_count, back_wait, 0)
        lax.fori_loop(0, q_count, unturn, 0)

    for one in started:
        one.wait_send()

    def drain_pb(d, carry):
        spread_copy(d).wait_send()
        mate_copy(d).wait_send()
        return carry

    def drain_ga(d, carry):
        column_copy(d).wait_send()
        for h in parts:
            back_copy(h, d).wait_send()
        return carry

    lax.fori_loop(1, q_count, drain_pb, 0)
    lax.fori_loop(1, g_count, drain_ga, 0)


def on_device(
    irr_vectors, inv_dielectric, pair_density, minus_q, sym_op, rot_blocks, rot_rows, phase_bits
):
    q_count = lax.axis_size("pb")
    g_count = lax.axis_size("ga")
    owner = lax.axis_index("pb")
    slab_index = lax.axis_index("ga")
    irr_count, block_rows, width = irr_vectors.shape
    density_width = pair_density.shape[2]
    blocks_all = q_count * g_count
    slab_rows = q_count * block_rows
    basis_rows = width // g_count
    slot_count = g_count * CAP
    ratio = math.sqrt(slab_rows * g_count / width)

    operation = lax.dynamic_index_in_dim(sym_op, owner, 0, keepdims=False)
    table = lax.dynamic_index_in_dim(rot_blocks, operation, 0, keepdims=False)
    places = jnp.arange(blocks_all, dtype=jnp.int32)
    source_ga = table % g_count
    earlier = (places[None, :] < places[:, None]) & (
        places[None, :] // q_count == places[:, None] // q_count
    )
    ranks = jnp.sum(
        (earlier & (source_ga[None, :] == source_ga[:, None])).astype(jnp.int32), axis=1
    )
    mine_source = lax.dynamic_slice_in_dim(table, slab_index * q_count, q_count)
    mine_rank = lax.dynamic_slice_in_dim(ranks, slab_index * q_count, q_count)
    send_slot = mine_source % g_count * CAP + mine_rank
    slots = jnp.arange(slot_count, dtype=jnp.int32)
    local = jnp.arange(q_count, dtype=jnp.int32)
    block_of_slot = jnp.sum(
        jnp.where(slots[:, None] == send_slot[None, :], local[None, :], 0), axis=1
    )
    senders = local * g_count + slab_index
    match = table[None, :] == senders[:, None]
    dest_block = jnp.sum(jnp.where(match, places[None, :], 0), axis=1)
    dest_rank = jnp.sum(jnp.where(match, ranks[None, :], 0), axis=1)
    held_slot = dest_block // q_count * CAP + dest_rank
    held_of_slot = jnp.sum(
        jnp.where(slots[:, None] == held_slot[None, :], local[None, :], 0), axis=1
    )

    row_table = lax.dynamic_slice_in_dim(
        lax.dynamic_index_in_dim(rot_rows, operation, 0, keepdims=False),
        slab_index * q_count,
        q_count,
    )
    bits = lax.dynamic_slice_in_dim(
        lax.dynamic_index_in_dim(phase_bits, operation, 0, keepdims=False),
        slab_index * slab_rows,
        slab_rows,
    ).reshape(q_count, block_rows)

    vmem = pltpu.VMEM
    dma = pltpu.SemaphoreType.DMA
    wide = density_width // 2
    slab = (wide, basis_rows)
    square = (basis_rows, wide)
    slots = (slot_count, block_rows, wide)
    chunk = width // q_count
    any_spec = pl.BlockSpec(memory_space=pl.ANY)
    smem_spec = pl.BlockSpec(memory_space=pltpu.SMEM)
    vmem_spec = pl.BlockSpec(memory_space=pltpu.VMEM)

    def run(*operands):
        return pl.pallas_call(
            lambda *refs: kernel(ratio, *refs),
            out_shape=jax.ShapeDtypeStruct((q_count, block_rows, density_width), BF16),
            in_specs=[any_spec] * 4 + [vmem_spec] * 2 + [smem_spec] * 5,
            out_specs=vmem_spec,
            scratch_shapes=[
                vmem((NX, NX, block_rows, width), BF16),
                vmem((NX, block_rows, width), BF16),
                vmem((2, block_rows, width), BF16),
                vmem((2, *slots), BF16),
                vmem(slots, BF16),
                vmem(slots, BF16),
                vmem((wide, NX * block_rows), BF16),
                vmem((2, wide, NX * block_rows), BF16),
                vmem((2, wide, NX * block_rows), BF16),
                vmem((2, g_count, *slab), F32),
                vmem((2, g_count, *slab), F32),
                vmem((2, g_count // NC, *slab), F32),
                vmem((2, g_count // NC, *slab), F32),
                vmem((2, g_count // NC, *slab), BF16),
                vmem((2, g_count // NC, *slab), BF16),
                vmem((2, g_count // NC, *slab), BF16),
                vmem((2, g_count // NC, *slab), BF16),
                vmem((2, 2, *slab), BF16),
                vmem((2, g_count, *square), BF16),
                vmem((2, *square), F32),
                vmem((basis_rows, width), BF16),
                vmem((q_count, chunk, basis_rows), BF16),
                vmem((q_count, chunk, basis_rows), BF16),
                vmem((g_count, 2, chunk, basis_rows), BF16),
                vmem((q_count, chunk, basis_rows), BF16),
                vmem((basis_rows, width), BF16),
                vmem((2, g_count, *square), BF16),
                vmem((2, g_count, *square), BF16),
                vmem((q_count, block_rows, wide), BF16),
                vmem((q_count, block_rows, wide), BF16),
                vmem((2, NX, block_rows, wide), BF16),
                vmem(slots, BF16),
                vmem(slots, BF16),
                vmem((q_count, block_rows, block_rows), BF16),
                dma((5,)),
                dma((SEMS,)),
                dma((SEMS,)),
            ],
            compiler_params=pltpu.CompilerParams(
                collective_id=0, has_side_effects=True, vmem_limit_bytes=62 * 1024 * 1024
            ),
        )(*operands)

    out = run(
        irr_vectors,
        inv_dielectric[0].reshape(2, chunk, width),
        inv_dielectric[0],
        pair_density[0].reshape(q_count, block_rows, density_width),
        row_table,
        bits,
        minus_q,
        block_of_slot,
        held_slot,
        held_of_slot,
        send_slot,
    )
    return out.reshape(1, slab_rows, density_width)


def solution(mesh):
    in_specs = (
        P(None, ("pb", "ga"), None),
        P("pb", "ga", None),
        P("pb", "ga", None),
        P(),
        P(),
        P(),
        P(),
        P(),
    )
    out_specs = P("pb", "ga", None)
    return jax.shard_map(
        on_device, mesh=mesh, in_specs=in_specs, out_specs=out_specs, check_vma=False
    )
```

```python
import math

import jax
import jax.numpy as jnp
from jax import lax
from jax.experimental import pallas as pl
from jax.experimental.pallas import tpu as pltpu
from jax.sharding import PartitionSpec as P

MESH = pl.DeviceIdType.MESH
NX = 4
NC = 2
SEMS = 200
CAP = 3
BF16 = jnp.bfloat16
F32 = jnp.float32


def kernel(
    ratio,
    irr,
    dmat,
    drows,
    density,
    row_table,
    bits,
    minus_q,
    block_of_slot,
    held_slot,
    held_of_slot,
    send_slot,
    out,
    held,
    fwd,
    via_x,
    rho_tx,
    rho_rx_low,
    rho_rx_high,
    rho_group,
    part_tx,
    part_rx,
    acc,
    acc2,
    core_rx,
    core_rx2,
    sum_tx,
    sum_tx2,
    sum_rx,
    sum_rx2,
    mate_sum,
    coef,
    slab_sum,
    own_d,
    spread,
    chosen,
    dcols,
    mate_cols,
    mate_t,
    screened,
    mate_scr,
    res_low,
    res_high,
    mate_res,
    back_low,
    back_high,
    turn_back,
    local_sem,
    send_sem,
    recv_sem,
):
    q_count = lax.axis_size("pb")
    g_count = lax.axis_size("ga")
    pb = lax.axis_index("pb")
    ga = lax.axis_index("ga")
    y, x = pb // NX, pb % NX
    z, c = ga // NC, ga % NC
    z_count = g_count // NC
    sibling = z * NC + (1 - c)
    basis = own_d.shape[0]
    rows = row_table.shape[1]
    plus, minus, beyond = (lambda v: (v + 1) % NX), (lambda v: (v + 3) % NX), (lambda v: (v + 2) % NX)
    ahead, behind = (lambda v: (v + 1 + 2 * c) % NX), (lambda v: (v + 3 - 2 * c) % NX)
    up, down, across = plus(y), minus(y), beyond(y)
    parts = range(2)
    res = (res_low, res_high)
    rho_rx = (rho_rx_low, rho_rx_high)
    back = (back_low, back_high)
    wide = res_low.shape[2]
    started = []
    taken = [0]

    def sems(count):
        first = taken[0]
        taken[0] += count
        assert taken[0] <= SEMS
        return first

    def copy(src, dst, i, to):
        return pltpu.make_async_remote_copy(
            src_ref=src,
            dst_ref=dst,
            send_sem=send_sem.at[i],
            recv_sem=recv_sem.at[i],
            device_id=to,
            device_id_type=MESH,
        )

    def send(src, dst, i, to):
        one = copy(src, dst, i, to)
        one.start()
        started.append(one)

    def arrive(dst, i):
        copy(dst, dst, i, (pb, ga)).wait_recv()

    def on_x(t):
        return (y * NX + t, ga)

    def on_y(t):
        return (t * NX + x, ga)

    class Exchange:
        def __init__(self, me, to, src, dst, via):
            self.me, self.to, self.src, self.dst, self.via = me, to, src, dst, via
            self.i = sems(4)

        def start(self):
            me = self.me
            send(self.src(plus(me)), self.dst(me), self.i, self.to(plus(me)))
            send(self.src(minus(me)), self.dst(me), self.i + 1, self.to(minus(me)))
            send(self.src(beyond(me)), self.via, self.i + 2, self.to(ahead(me)))

        def forward(self):
            arrive(self.via, self.i + 2)
            send(self.via, self.dst(behind(self.me)), self.i + 3, self.to(ahead(self.me)))

        def from_minus(self):
            arrive(self.dst(minus(self.me)), self.i)

        def from_plus(self):
            arrive(self.dst(plus(self.me)), self.i + 1)

        def from_beyond(self):
            arrive(self.dst(beyond(self.me)), self.i + 3)

        def finish(self):
            self.from_minus()
            self.from_plus()
            self.from_beyond()

    load_rho = pltpu.make_async_copy(density, out, local_sem.at[0])
    load_rho.start()

    barrier = pltpu.get_barrier_semaphore()

    def greet_pb(d, carry):
        pl.semaphore_signal(
            barrier, inc=1, device_id=((pb + d) % q_count, ga), device_id_type=MESH
        )
        return carry

    def greet_ga(d, carry):
        pl.semaphore_signal(
            barrier, inc=1, device_id=(pb, (ga + d) % g_count), device_id_type=MESH
        )
        return carry

    lax.fori_loop(1, q_count, greet_pb, 0)
    lax.fori_loop(1, g_count, greet_ga, 0)
    pl.semaphore_wait(barrier, q_count + g_count - 2)

    own_irr = NX * (y % 2)
    next_irr = NX * ((y + 1) % 2)
    next_x = Exchange(x, on_x, lambda t: irr.at[next_irr + t], lambda s: fwd.at[s], via_x.at[0])
    own_x = Exchange(x, on_x, lambda t: irr.at[own_irr + t], lambda s: held.at[y, s], via_x.at[1])
    next_x.start()
    keep = pltpu.make_async_copy(irr.at[own_irr + x], held.at[y, x], local_sem.at[1])
    keep.start()
    y_sem = sems(8)

    def to_neighbours(k, source, src):
        there = held.at[y, source]
        send(src, there, y_sem + k, on_y(up))
        send(src, there, y_sem + 4 + k, on_y(down))

    to_neighbours(0, x, irr.at[next_irr + x])

    def turn_of(j):
        sources = lax.broadcasted_iota(jnp.int32, (rows, rows), 0)
        sign = (1 - 2 * bits[pl.ds(j, 1), :]).astype(F32)
        return jnp.where(row_table[pl.ds(j, 1), :] == sources, sign, 0.0)

    load_rho.wait()
    rho_sem = sems(2 * g_count)

    def rho_copy(h, d):
        to = (ga + d) % g_count
        return copy(
            rho_tx.at[h, pl.ds(to * CAP, CAP)],
            rho_rx[h].at[pl.ds(ga * CAP, CAP)],
            rho_sem + h * g_count + d,
            (pb, to),
        )

    for h in parts:

        def make_turned(j, carry):
            value = jnp.dot(
                turn_of(j).astype(BF16),
                out[j, :, h * wide : (h + 1) * wide],
                preferred_element_type=F32,
            )
            res[h][j] = value.astype(BF16)
            return carry

        def rho_start(k, carry):
            d = (k + 2) % (g_count - 1) + 1
            to = (ga + d) % g_count
            for i in range(CAP):
                rho_tx[h, to * CAP + i] = res[h][block_of_slot[to * CAP + i]]
            rho_copy(h, d).start()
            return carry

        lax.fori_loop(0, q_count, make_turned, 0)
        lax.fori_loop(0, g_count - 1, rho_start, 0)
        for i in range(CAP):
            rho_rx[h][ga * CAP + i] = res[h][block_of_slot[ga * CAP + i]]

    load_d = pltpu.make_async_copy(drows, own_d, local_sem.at[3])
    load_d.start()

    next_x.from_minus()
    to_neighbours(1, minus(x), fwd.at[minus(x)])
    next_x.from_plus()
    to_neighbours(2, plus(x), fwd.at[plus(x)])
    next_x.forward()
    own_x.start()

    def make_turn_back(j, carry):
        turn_back[j] = turn_of(j).T.astype(BF16)
        return carry

    lax.fori_loop(0, q_count, make_turn_back, 0)
    next_x.from_beyond()
    to_neighbours(3, beyond(x), fwd.at[beyond(x)])
    own_x.forward()

    def group(h, row):
        return jnp.concatenate([rho_rx[h][held_slot[row * NX + i]] for i in range(NX)], axis=0).T

    def project(row, values, total, first):
        def one(n, carry):
            columns = pl.ds(pl.multiple_of(n * basis, basis), basis)
            block = held[row, :, :, columns].reshape(-1, basis)
            part = jnp.dot(values[...], block, preferred_element_type=F32)
            total[n] = part if first else total[n] + part
            return carry

        lax.fori_loop(0, g_count, one, 0)

    part_sem = sems(4)
    column_sem = sems(g_count)

    def column_copy(d):
        to = (ga + d) % g_count
        columns = pl.ds(pl.multiple_of(to * basis, basis), basis)
        return copy(dmat.at[:, :, columns], dcols.at[ga], column_sem + d, (pb, to))

    def column_start(d, carry):
        column_copy(d).start()
        return carry

    own_columns = pl.ds(pl.multiple_of(ga * basis, basis), basis)
    keep_cols = pltpu.make_async_copy(
        dmat.at[:, :, own_columns], dcols.at[ga], local_sem.at[4]
    )

    for h in parts:
        if h:
            lax.fori_loop(1, g_count, column_start, 0)
            keep_cols.start()

        def rho_wait(d, carry):
            source = (ga + g_count - d) % g_count
            arrive(rho_rx[h].at[pl.ds(source * CAP, CAP)], rho_sem + h * g_count + d)
            return carry

        lax.fori_loop(1, g_count, rho_wait, 0)
        part_tx[h] = group(h, across)
        send(part_tx.at[h], part_rx.at[h], part_sem + h, on_y(across))

    class Reduce:
        def __init__(self, total, landing, outgoing, incoming):
            self.total, self.landing = total, landing
            self.outgoing, self.incoming = outgoing, incoming
            self.i = sems(2 * z_count)

        def to_core(self, k):
            return copy(
                self.total.at[k * NC + (1 - c)], self.landing.at[k], self.i + k, (pb, sibling)
            )

        def start(self):
            for k in range(z_count):
                self.to_core(k).start()

        def sent(self):
            for k in range(z_count):
                self.to_core(k).wait_send()

        def along_z(self):
            for d in (2, 1, 3):
                k = (z + d) % z_count
                arrive(self.landing.at[k], self.i + k)
                self.outgoing[d] = (self.total[k * NC + c] + self.landing[k]).astype(BF16)
                send(
                    self.outgoing.at[d],
                    self.incoming.at[d],
                    self.i + z_count + d,
                    (pb, k * NC + c),
                )
            arrive(self.landing.at[z], self.i + z)

        def finish(self):
            value = self.total[ga] + self.landing[z]
            for d in (1, 3, 2):
                arrive(self.incoming.at[d], self.i + z_count + d)
                value = value + self.incoming[d].astype(F32)
            return value

    reduce1 = [Reduce(acc.at[h], core_rx.at[h], sum_tx.at[h], sum_rx.at[h]) for h in parts]
    reduce2 = [Reduce(acc2.at[h], core_rx2.at[h], sum_tx2.at[h], sum_rx2.at[h]) for h in parts]

    own_x.finish()
    keep.wait()
    def column_wait(d, carry):
        arrive(dcols.at[(ga + g_count - d) % g_count], column_sem + d)
        return carry

    lax.fori_loop(1, g_count, column_wait, 0)
    keep_cols.wait()
    d1_sem, d2_sem = sems(q_count), sems(q_count)

    def spread_copy(d):
        to = (pb + d) % q_count
        return copy(dcols.at[to // 2, to % 2], spread.at[pb], d1_sem + d, (to, ga))

    def spread_start(d, carry):
        spread_copy(d).start()
        return carry

    lax.fori_loop(1, q_count, spread_start, 0)
    keep_d1 = pltpu.make_async_copy(dcols.at[pb // 2, pb % 2], spread.at[pb], local_sem.at[2])
    keep_d1.start()

    for h in parts:
        rho_group[...] = group(h, y)
        project(y, rho_group, acc.at[h], True)
        arrive(part_rx.at[h], part_sem + h)
        project(y, part_rx.at[h], acc2.at[h], True)
        reduce2[h].start()
    reduce2[0].along_z()
    for k, s in enumerate((x, minus(x), plus(x), beyond(x))):
        arrive(held.at[down, s], y_sem + k)
        arrive(held.at[up, s], y_sem + 4 + k)
    for h in parts:
        for row in (down, up):
            rho_group[...] = group(h, row)
            project(row, rho_group, acc.at[h], False)
        reduce1[h].start()
        if h == 0:
            reduce2[1].along_z()
    def spread_wait(d, carry):
        arrive(spread.at[(pb + q_count - d) % q_count], d1_sem + d)
        return carry

    lax.fori_loop(1, q_count, spread_wait, 0)
    keep_d1.wait()

    def choose(q, carry):
        chosen[q] = spread[minus_q[q]]
        return carry

    lax.fori_loop(0, q_count, choose, 0)

    def mate_copy(d):
        to = (pb + d) % q_count
        return copy(chosen.at[to], mate_cols.at[pb], d2_sem + d, (to, ga))

    def mate_start(d, carry):
        mate_copy(d).start()
        return carry

    lax.fori_loop(1, q_count, mate_start, 0)
    keep_d2 = pltpu.make_async_copy(chosen.at[pb], mate_cols.at[pb], local_sem.at[2])
    keep_d2.start()

    for h in parts:
        mate_sum[h, 0] = reduce2[h].finish().astype(BF16)
        send(mate_sum.at[h, 0], mate_sum.at[h, 1], part_sem + 2 + h, on_y(across))
        reduce1[h].along_z()

    class Gather:
        def __init__(self, ref, use):
            self.ref, self.use = ref, use
            self.i = sems(8)

        def start(self):
            mine = self.ref.at[ga]
            for d in (2, 1, 3):
                send(mine, mine, self.i + d, (pb, (z + d) % z_count * NC + c))
            send(mine, mine, self.i, (pb, sibling))

        def own(self):
            self.use(ga)

        def beside(self):
            arrive(self.ref.at[sibling], self.i)
            self.use(sibling)

        def along_z(self):
            for d in (1, 3, 2):
                source = (z + z_count - d) % z_count * NC + c
                there = self.ref.at[source]
                arrive(there, self.i + d)
                send(there, there, self.i + 4 + d, (pb, sibling))
                self.use(source)

        def rest(self):
            for d in (1, 3, 2):
                source = (z + z_count - d) % z_count * NC + (1 - c)
                arrive(self.ref.at[source], self.i + 4 + d)
                self.use(source)

    def apply(h):
        def use(n):
            columns = pl.ds(pl.multiple_of(n * basis, basis), basis)
            slab_sum[h] += jnp.dot(
                own_d[:, columns], coef[h, n], preferred_element_type=F32
            ) + jnp.dot(mate_t[:, columns], coef[h, n], preferred_element_type=F32)

        return use

    gather_coef = [Gather(coef.at[h], apply(h)) for h in parts]
    for h in parts:
        value = reduce1[h].finish()
        arrive(mate_sum.at[h, 1], part_sem + 2 + h)
        coef[h, ga] = (value + mate_sum[h, 1].astype(F32)).astype(BF16).T
        gather_coef[h].start()

    def mate_wait(d, carry):
        arrive(mate_cols.at[(pb + q_count - d) % q_count], d2_sem + d)
        return carry

    lax.fori_loop(1, q_count, mate_wait, 0)
    keep_d2.wait()
    load_d.wait()
    chunk = mate_cols.shape[1]

    def turn_columns(k, carry):
        mate_t[:, pl.ds(pl.multiple_of(k * chunk, chunk), chunk)] = mate_cols[k].T
        return carry

    lax.fori_loop(0, q_count, turn_columns, 0)
    slab_sum[...] = jnp.zeros_like(slab_sum)

    half = NX // 2

    def row_of(k):
        return (y + NX - 1 + k) % NX

    def expand(values, total, first_row, count):
        first = [True]

        def use(n):
            columns = pl.ds(pl.multiple_of(n * basis, basis), basis)
            fresh = first.pop() if first else False

            def one(k, carry):
                block = held[row_of(first_row + k), :, :, columns].reshape(-1, basis)
                value = jnp.dot(block, values[n], preferred_element_type=F32)
                value = value.reshape(half, -1, wide)
                place = pl.ds(k * half, half)
                total[place] = value if fresh else total[place] + value
                return carry

            lax.fori_loop(0, count, one, 0)

        return use

    mate_sem = sems(4)
    gather_own, gather_mate = [], []
    for h in parts:
        gather_own.append(
            Gather(screened.at[h], expand(screened.at[h], acc2.at[h], 0, NX - 1))
        )
        gather_mate.append(Gather(mate_scr.at[h], expand(mate_scr.at[h], acc.at[h], 1, 1)))
    for h in parts:
        gather_coef[h].own()
        gather_coef[h].beside()
    for h in parts:
        gather_coef[h].along_z()
        gather_coef[h].rest()
        screened[h, ga] = (0.5 * slab_sum[h] - coef[h, ga].astype(F32)).astype(BF16)
        send(screened.at[h, ga], mate_scr.at[h, ga], mate_sem + h, on_y(across))
        if h == 0:
            gather_own[h].start()
    for h in parts:
        reduce1[h].sent()
        reduce2[h].sent()
    gather_own[0].own()
    arrive(mate_scr.at[0, ga], mate_sem)
    gather_mate[0].start()

    def rho_sent(d, carry):
        for h in parts:
            rho_copy(h, d).wait_send()
        return carry

    lax.fori_loop(1, g_count, rho_sent, 0)
    back_sem = sems(2 * g_count)

    def back_copy(h, d):
        to = (ga + d) % g_count
        return copy(
            rho_tx.at[h, pl.ds(to * CAP, CAP)],
            back[h].at[pl.ds(ga * CAP, CAP)],
            back_sem + h * g_count + d,
            (pb, to),
        )

    for h in parts:
        if h:
            gather_own[h].own()
        gather_own[h].beside()
        gather_own[h].along_z()
        gather_mate[h].own()
        gather_mate[h].beside()
        gather_mate[h].along_z()
        if h == 0:
            gather_own[1].start()
            arrive(mate_scr.at[1, ga], mate_sem + 1)
            gather_mate[1].start()
        gather_mate[h].rest()
        mate_res[h] = (acc[h, :half] * ratio).astype(BF16).reshape(NX, rows, wide)
        send(mate_res.at[h], res[h].at[pl.ds(y * NX, NX)], mate_sem + 2 + h, on_y(across))
        gather_own[h].rest()

        def finish_rows(k, carry):
            value = (acc2[h, pl.ds(k * half, half)] * ratio).astype(BF16)
            res[h][pl.ds(row_of(k) * NX, NX)] = value.reshape(NX, rows, wide)
            return carry

        lax.fori_loop(0, NX - 1, finish_rows, 0)
        arrive(res[h].at[pl.ds(across * NX, NX)], mate_sem + 2 + h)

        def back_start(k, carry):
            d = (k + 2) % (g_count - 1) + 1
            to = (ga + d) % g_count
            for i in range(CAP):
                rho_tx[h, to * CAP + i] = res[h][held_of_slot[to * CAP + i]]
            back_copy(h, d).start()
            return carry

        lax.fori_loop(0, g_count - 1, back_start, 0)
        for i in range(CAP):
            back[h][ga * CAP + i] = res[h][held_of_slot[ga * CAP + i]]

    for h in parts:

        def back_wait(d, carry):
            source = (ga + g_count - d) % g_count
            arrive(back[h].at[pl.ds(source * CAP, CAP)], back_sem + h * g_count + d)
            return carry

        def unturn(j, carry):
            value = jnp.dot(turn_back[j], back[h][send_slot[j]], preferred_element_type=F32)
            out[j, :, h * wide : (h + 1) * wide] = value.astype(BF16)
            return carry

        lax.fori_loop(1, g_count, back_wait, 0)
        lax.fori_loop(0, q_count, unturn, 0)

    for one in started:
        one.wait_send()

    def drain_pb(d, carry):
        spread_copy(d).wait_send()
        mate_copy(d).wait_send()
        return carry

    def drain_ga(d, carry):
        column_copy(d).wait_send()
        for h in parts:
            back_copy(h, d).wait_send()
        return carry

    lax.fori_loop(1, q_count, drain_pb, 0)
    lax.fori_loop(1, g_count, drain_ga, 0)


def on_device(
    irr_vectors, inv_dielectric, pair_density, minus_q, sym_op, rot_blocks, rot_rows, phase_bits
):
    q_count = lax.axis_size("pb")
    g_count = lax.axis_size("ga")
    owner = lax.axis_index("pb")
    slab_index = lax.axis_index("ga")
    irr_count, block_rows, width = irr_vectors.shape
    density_width = pair_density.shape[2]
    blocks_all = q_count * g_count
    slab_rows = q_count * block_rows
    basis_rows = width // g_count
    slot_count = g_count * CAP
    ratio = math.sqrt(slab_rows * g_count / width)

    operation = lax.dynamic_index_in_dim(sym_op, owner, 0, keepdims=False)
    table = lax.dynamic_index_in_dim(rot_blocks, operation, 0, keepdims=False)
    places = jnp.arange(blocks_all, dtype=jnp.int32)
    source_ga = table % g_count
    earlier = (places[None, :] < places[:, None]) & (
        places[None, :] // q_count == places[:, None] // q_count
    )
    ranks = jnp.sum(
        (earlier & (source_ga[None, :] == source_ga[:, None])).astype(jnp.int32), axis=1
    )
    mine_source = lax.dynamic_slice_in_dim(table, slab_index * q_count, q_count)
    mine_rank = lax.dynamic_slice_in_dim(ranks, slab_index * q_count, q_count)
    send_slot = mine_source % g_count * CAP + mine_rank
    slots = jnp.arange(slot_count, dtype=jnp.int32)
    local = jnp.arange(q_count, dtype=jnp.int32)
    block_of_slot = jnp.sum(
        jnp.where(slots[:, None] == send_slot[None, :], local[None, :], 0), axis=1
    )
    senders = local * g_count + slab_index
    match = table[None, :] == senders[:, None]
    dest_block = jnp.sum(jnp.where(match, places[None, :], 0), axis=1)
    dest_rank = jnp.sum(jnp.where(match, ranks[None, :], 0), axis=1)
    held_slot = dest_block // q_count * CAP + dest_rank
    held_of_slot = jnp.sum(
        jnp.where(slots[:, None] == held_slot[None, :], local[None, :], 0), axis=1
    )

    row_table = lax.dynamic_slice_in_dim(
        lax.dynamic_index_in_dim(rot_rows, operation, 0, keepdims=False),
        slab_index * q_count,
        q_count,
    )
    bits = lax.dynamic_slice_in_dim(
        lax.dynamic_index_in_dim(phase_bits, operation, 0, keepdims=False),
        slab_index * slab_rows,
        slab_rows,
    ).reshape(q_count, block_rows)

    vmem = pltpu.VMEM
    dma = pltpu.SemaphoreType.DMA
    wide = density_width // 2
    slab = (wide, basis_rows)
    square = (basis_rows, wide)
    slots = (slot_count, block_rows, wide)
    chunk = width // q_count
    any_spec = pl.BlockSpec(memory_space=pl.ANY)
    smem_spec = pl.BlockSpec(memory_space=pltpu.SMEM)
    vmem_spec = pl.BlockSpec(memory_space=pltpu.VMEM)

    def run(*operands):
        return pl.pallas_call(
            lambda *refs: kernel(ratio, *refs),
            out_shape=jax.ShapeDtypeStruct((q_count, block_rows, density_width), BF16),
            in_specs=[any_spec] * 4 + [vmem_spec] * 2 + [smem_spec] * 5,
            out_specs=vmem_spec,
            scratch_shapes=[
                vmem((NX, NX, block_rows, width), BF16),
                vmem((NX, block_rows, width), BF16),
                vmem((2, block_rows, width), BF16),
                vmem((2, *slots), BF16),
                vmem(slots, BF16),
                vmem(slots, BF16),
                vmem((wide, NX * block_rows), BF16),
                vmem((2, wide, NX * block_rows), BF16),
                vmem((2, wide, NX * block_rows), BF16),
                vmem((2, g_count, *slab), F32),
                vmem((2, g_count, *slab), F32),
                vmem((2, g_count // NC, *slab), F32),
                vmem((2, g_count // NC, *slab), F32),
                vmem((2, g_count // NC, *slab), BF16),
                vmem((2, g_count // NC, *slab), BF16),
                vmem((2, g_count // NC, *slab), BF16),
                vmem((2, g_count // NC, *slab), BF16),
                vmem((2, 2, *slab), BF16),
                vmem((2, g_count, *square), BF16),
                vmem((2, *square), F32),
                vmem((basis_rows, width), BF16),
                vmem((q_count, chunk, basis_rows), BF16),
                vmem((q_count, chunk, basis_rows), BF16),
                vmem((g_count, 2, chunk, basis_rows), BF16),
                vmem((q_count, chunk, basis_rows), BF16),
                vmem((basis_rows, width), BF16),
                vmem((2, g_count, *square), BF16),
                vmem((2, g_count, *square), BF16),
                vmem((q_count, block_rows, wide), BF16),
                vmem((q_count, block_rows, wide), BF16),
                vmem((2, NX, block_rows, wide), BF16),
                vmem(slots, BF16),
                vmem(slots, BF16),
                vmem((q_count, block_rows, block_rows), BF16),
                dma((5,)),
                dma((SEMS,)),
                dma((SEMS,)),
            ],
            compiler_params=pltpu.CompilerParams(
                collective_id=0, has_side_effects=True, vmem_limit_bytes=62 * 1024 * 1024
            ),
        )(*operands)

    out = run(
        irr_vectors,
        inv_dielectric[0].reshape(2, chunk, width),
        inv_dielectric[0],
        pair_density[0].reshape(q_count, block_rows, density_width),
        row_table,
        bits,
        minus_q,
        block_of_slot,
        held_slot,
        held_of_slot,
        send_slot,
    )
    return out.reshape(1, slab_rows, density_width)


def solution(mesh):
    in_specs = (
        P(None, ("pb", "ga"), None),
        P("pb", "ga", None),
        P("pb", "ga", None),
        P(),
        P(),
        P(),
        P(),
        P(),
    )
    out_specs = P("pb", "ga", None)
    return jax.shard_map(
        on_device, mesh=mesh, in_specs=in_specs, out_specs=out_specs, check_vma=False
    )
```

```python
import math

import jax
import jax.numpy as jnp
from jax import lax
from jax.experimental import pallas as pl
from jax.experimental.pallas import tpu as pltpu
from jax.sharding import PartitionSpec as P

MESH = pl.DeviceIdType.MESH
NX = 4
NC = 2
SEMS = 200
CAP = 3
BF16 = jnp.bfloat16
F32 = jnp.float32


def kernel(
    ratio,
    irr,
    dmat,
    drows,
    density,
    row_table,
    bits,
    minus_q,
    block_of_slot,
    held_slot,
    held_of_slot,
    send_slot,
    out,
    held,
    fwd,
    via_x,
    rho_tx,
    rho_rx_low,
    rho_rx_high,
    rho_group,
    part_tx,
    part_rx,
    acc,
    acc2,
    core_rx,
    core_rx2,
    sum_tx,
    sum_tx2,
    sum_rx,
    sum_rx2,
    mate_sum,
    coef,
    slab_sum,
    own_d,
    spread,
    chosen,
    dcols,
    mate_cols,
    mate_t,
    screened,
    mate_scr,
    res_low,
    res_high,
    mate_res,
    back_low,
    back_high,
    turn_back,
    local_sem,
    send_sem,
    recv_sem,
):
    q_count = lax.axis_size("pb")
    g_count = lax.axis_size("ga")
    pb = lax.axis_index("pb")
    ga = lax.axis_index("ga")
    y, x = pb // NX, pb % NX
    z, c = ga // NC, ga % NC
    z_count = g_count // NC
    sibling = z * NC + (1 - c)
    basis = own_d.shape[0]
    rows = row_table.shape[1]
    plus, minus, beyond = (lambda v: (v + 1) % NX), (lambda v: (v + 3) % NX), (lambda v: (v + 2) % NX)
    ahead, behind = (lambda v: (v + 1 + 2 * c) % NX), (lambda v: (v + 3 - 2 * c) % NX)
    up, down, across = plus(y), minus(y), beyond(y)
    parts = range(2)
    res = (res_low, res_high)
    rho_rx = (rho_rx_low, rho_rx_high)
    back = (back_low, back_high)
    wide = res_low.shape[2]
    started = []
    taken = [0]

    def sems(count):
        first = taken[0]
        taken[0] += count
        assert taken[0] <= SEMS
        return first

    def copy(src, dst, i, to):
        return pltpu.make_async_remote_copy(
            src_ref=src,
            dst_ref=dst,
            send_sem=send_sem.at[i],
            recv_sem=recv_sem.at[i],
            device_id=to,
            device_id_type=MESH,
        )

    def send(src, dst, i, to):
        one = copy(src, dst, i, to)
        one.start()
        started.append(one)

    def arrive(dst, i):
        copy(dst, dst, i, (pb, ga)).wait_recv()

    def on_x(t):
        return (y * NX + t, ga)

    def on_y(t):
        return (t * NX + x, ga)

    class Exchange:
        def __init__(self, me, to, src, dst, via):
            self.me, self.to, self.src, self.dst, self.via = me, to, src, dst, via
            self.i = sems(4)

        def start(self):
            me = self.me
            send(self.src(plus(me)), self.dst(me), self.i, self.to(plus(me)))
            send(self.src(minus(me)), self.dst(me), self.i + 1, self.to(minus(me)))
            send(self.src(beyond(me)), self.via, self.i + 2, self.to(ahead(me)))

        def forward(self):
            arrive(self.via, self.i + 2)
            send(self.via, self.dst(behind(self.me)), self.i + 3, self.to(ahead(self.me)))

        def from_minus(self):
            arrive(self.dst(minus(self.me)), self.i)

        def from_plus(self):
            arrive(self.dst(plus(self.me)), self.i + 1)

        def from_beyond(self):
            arrive(self.dst(beyond(self.me)), self.i + 3)

        def finish(self):
            self.from_minus()
            self.from_plus()
            self.from_beyond()

    load_rho = pltpu.make_async_copy(density, out, local_sem.at[0])
    load_rho.start()

    barrier = pltpu.get_barrier_semaphore()

    def greet_pb(d, carry):
        pl.semaphore_signal(
            barrier, inc=1, device_id=((pb + d) % q_count, ga), device_id_type=MESH
        )
        return carry

    def greet_ga(d, carry):
        pl.semaphore_signal(
            barrier, inc=1, device_id=(pb, (ga + d) % g_count), device_id_type=MESH
        )
        return carry

    lax.fori_loop(1, q_count, greet_pb, 0)
    lax.fori_loop(1, g_count, greet_ga, 0)
    pl.semaphore_wait(barrier, q_count + g_count - 2)

    own_irr = NX * (y % 2)
    next_irr = NX * ((y + 1) % 2)
    next_x = Exchange(x, on_x, lambda t: irr.at[next_irr + t], lambda s: fwd.at[s], via_x.at[0])
    own_x = Exchange(x, on_x, lambda t: irr.at[own_irr + t], lambda s: held.at[y, s], via_x.at[1])
    next_x.start()
    keep = pltpu.make_async_copy(irr.at[own_irr + x], held.at[y, x], local_sem.at[1])
    keep.start()
    y_sem = sems(8)

    def to_neighbours(k, source, src):
        there = held.at[y, source]
        send(src, there, y_sem + k, on_y(up))
        send(src, there, y_sem + 4 + k, on_y(down))

    to_neighbours(0, x, irr.at[next_irr + x])

    def turn_of(j):
        sources = lax.broadcasted_iota(jnp.int32, (rows, rows), 0)
        sign = (1 - 2 * bits[pl.ds(j, 1), :]).astype(F32)
        return jnp.where(row_table[pl.ds(j, 1), :] == sources, sign, 0.0)

    load_rho.wait()
    rho_sem = sems(2 * g_count)

    def rho_copy(h, d):
        to = (ga + d) % g_count
        return copy(
            rho_tx.at[h, pl.ds(to * CAP, CAP)],
            rho_rx[h].at[pl.ds(ga * CAP, CAP)],
            rho_sem + h * g_count + d,
            (pb, to),
        )

    for h in parts:

        def make_turned(j, carry):
            value = jnp.dot(
                turn_of(j).astype(BF16),
                out[j, :, h * wide : (h + 1) * wide],
                preferred_element_type=F32,
            )
            res[h][j] = value.astype(BF16)
            return carry

        def rho_start(k, carry):
            d = (k + 2) % (g_count - 1) + 1
            to = (ga + d) % g_count
            for i in range(CAP):
                rho_tx[h, to * CAP + i] = res[h][block_of_slot[to * CAP + i]]
            rho_copy(h, d).start()
            return carry

        lax.fori_loop(0, q_count, make_turned, 0)
        lax.fori_loop(0, g_count - 1, rho_start, 0)
        for i in range(CAP):
            rho_rx[h][ga * CAP + i] = res[h][block_of_slot[ga * CAP + i]]

    load_d = pltpu.make_async_copy(drows, own_d, local_sem.at[3])
    load_d.start()

    next_x.from_minus()
    to_neighbours(1, minus(x), fwd.at[minus(x)])
    next_x.from_plus()
    to_neighbours(2, plus(x), fwd.at[plus(x)])
    next_x.forward()
    own_x.start()

    def make_turn_back(j, carry):
        turn_back[j] = turn_of(j).T.astype(BF16)
        return carry

    lax.fori_loop(0, q_count, make_turn_back, 0)
    next_x.from_beyond()
    to_neighbours(3, beyond(x), fwd.at[beyond(x)])
    own_x.forward()

    def group(h, row):
        return jnp.concatenate([rho_rx[h][held_slot[row * NX + i]] for i in range(NX)], axis=0).T

    def project(row, values, total, first):
        def one(n, carry):
            columns = pl.ds(pl.multiple_of(n * basis, basis), basis)
            block = held[row, :, :, columns].reshape(-1, basis)
            part = jnp.dot(values[...], block, preferred_element_type=F32)
            total[n] = part if first else total[n] + part
            return carry

        lax.fori_loop(0, g_count, one, 0)

    part_sem = sems(4)
    column_sem = sems(g_count)

    def column_copy(d):
        to = (ga + d) % g_count
        columns = pl.ds(pl.multiple_of(to * basis, basis), basis)
        return copy(dmat.at[:, :, columns], dcols.at[ga], column_sem + d, (pb, to))

    def column_start(d, carry):
        column_copy(d).start()
        return carry

    own_columns = pl.ds(pl.multiple_of(ga * basis, basis), basis)
    keep_cols = pltpu.make_async_copy(
        dmat.at[:, :, own_columns], dcols.at[ga], local_sem.at[4]
    )

    for h in parts:

        def rho_wait(d, carry):
            source = (ga + g_count - d) % g_count
            arrive(rho_rx[h].at[pl.ds(source * CAP, CAP)], rho_sem + h * g_count + d)
            return carry

        lax.fori_loop(1, g_count, rho_wait, 0)
        part_tx[h] = group(h, across)
        send(part_tx.at[h], part_rx.at[h], part_sem + h, on_y(across))

    lax.fori_loop(1, g_count, column_start, 0)
    keep_cols.start()

    class Reduce:
        def __init__(self, total, landing, outgoing, incoming):
            self.total, self.landing = total, landing
            self.outgoing, self.incoming = outgoing, incoming
            self.i = sems(2 * z_count)

        def to_core(self, k):
            return copy(
                self.total.at[k * NC + (1 - c)], self.landing.at[k], self.i + k, (pb, sibling)
            )

        def start(self):
            for k in range(z_count):
                self.to_core(k).start()

        def sent(self):
            for k in range(z_count):
                self.to_core(k).wait_send()

        def along_z(self):
            for d in (2, 1, 3):
                k = (z + d) % z_count
                arrive(self.landing.at[k], self.i + k)
                self.outgoing[d] = (self.total[k * NC + c] + self.landing[k]).astype(BF16)
                send(
                    self.outgoing.at[d],
                    self.incoming.at[d],
                    self.i + z_count + d,
                    (pb, k * NC + c),
                )
            arrive(self.landing.at[z], self.i + z)

        def finish(self):
            value = self.total[ga] + self.landing[z]
            for d in (1, 3, 2):
                arrive(self.incoming.at[d], self.i + z_count + d)
                value = value + self.incoming[d].astype(F32)
            return value

    reduce1 = [Reduce(acc.at[h], core_rx.at[h], sum_tx.at[h], sum_rx.at[h]) for h in parts]
    reduce2 = [Reduce(acc2.at[h], core_rx2.at[h], sum_tx2.at[h], sum_rx2.at[h]) for h in parts]

    own_x.finish()
    keep.wait()
    for h in parts:
        rho_group[...] = group(h, y)
        project(y, rho_group, acc.at[h], True)
        arrive(part_rx.at[h], part_sem + h)
        project(y, part_rx.at[h], acc2.at[h], True)
        reduce2[h].start()
    def column_wait(d, carry):
        arrive(dcols.at[(ga + g_count - d) % g_count], column_sem + d)
        return carry

    lax.fori_loop(1, g_count, column_wait, 0)
    keep_cols.wait()
    d1_sem, d2_sem = sems(q_count), sems(q_count)

    def spread_copy(d):
        to = (pb + d) % q_count
        return copy(dcols.at[to // 2, to % 2], spread.at[pb], d1_sem + d, (to, ga))

    def spread_start(d, carry):
        spread_copy(d).start()
        return carry

    lax.fori_loop(1, q_count, spread_start, 0)
    keep_d1 = pltpu.make_async_copy(dcols.at[pb // 2, pb % 2], spread.at[pb], local_sem.at[2])
    keep_d1.start()

    reduce2[0].along_z()
    for k, s in enumerate((x, minus(x), plus(x), beyond(x))):
        arrive(held.at[down, s], y_sem + k)
        arrive(held.at[up, s], y_sem + 4 + k)
    for h in parts:
        for row in (down, up):
            rho_group[...] = group(h, row)
            project(row, rho_group, acc.at[h], False)
        reduce1[h].start()
        if h == 0:
            reduce2[1].along_z()
    def spread_wait(d, carry):
        arrive(spread.at[(pb + q_count - d) % q_count], d1_sem + d)
        return carry

    lax.fori_loop(1, q_count, spread_wait, 0)
    keep_d1.wait()

    def choose(q, carry):
        chosen[q] = spread[minus_q[q]]
        return carry

    lax.fori_loop(0, q_count, choose, 0)

    def mate_copy(d):
        to = (pb + d) % q_count
        return copy(chosen.at[to], mate_cols.at[pb], d2_sem + d, (to, ga))

    def mate_start(d, carry):
        mate_copy(d).start()
        return carry

    lax.fori_loop(1, q_count, mate_start, 0)
    keep_d2 = pltpu.make_async_copy(chosen.at[pb], mate_cols.at[pb], local_sem.at[2])
    keep_d2.start()

    for h in parts:
        mate_sum[h, 0] = reduce2[h].finish().astype(BF16)
        send(mate_sum.at[h, 0], mate_sum.at[h, 1], part_sem + 2 + h, on_y(across))
        reduce1[h].along_z()

    class Gather:
        def __init__(self, ref, use):
            self.ref, self.use = ref, use
            self.i = sems(8)

        def start(self):
            mine = self.ref.at[ga]
            for d in (2, 1, 3):
                send(mine, mine, self.i + d, (pb, (z + d) % z_count * NC + c))
            send(mine, mine, self.i, (pb, sibling))

        def own(self):
            self.use(ga)

        def beside(self):
            arrive(self.ref.at[sibling], self.i)
            self.use(sibling)

        def along_z(self):
            for d in (1, 3, 2):
                source = (z + z_count - d) % z_count * NC + c
                there = self.ref.at[source]
                arrive(there, self.i + d)
                send(there, there, self.i + 4 + d, (pb, sibling))
                self.use(source)

        def rest(self):
            for d in (1, 3, 2):
                source = (z + z_count - d) % z_count * NC + (1 - c)
                arrive(self.ref.at[source], self.i + 4 + d)
                self.use(source)

    def apply(h):
        def use(n):
            columns = pl.ds(pl.multiple_of(n * basis, basis), basis)
            slab_sum[h] += jnp.dot(
                own_d[:, columns], coef[h, n], preferred_element_type=F32
            ) + jnp.dot(mate_t[:, columns], coef[h, n], preferred_element_type=F32)

        return use

    gather_coef = [Gather(coef.at[h], apply(h)) for h in parts]
    for h in parts:
        value = reduce1[h].finish()
        arrive(mate_sum.at[h, 1], part_sem + 2 + h)
        coef[h, ga] = (value + mate_sum[h, 1].astype(F32)).astype(BF16).T
        gather_coef[h].start()

    def mate_wait(d, carry):
        arrive(mate_cols.at[(pb + q_count - d) % q_count], d2_sem + d)
        return carry

    lax.fori_loop(1, q_count, mate_wait, 0)
    keep_d2.wait()
    load_d.wait()
    chunk = mate_cols.shape[1]

    def turn_columns(k, carry):
        mate_t[:, pl.ds(pl.multiple_of(k * chunk, chunk), chunk)] = mate_cols[k].T
        return carry

    lax.fori_loop(0, q_count, turn_columns, 0)
    slab_sum[...] = jnp.zeros_like(slab_sum)

    half = NX // 2

    def row_of(k):
        return (y + NX - 1 + k) % NX

    def expand(values, total, first_row, count):
        first = [True]

        def use(n):
            columns = pl.ds(pl.multiple_of(n * basis, basis), basis)
            fresh = first.pop() if first else False

            def one(k, carry):
                block = held[row_of(first_row + k), :, :, columns].reshape(-1, basis)
                value = jnp.dot(block, values[n], preferred_element_type=F32)
                value = value.reshape(half, -1, wide)
                place = pl.ds(k * half, half)
                total[place] = value if fresh else total[place] + value
                return carry

            lax.fori_loop(0, count, one, 0)

        return use

    mate_sem = sems(4)
    gather_own, gather_mate = [], []
    for h in parts:
        gather_own.append(
            Gather(screened.at[h], expand(screened.at[h], acc2.at[h], 0, NX - 1))
        )
        gather_mate.append(Gather(mate_scr.at[h], expand(mate_scr.at[h], acc.at[h], 1, 1)))
    for h in parts:
        gather_coef[h].own()
        gather_coef[h].beside()
    for h in parts:
        gather_coef[h].along_z()
        gather_coef[h].rest()
        screened[h, ga] = (0.5 * slab_sum[h] - coef[h, ga].astype(F32)).astype(BF16)
        send(screened.at[h, ga], mate_scr.at[h, ga], mate_sem + h, on_y(across))
        if h == 0:
            gather_own[h].start()
    for h in parts:
        reduce1[h].sent()
        reduce2[h].sent()
    gather_own[0].own()
    arrive(mate_scr.at[0, ga], mate_sem)
    gather_mate[0].start()

    def rho_sent(d, carry):
        for h in parts:
            rho_copy(h, d).wait_send()
        return carry

    lax.fori_loop(1, g_count, rho_sent, 0)
    back_sem = sems(2 * g_count)

    def back_copy(h, d):
        to = (ga + d) % g_count
        return copy(
            rho_tx.at[h, pl.ds(to * CAP, CAP)],
            back[h].at[pl.ds(ga * CAP, CAP)],
            back_sem + h * g_count + d,
            (pb, to),
        )

    for h in parts:
        if h:
            gather_own[h].own()
        gather_own[h].beside()
        gather_own[h].along_z()
        gather_mate[h].own()
        gather_mate[h].beside()
        gather_mate[h].along_z()
        if h == 0:
            gather_own[1].start()
            arrive(mate_scr.at[1, ga], mate_sem + 1)
            gather_mate[1].start()
        gather_mate[h].rest()
        mate_res[h] = (acc[h, :half] * ratio).astype(BF16).reshape(NX, rows, wide)
        send(mate_res.at[h], res[h].at[pl.ds(y * NX, NX)], mate_sem + 2 + h, on_y(across))
        gather_own[h].rest()

        def finish_rows(k, carry):
            value = (acc2[h, pl.ds(k * half, half)] * ratio).astype(BF16)
            res[h][pl.ds(row_of(k) * NX, NX)] = value.reshape(NX, rows, wide)
            return carry

        lax.fori_loop(0, NX - 1, finish_rows, 0)
        arrive(res[h].at[pl.ds(across * NX, NX)], mate_sem + 2 + h)

        def back_start(k, carry):
            d = (k + 2) % (g_count - 1) + 1
            to = (ga + d) % g_count
            for i in range(CAP):
                rho_tx[h, to * CAP + i] = res[h][held_of_slot[to * CAP + i]]
            back_copy(h, d).start()
            return carry

        lax.fori_loop(0, g_count - 1, back_start, 0)
        for i in range(CAP):
            back[h][ga * CAP + i] = res[h][held_of_slot[ga * CAP + i]]

    for h in parts:

        def back_wait(d, carry):
            source = (ga + g_count - d) % g_count
            arrive(back[h].at[pl.ds(source * CAP, CAP)], back_sem + h * g_count + d)
            return carry

        def unturn(j, carry):
            value = jnp.dot(turn_back[j], back[h][send_slot[j]], preferred_element_type=F32)
            out[j, :, h * wide : (h + 1) * wide] = value.astype(BF16)
            return carry

        lax.fori_loop(1, g_count, back_wait, 0)
        lax.fori_loop(0, q_count, unturn, 0)

    for one in started:
        one.wait_send()

    def drain_pb(d, carry):
        spread_copy(d).wait_send()
        mate_copy(d).wait_send()
        return carry

    def drain_ga(d, carry):
        column_copy(d).wait_send()
        for h in parts:
            back_copy(h, d).wait_send()
        return carry

    lax.fori_loop(1, q_count, drain_pb, 0)
    lax.fori_loop(1, g_count, drain_ga, 0)


def on_device(
    irr_vectors, inv_dielectric, pair_density, minus_q, sym_op, rot_blocks, rot_rows, phase_bits
):
    q_count = lax.axis_size("pb")
    g_count = lax.axis_size("ga")
    owner = lax.axis_index("pb")
    slab_index = lax.axis_index("ga")
    irr_count, block_rows, width = irr_vectors.shape
    density_width = pair_density.shape[2]
    blocks_all = q_count * g_count
    slab_rows = q_count * block_rows
    basis_rows = width // g_count
    slot_count = g_count * CAP
    ratio = math.sqrt(slab_rows * g_count / width)

    operation = lax.dynamic_index_in_dim(sym_op, owner, 0, keepdims=False)
    table = lax.dynamic_index_in_dim(rot_blocks, operation, 0, keepdims=False)
    places = jnp.arange(blocks_all, dtype=jnp.int32)
    source_ga = table % g_count
    earlier = (places[None, :] < places[:, None]) & (
        places[None, :] // q_count == places[:, None] // q_count
    )
    ranks = jnp.sum(
        (earlier & (source_ga[None, :] == source_ga[:, None])).astype(jnp.int32), axis=1
    )
    mine_source = lax.dynamic_slice_in_dim(table, slab_index * q_count, q_count)
    mine_rank = lax.dynamic_slice_in_dim(ranks, slab_index * q_count, q_count)
    send_slot = mine_source % g_count * CAP + mine_rank
    slots = jnp.arange(slot_count, dtype=jnp.int32)
    local = jnp.arange(q_count, dtype=jnp.int32)
    block_of_slot = jnp.sum(
        jnp.where(slots[:, None] == send_slot[None, :], local[None, :], 0), axis=1
    )
    senders = local * g_count + slab_index
    match = table[None, :] == senders[:, None]
    dest_block = jnp.sum(jnp.where(match, places[None, :], 0), axis=1)
    dest_rank = jnp.sum(jnp.where(match, ranks[None, :], 0), axis=1)
    held_slot = dest_block // q_count * CAP + dest_rank
    held_of_slot = jnp.sum(
        jnp.where(slots[:, None] == held_slot[None, :], local[None, :], 0), axis=1
    )

    row_table = lax.dynamic_slice_in_dim(
        lax.dynamic_index_in_dim(rot_rows, operation, 0, keepdims=False),
        slab_index * q_count,
        q_count,
    )
    bits = lax.dynamic_slice_in_dim(
        lax.dynamic_index_in_dim(phase_bits, operation, 0, keepdims=False),
        slab_index * slab_rows,
        slab_rows,
    ).reshape(q_count, block_rows)

    vmem = pltpu.VMEM
    dma = pltpu.SemaphoreType.DMA
    wide = density_width // 2
    slab = (wide, basis_rows)
    square = (basis_rows, wide)
    slots = (slot_count, block_rows, wide)
    chunk = width // q_count
    any_spec = pl.BlockSpec(memory_space=pl.ANY)
    smem_spec = pl.BlockSpec(memory_space=pltpu.SMEM)
    vmem_spec = pl.BlockSpec(memory_space=pltpu.VMEM)

    def run(*operands):
        return pl.pallas_call(
            lambda *refs: kernel(ratio, *refs),
            out_shape=jax.ShapeDtypeStruct((q_count, block_rows, density_width), BF16),
            in_specs=[any_spec] * 4 + [vmem_spec] * 2 + [smem_spec] * 5,
            out_specs=vmem_spec,
            scratch_shapes=[
                vmem((NX, NX, block_rows, width), BF16),
                vmem((NX, block_rows, width), BF16),
                vmem((2, block_rows, width), BF16),
                vmem((2, *slots), BF16),
                vmem(slots, BF16),
                vmem(slots, BF16),
                vmem((wide, NX * block_rows), BF16),
                vmem((2, wide, NX * block_rows), BF16),
                vmem((2, wide, NX * block_rows), BF16),
                vmem((2, g_count, *slab), F32),
                vmem((2, g_count, *slab), F32),
                vmem((2, g_count // NC, *slab), F32),
                vmem((2, g_count // NC, *slab), F32),
                vmem((2, g_count // NC, *slab), BF16),
                vmem((2, g_count // NC, *slab), BF16),
                vmem((2, g_count // NC, *slab), BF16),
                vmem((2, g_count // NC, *slab), BF16),
                vmem((2, 2, *slab), BF16),
                vmem((2, g_count, *square), BF16),
                vmem((2, *square), F32),
                vmem((basis_rows, width), BF16),
                vmem((q_count, chunk, basis_rows), BF16),
                vmem((q_count, chunk, basis_rows), BF16),
                vmem((g_count, 2, chunk, basis_rows), BF16),
                vmem((q_count, chunk, basis_rows), BF16),
                vmem((basis_rows, width), BF16),
                vmem((2, g_count, *square), BF16),
                vmem((2, g_count, *square), BF16),
                vmem((q_count, block_rows, wide), BF16),
                vmem((q_count, block_rows, wide), BF16),
                vmem((2, NX, block_rows, wide), BF16),
                vmem(slots, BF16),
                vmem(slots, BF16),
                vmem((q_count, block_rows, block_rows), BF16),
                dma((5,)),
                dma((SEMS,)),
                dma((SEMS,)),
            ],
            compiler_params=pltpu.CompilerParams(
                collective_id=0, has_side_effects=True, vmem_limit_bytes=62 * 1024 * 1024
            ),
        )(*operands)

    out = run(
        irr_vectors,
        inv_dielectric[0].reshape(2, chunk, width),
        inv_dielectric[0],
        pair_density[0].reshape(q_count, block_rows, density_width),
        row_table,
        bits,
        minus_q,
        block_of_slot,
        held_slot,
        held_of_slot,
        send_slot,
    )
    return out.reshape(1, slab_rows, density_width)


def solution(mesh):
    in_specs = (
        P(None, ("pb", "ga"), None),
        P("pb", "ga", None),
        P("pb", "ga", None),
        P(),
        P(),
        P(),
        P(),
        P(),
    )
    out_specs = P("pb", "ga", None)
    return jax.shard_map(
        on_device, mesh=mesh, in_specs=in_specs, out_specs=out_specs, check_vma=False
    )
```

```python
import math

import jax
import jax.numpy as jnp
from jax import lax
from jax.experimental import pallas as pl
from jax.experimental.pallas import tpu as pltpu
from jax.sharding import PartitionSpec as P

MESH = pl.DeviceIdType.MESH
NX = 4
NC = 2
SEMS = 200
CAP = 3
BF16 = jnp.bfloat16
F32 = jnp.float32


def kernel(
    ratio,
    irr,
    dmat,
    drows,
    density,
    row_table,
    bits,
    minus_q,
    block_of_slot,
    held_slot,
    held_of_slot,
    send_slot,
    out,
    held,
    fwd,
    via_x,
    rho_tx,
    rho_rx_low,
    rho_rx_high,
    rho_group,
    part_tx,
    part_rx,
    acc,
    acc2,
    core_rx,
    core_rx2,
    sum_tx,
    sum_tx2,
    sum_rx,
    sum_rx2,
    mate_sum,
    coef,
    slab_sum,
    own_d,
    spread,
    chosen,
    dcols,
    mate_cols,
    mate_t,
    screened,
    mate_scr,
    res_low,
    res_high,
    mate_res,
    back_low,
    back_high,
    turn_back,
    local_sem,
    send_sem,
    recv_sem,
):
    q_count = lax.axis_size("pb")
    g_count = lax.axis_size("ga")
    pb = lax.axis_index("pb")
    ga = lax.axis_index("ga")
    y, x = pb // NX, pb % NX
    z, c = ga // NC, ga % NC
    z_count = g_count // NC
    sibling = z * NC + (1 - c)
    basis = own_d.shape[0]
    rows = row_table.shape[1]
    plus, minus, beyond = (lambda v: (v + 1) % NX), (lambda v: (v + 3) % NX), (lambda v: (v + 2) % NX)
    ahead, behind = (lambda v: (v + 1 + 2 * c) % NX), (lambda v: (v + 3 - 2 * c) % NX)
    up, down, across = plus(y), minus(y), beyond(y)
    parts = range(2)
    res = (res_low, res_high)
    rho_rx = (rho_rx_low, rho_rx_high)
    back = (back_low, back_high)
    wide = res_low.shape[2]
    started = []
    taken = [0]

    def sems(count):
        first = taken[0]
        taken[0] += count
        assert taken[0] <= SEMS
        return first

    def copy(src, dst, i, to):
        return pltpu.make_async_remote_copy(
            src_ref=src,
            dst_ref=dst,
            send_sem=send_sem.at[i],
            recv_sem=recv_sem.at[i],
            device_id=to,
            device_id_type=MESH,
        )

    def send(src, dst, i, to):
        one = copy(src, dst, i, to)
        one.start()
        started.append(one)

    def arrive(dst, i):
        copy(dst, dst, i, (pb, ga)).wait_recv()

    def on_x(t):
        return (y * NX + t, ga)

    def on_y(t):
        return (t * NX + x, ga)

    class Exchange:
        def __init__(self, me, to, src, dst, via):
            self.me, self.to, self.src, self.dst, self.via = me, to, src, dst, via
            self.i = sems(4)

        def start(self):
            me = self.me
            send(self.src(plus(me)), self.dst(me), self.i, self.to(plus(me)))
            send(self.src(minus(me)), self.dst(me), self.i + 1, self.to(minus(me)))
            send(self.src(beyond(me)), self.via, self.i + 2, self.to(ahead(me)))

        def forward(self):
            arrive(self.via, self.i + 2)
            send(self.via, self.dst(behind(self.me)), self.i + 3, self.to(ahead(self.me)))

        def from_minus(self):
            arrive(self.dst(minus(self.me)), self.i)

        def from_plus(self):
            arrive(self.dst(plus(self.me)), self.i + 1)

        def from_beyond(self):
            arrive(self.dst(beyond(self.me)), self.i + 3)

        def finish(self):
            self.from_minus()
            self.from_plus()
            self.from_beyond()

    load_rho = pltpu.make_async_copy(density, out, local_sem.at[0])
    load_rho.start()

    barrier = pltpu.get_barrier_semaphore()

    def greet_pb(d, carry):
        pl.semaphore_signal(
            barrier, inc=1, device_id=((pb + d) % q_count, ga), device_id_type=MESH
        )
        return carry

    def greet_ga(d, carry):
        pl.semaphore_signal(
            barrier, inc=1, device_id=(pb, (ga + d) % g_count), device_id_type=MESH
        )
        return carry

    lax.fori_loop(1, q_count, greet_pb, 0)
    lax.fori_loop(1, g_count, greet_ga, 0)

    def turn_of(j):
        sources = lax.broadcasted_iota(jnp.int32, (rows, rows), 0)
        sign = (1 - 2 * bits[pl.ds(j, 1), :]).astype(F32)
        return jnp.where(row_table[pl.ds(j, 1), :] == sources, sign, 0.0)

    def make_turned(h):
        def one(j, carry):
            value = jnp.dot(
                turn_of(j).astype(BF16),
                out[j, :, h * wide : (h + 1) * wide],
                preferred_element_type=F32,
            )
            res[h][j] = value.astype(BF16)
            return carry

        lax.fori_loop(0, q_count, one, 0)

    load_rho.wait()
    make_turned(0)
    pl.semaphore_wait(barrier, q_count + g_count - 2)

    own_irr = NX * (y % 2)
    next_irr = NX * ((y + 1) % 2)
    next_x = Exchange(x, on_x, lambda t: irr.at[next_irr + t], lambda s: fwd.at[s], via_x.at[0])
    own_x = Exchange(x, on_x, lambda t: irr.at[own_irr + t], lambda s: held.at[y, s], via_x.at[1])
    next_x.start()
    keep = pltpu.make_async_copy(irr.at[own_irr + x], held.at[y, x], local_sem.at[1])
    keep.start()
    y_sem = sems(8)

    def to_neighbours(k, source, src):
        there = held.at[y, source]
        send(src, there, y_sem + k, on_y(up))
        send(src, there, y_sem + 4 + k, on_y(down))

    to_neighbours(0, x, irr.at[next_irr + x])

    rho_sem = sems(2 * g_count)

    def rho_copy(h, d):
        to = (ga + d) % g_count
        return copy(
            rho_tx.at[h, pl.ds(to * CAP, CAP)],
            rho_rx[h].at[pl.ds(ga * CAP, CAP)],
            rho_sem + h * g_count + d,
            (pb, to),
        )

    for h in parts:

        def rho_start(k, carry):
            d = (k + 2) % (g_count - 1) + 1
            to = (ga + d) % g_count
            for i in range(CAP):
                rho_tx[h, to * CAP + i] = res[h][block_of_slot[to * CAP + i]]
            rho_copy(h, d).start()
            return carry

        if h:
            make_turned(h)
        lax.fori_loop(0, g_count - 1, rho_start, 0)
        for i in range(CAP):
            rho_rx[h][ga * CAP + i] = res[h][block_of_slot[ga * CAP + i]]

    load_d = pltpu.make_async_copy(drows, own_d, local_sem.at[3])
    load_d.start()

    next_x.from_minus()
    to_neighbours(1, minus(x), fwd.at[minus(x)])
    next_x.from_plus()
    to_neighbours(2, plus(x), fwd.at[plus(x)])
    next_x.forward()
    own_x.start()

    def make_turn_back(j, carry):
        turn_back[j] = turn_of(j).T.astype(BF16)
        return carry

    lax.fori_loop(0, q_count, make_turn_back, 0)
    next_x.from_beyond()
    to_neighbours(3, beyond(x), fwd.at[beyond(x)])
    own_x.forward()

    def group(h, row):
        return jnp.concatenate([rho_rx[h][held_slot[row * NX + i]] for i in range(NX)], axis=0).T

    def project(row, values, total, first):
        def one(n, carry):
            columns = pl.ds(pl.multiple_of(n * basis, basis), basis)
            block = held[row, :, :, columns].reshape(-1, basis)
            part = jnp.dot(values[...], block, preferred_element_type=F32)
            total[n] = part if first else total[n] + part
            return carry

        lax.fori_loop(0, g_count, one, 0)

    part_sem = sems(4)
    column_sem = sems(g_count)

    def column_copy(d):
        to = (ga + d) % g_count
        columns = pl.ds(pl.multiple_of(to * basis, basis), basis)
        return copy(dmat.at[:, :, columns], dcols.at[ga], column_sem + d, (pb, to))

    def column_start(d, carry):
        column_copy(d).start()
        return carry

    own_columns = pl.ds(pl.multiple_of(ga * basis, basis), basis)
    keep_cols = pltpu.make_async_copy(
        dmat.at[:, :, own_columns], dcols.at[ga], local_sem.at[4]
    )

    for h in parts:

        def rho_wait(d, carry):
            source = (ga + g_count - d) % g_count
            arrive(rho_rx[h].at[pl.ds(source * CAP, CAP)], rho_sem + h * g_count + d)
            return carry

        lax.fori_loop(1, g_count, rho_wait, 0)
        part_tx[h] = group(h, across)
        send(part_tx.at[h], part_rx.at[h], part_sem + h, on_y(across))

    lax.fori_loop(1, g_count, column_start, 0)
    keep_cols.start()

    class Reduce:
        def __init__(self, total, landing, outgoing, incoming):
            self.total, self.landing = total, landing
            self.outgoing, self.incoming = outgoing, incoming
            self.i = sems(2 * z_count)

        def to_core(self, k):
            return copy(
                self.total.at[k * NC + (1 - c)], self.landing.at[k], self.i + k, (pb, sibling)
            )

        def start(self):
            for k in range(z_count):
                self.to_core(k).start()

        def sent(self):
            for k in range(z_count):
                self.to_core(k).wait_send()

        def along_z(self):
            for d in (2, 1, 3):
                k = (z + d) % z_count
                arrive(self.landing.at[k], self.i + k)
                self.outgoing[d] = (self.total[k * NC + c] + self.landing[k]).astype(BF16)
                send(
                    self.outgoing.at[d],
                    self.incoming.at[d],
                    self.i + z_count + d,
                    (pb, k * NC + c),
                )
            arrive(self.landing.at[z], self.i + z)

        def finish(self):
            value = self.total[ga] + self.landing[z]
            for d in (1, 3, 2):
                arrive(self.incoming.at[d], self.i + z_count + d)
                value = value + self.incoming[d].astype(F32)
            return value

    reduce1 = [Reduce(acc.at[h], core_rx.at[h], sum_tx.at[h], sum_rx.at[h]) for h in parts]
    reduce2 = [Reduce(acc2.at[h], core_rx2.at[h], sum_tx2.at[h], sum_rx2.at[h]) for h in parts]

    own_x.finish()
    keep.wait()
    for h in parts:
        rho_group[...] = group(h, y)
        project(y, rho_group, acc.at[h], True)
        arrive(part_rx.at[h], part_sem + h)
        project(y, part_rx.at[h], acc2.at[h], True)
        reduce2[h].start()
    def column_wait(d, carry):
        arrive(dcols.at[(ga + g_count - d) % g_count], column_sem + d)
        return carry

    lax.fori_loop(1, g_count, column_wait, 0)
    keep_cols.wait()
    d1_sem, d2_sem = sems(q_count), sems(q_count)

    def spread_copy(d):
        to = (pb + d) % q_count
        return copy(dcols.at[to // 2, to % 2], spread.at[pb], d1_sem + d, (to, ga))

    def spread_start(d, carry):
        spread_copy(d).start()
        return carry

    lax.fori_loop(1, q_count, spread_start, 0)
    keep_d1 = pltpu.make_async_copy(dcols.at[pb // 2, pb % 2], spread.at[pb], local_sem.at[2])
    keep_d1.start()

    reduce2[0].along_z()
    for k, s in enumerate((x, minus(x), plus(x), beyond(x))):
        arrive(held.at[down, s], y_sem + k)
        arrive(held.at[up, s], y_sem + 4 + k)
    for h in parts:
        for row in (down, up):
            rho_group[...] = group(h, row)
            project(row, rho_group, acc.at[h], False)
        reduce1[h].start()
        if h == 0:
            reduce2[1].along_z()
    def spread_wait(d, carry):
        arrive(spread.at[(pb + q_count - d) % q_count], d1_sem + d)
        return carry

    lax.fori_loop(1, q_count, spread_wait, 0)
    keep_d1.wait()

    def choose(q, carry):
        chosen[q] = spread[minus_q[q]]
        return carry

    lax.fori_loop(0, q_count, choose, 0)

    def mate_copy(d):
        to = (pb + d) % q_count
        return copy(chosen.at[to], mate_cols.at[pb], d2_sem + d, (to, ga))

    def mate_start(d, carry):
        mate_copy(d).start()
        return carry

    lax.fori_loop(1, q_count, mate_start, 0)
    keep_d2 = pltpu.make_async_copy(chosen.at[pb], mate_cols.at[pb], local_sem.at[2])
    keep_d2.start()

    for h in parts:
        mate_sum[h, 0] = reduce2[h].finish().astype(BF16)
        send(mate_sum.at[h, 0], mate_sum.at[h, 1], part_sem + 2 + h, on_y(across))
        reduce1[h].along_z()

    class Gather:
        def __init__(self, ref, use):
            self.ref, self.use = ref, use
            self.i = sems(8)

        def start(self):
            mine = self.ref.at[ga]
            for d in (2, 1, 3):
                send(mine, mine, self.i + d, (pb, (z + d) % z_count * NC + c))
            send(mine, mine, self.i, (pb, sibling))

        def own(self):
            self.use(ga)

        def beside(self):
            arrive(self.ref.at[sibling], self.i)
            self.use(sibling)

        def along_z(self):
            for d in (1, 3, 2):
                source = (z + z_count - d) % z_count * NC + c
                there = self.ref.at[source]
                arrive(there, self.i + d)
                send(there, there, self.i + 4 + d, (pb, sibling))
                self.use(source)

        def rest(self):
            for d in (1, 3, 2):
                source = (z + z_count - d) % z_count * NC + (1 - c)
                arrive(self.ref.at[source], self.i + 4 + d)
                self.use(source)

    def apply(h):
        def use(n):
            columns = pl.ds(pl.multiple_of(n * basis, basis), basis)
            slab_sum[h] += jnp.dot(
                own_d[:, columns], coef[h, n], preferred_element_type=F32
            ) + jnp.dot(mate_t[:, columns], coef[h, n], preferred_element_type=F32)

        return use

    gather_coef = [Gather(coef.at[h], apply(h)) for h in parts]
    for h in parts:
        value = reduce1[h].finish()
        arrive(mate_sum.at[h, 1], part_sem + 2 + h)
        coef[h, ga] = (value + mate_sum[h, 1].astype(F32)).astype(BF16).T
        gather_coef[h].start()

    def mate_wait(d, carry):
        arrive(mate_cols.at[(pb + q_count - d) % q_count], d2_sem + d)
        return carry

    lax.fori_loop(1, q_count, mate_wait, 0)
    keep_d2.wait()
    load_d.wait()
    chunk = mate_cols.shape[1]

    def turn_columns(k, carry):
        mate_t[:, pl.ds(pl.multiple_of(k * chunk, chunk), chunk)] = mate_cols[k].T
        return carry

    lax.fori_loop(0, q_count, turn_columns, 0)
    slab_sum[...] = jnp.zeros_like(slab_sum)

    half = NX // 2

    def row_of(k):
        return (y + NX - 1 + k) % NX

    def expand(values, total, first_row, count):
        first = [True]

        def use(n):
            columns = pl.ds(pl.multiple_of(n * basis, basis), basis)
            fresh = first.pop() if first else False

            def one(k, carry):
                block = held[row_of(first_row + k), :, :, columns].reshape(-1, basis)
                value = jnp.dot(block, values[n], preferred_element_type=F32)
                value = value.reshape(half, -1, wide)
                place = pl.ds(k * half, half)
                total[place] = value if fresh else total[place] + value
                return carry

            lax.fori_loop(0, count, one, 0)

        return use

    mate_sem = sems(4)
    gather_own, gather_mate = [], []
    for h in parts:
        gather_own.append(
            Gather(screened.at[h], expand(screened.at[h], acc2.at[h], 0, NX - 1))
        )
        gather_mate.append(Gather(mate_scr.at[h], expand(mate_scr.at[h], acc.at[h], 1, 1)))
    for h in parts:
        gather_coef[h].own()
        gather_coef[h].beside()
    for h in parts:
        gather_coef[h].along_z()
        gather_coef[h].rest()
        screened[h, ga] = (0.5 * slab_sum[h] - coef[h, ga].astype(F32)).astype(BF16)
        send(screened.at[h, ga], mate_scr.at[h, ga], mate_sem + h, on_y(across))
        if h == 0:
            gather_own[h].start()
    for h in parts:
        reduce1[h].sent()
        reduce2[h].sent()
    gather_own[0].own()
    arrive(mate_scr.at[0, ga], mate_sem)
    gather_mate[0].start()

    def rho_sent(d, carry):
        for h in parts:
            rho_copy(h, d).wait_send()
        return carry

    lax.fori_loop(1, g_count, rho_sent, 0)
    back_sem = sems(2 * g_count)

    def back_copy(h, d):
        to = (ga + d) % g_count
        return copy(
            rho_tx.at[h, pl.ds(to * CAP, CAP)],
            back[h].at[pl.ds(ga * CAP, CAP)],
            back_sem + h * g_count + d,
            (pb, to),
        )

    for h in parts:
        gather_mate[h].own()
        gather_mate[h].beside()
        gather_mate[h].along_z()
        if h == 0:
            gather_own[1].start()
            arrive(mate_scr.at[1, ga], mate_sem + 1)
            gather_mate[1].start()
        gather_mate[h].rest()
        mate_res[h] = (acc[h, :half] * ratio).astype(BF16).reshape(NX, rows, wide)
        send(mate_res.at[h], res[h].at[pl.ds(y * NX, NX)], mate_sem + 2 + h, on_y(across))
        if h:
            gather_own[h].own()
        gather_own[h].beside()
        gather_own[h].along_z()
        gather_own[h].rest()

        def finish_rows(k, carry):
            value = (acc2[h, pl.ds(k * half, half)] * ratio).astype(BF16)
            res[h][pl.ds(row_of(k) * NX, NX)] = value.reshape(NX, rows, wide)
            return carry

        lax.fori_loop(0, NX - 1, finish_rows, 0)
        arrive(res[h].at[pl.ds(across * NX, NX)], mate_sem + 2 + h)

        def back_start(k, carry):
            d = (k + 2) % (g_count - 1) + 1
            to = (ga + d) % g_count
            for i in range(CAP):
                rho_tx[h, to * CAP + i] = res[h][held_of_slot[to * CAP + i]]
            back_copy(h, d).start()
            return carry

        lax.fori_loop(0, g_count - 1, back_start, 0)
        for i in range(CAP):
            back[h][ga * CAP + i] = res[h][held_of_slot[ga * CAP + i]]

    for h in parts:

        def back_wait(d, carry):
            source = (ga + g_count - d) % g_count
            arrive(back[h].at[pl.ds(source * CAP, CAP)], back_sem + h * g_count + d)
            return carry

        def unturn(j, carry):
            value = jnp.dot(turn_back[j], back[h][send_slot[j]], preferred_element_type=F32)
            out[j, :, h * wide : (h + 1) * wide] = value.astype(BF16)
            return carry

        lax.fori_loop(1, g_count, back_wait, 0)
        lax.fori_loop(0, q_count, unturn, 0)

    for one in started:
        one.wait_send()

    def drain_pb(d, carry):
        spread_copy(d).wait_send()
        mate_copy(d).wait_send()
        return carry

    def drain_ga(d, carry):
        column_copy(d).wait_send()
        for h in parts:
            back_copy(h, d).wait_send()
        return carry

    lax.fori_loop(1, q_count, drain_pb, 0)
    lax.fori_loop(1, g_count, drain_ga, 0)


def on_device(
    irr_vectors, inv_dielectric, pair_density, minus_q, sym_op, rot_blocks, rot_rows, phase_bits
):
    q_count = lax.axis_size("pb")
    g_count = lax.axis_size("ga")
    owner = lax.axis_index("pb")
    slab_index = lax.axis_index("ga")
    irr_count, block_rows, width = irr_vectors.shape
    density_width = pair_density.shape[2]
    blocks_all = q_count * g_count
    slab_rows = q_count * block_rows
    basis_rows = width // g_count
    slot_count = g_count * CAP
    ratio = math.sqrt(slab_rows * g_count / width)

    operation = lax.dynamic_index_in_dim(sym_op, owner, 0, keepdims=False)
    table = lax.dynamic_index_in_dim(rot_blocks, operation, 0, keepdims=False)
    places = jnp.arange(blocks_all, dtype=jnp.int32)
    source_ga = table % g_count
    earlier = (places[None, :] < places[:, None]) & (
        places[None, :] // q_count == places[:, None] // q_count
    )
    ranks = jnp.sum(
        (earlier & (source_ga[None, :] == source_ga[:, None])).astype(jnp.int32), axis=1
    )
    mine_source = lax.dynamic_slice_in_dim(table, slab_index * q_count, q_count)
    mine_rank = lax.dynamic_slice_in_dim(ranks, slab_index * q_count, q_count)
    send_slot = mine_source % g_count * CAP + mine_rank
    slots = jnp.arange(slot_count, dtype=jnp.int32)
    local = jnp.arange(q_count, dtype=jnp.int32)
    block_of_slot = jnp.sum(
        jnp.where(slots[:, None] == send_slot[None, :], local[None, :], 0), axis=1
    )
    senders = local * g_count + slab_index
    match = table[None, :] == senders[:, None]
    dest_block = jnp.sum(jnp.where(match, places[None, :], 0), axis=1)
    dest_rank = jnp.sum(jnp.where(match, ranks[None, :], 0), axis=1)
    held_slot = dest_block // q_count * CAP + dest_rank
    held_of_slot = jnp.sum(
        jnp.where(slots[:, None] == held_slot[None, :], local[None, :], 0), axis=1
    )

    row_table = lax.dynamic_slice_in_dim(
        lax.dynamic_index_in_dim(rot_rows, operation, 0, keepdims=False),
        slab_index * q_count,
        q_count,
    )
    bits = lax.dynamic_slice_in_dim(
        lax.dynamic_index_in_dim(phase_bits, operation, 0, keepdims=False),
        slab_index * slab_rows,
        slab_rows,
    ).reshape(q_count, block_rows)

    vmem = pltpu.VMEM
    dma = pltpu.SemaphoreType.DMA
    wide = density_width // 2
    slab = (wide, basis_rows)
    square = (basis_rows, wide)
    slots = (slot_count, block_rows, wide)
    chunk = width // q_count
    any_spec = pl.BlockSpec(memory_space=pl.ANY)
    smem_spec = pl.BlockSpec(memory_space=pltpu.SMEM)
    vmem_spec = pl.BlockSpec(memory_space=pltpu.VMEM)

    def run(*operands):
        return pl.pallas_call(
            lambda *refs: kernel(ratio, *refs),
            out_shape=jax.ShapeDtypeStruct((q_count, block_rows, density_width), BF16),
            in_specs=[any_spec] * 4 + [vmem_spec] * 2 + [smem_spec] * 5,
            out_specs=vmem_spec,
            scratch_shapes=[
                vmem((NX, NX, block_rows, width), BF16),
                vmem((NX, block_rows, width), BF16),
                vmem((2, block_rows, width), BF16),
                vmem((2, *slots), BF16),
                vmem(slots, BF16),
                vmem(slots, BF16),
                vmem((wide, NX * block_rows), BF16),
                vmem((2, wide, NX * block_rows), BF16),
                vmem((2, wide, NX * block_rows), BF16),
                vmem((2, g_count, *slab), F32),
                vmem((2, g_count, *slab), F32),
                vmem((2, g_count // NC, *slab), F32),
                vmem((2, g_count // NC, *slab), F32),
                vmem((2, g_count // NC, *slab), BF16),
                vmem((2, g_count // NC, *slab), BF16),
                vmem((2, g_count // NC, *slab), BF16),
                vmem((2, g_count // NC, *slab), BF16),
                vmem((2, 2, *slab), BF16),
                vmem((2, g_count, *square), BF16),
                vmem((2, *square), F32),
                vmem((basis_rows, width), BF16),
                vmem((q_count, chunk, basis_rows), BF16),
                vmem((q_count, chunk, basis_rows), BF16),
                vmem((g_count, 2, chunk, basis_rows), BF16),
                vmem((q_count, chunk, basis_rows), BF16),
                vmem((basis_rows, width), BF16),
                vmem((2, g_count, *square), BF16),
                vmem((2, g_count, *square), BF16),
                vmem((q_count, block_rows, wide), BF16),
                vmem((q_count, block_rows, wide), BF16),
                vmem((2, NX, block_rows, wide), BF16),
                vmem(slots, BF16),
                vmem(slots, BF16),
                vmem((q_count, block_rows, block_rows), BF16),
                dma((5,)),
                dma((SEMS,)),
                dma((SEMS,)),
            ],
            compiler_params=pltpu.CompilerParams(
                collective_id=0, has_side_effects=True, vmem_limit_bytes=62 * 1024 * 1024
            ),
        )(*operands)

    out = run(
        irr_vectors,
        inv_dielectric[0].reshape(2, chunk, width),
        inv_dielectric[0],
        pair_density[0].reshape(q_count, block_rows, density_width),
        row_table,
        bits,
        minus_q,
        block_of_slot,
        held_slot,
        held_of_slot,
        send_slot,
    )
    return out.reshape(1, slab_rows, density_width)


def solution(mesh):
    in_specs = (
        P(None, ("pb", "ga"), None),
        P("pb", "ga", None),
        P("pb", "ga", None),
        P(),
        P(),
        P(),
        P(),
        P(),
    )
    out_specs = P("pb", "ga", None)
    return jax.shard_map(
        on_device, mesh=mesh, in_specs=in_specs, out_specs=out_specs, check_vma=False
    )
```

```python
import math

import jax
import jax.numpy as jnp
from jax import lax
from jax.experimental import pallas as pl
from jax.experimental.pallas import tpu as pltpu
from jax.sharding import PartitionSpec as P

MESH = pl.DeviceIdType.MESH
NX = 4
NC = 2
SEMS = 200
CAP = 3
BF16 = jnp.bfloat16
F32 = jnp.float32


def kernel(
    ratio,
    irr,
    dmat,
    drows,
    density,
    row_table,
    bits,
    minus_q,
    block_of_slot,
    held_slot,
    held_of_slot,
    send_slot,
    out,
    held,
    fwd,
    via_x,
    rho_tx,
    rho_rx_low,
    rho_rx_high,
    rho_group,
    part_tx,
    part_rx,
    acc,
    acc2,
    core_rx,
    core_rx2,
    sum_tx,
    sum_tx2,
    sum_rx,
    sum_rx2,
    mate_sum,
    coef,
    slab_sum,
    own_d,
    spread,
    chosen,
    dcols,
    mate_cols,
    mate_t,
    screened,
    mate_scr,
    res_low,
    res_high,
    mate_res,
    back_low,
    back_high,
    turn_back,
    local_sem,
    send_sem,
    recv_sem,
):
    q_count = lax.axis_size("pb")
    g_count = lax.axis_size("ga")
    pb = lax.axis_index("pb")
    ga = lax.axis_index("ga")
    y, x = pb // NX, pb % NX
    z, c = ga // NC, ga % NC
    z_count = g_count // NC
    sibling = z * NC + (1 - c)
    basis = own_d.shape[0]
    rows = row_table.shape[1]
    plus, minus, beyond = (lambda v: (v + 1) % NX), (lambda v: (v + 3) % NX), (lambda v: (v + 2) % NX)
    ahead, behind = (lambda v: (v + 1 + 2 * c) % NX), (lambda v: (v + 3 - 2 * c) % NX)
    up, down, across = plus(y), minus(y), beyond(y)
    parts = range(2)
    res = (res_low, res_high)
    rho_rx = (rho_rx_low, rho_rx_high)
    back = (back_low, back_high)
    wide = res_low.shape[2]
    started = []
    taken = [0]

    def sems(count):
        first = taken[0]
        taken[0] += count
        assert taken[0] <= SEMS
        return first

    def copy(src, dst, i, to):
        return pltpu.make_async_remote_copy(
            src_ref=src,
            dst_ref=dst,
            send_sem=send_sem.at[i],
            recv_sem=recv_sem.at[i],
            device_id=to,
            device_id_type=MESH,
        )

    def send(src, dst, i, to):
        one = copy(src, dst, i, to)
        one.start()
        started.append(one)

    def arrive(dst, i):
        copy(dst, dst, i, (pb, ga)).wait_recv()

    def on_x(t):
        return (y * NX + t, ga)

    def on_y(t):
        return (t * NX + x, ga)

    class Exchange:
        def __init__(self, me, to, src, dst, via):
            self.me, self.to, self.src, self.dst, self.via = me, to, src, dst, via
            self.i = sems(4)

        def start(self):
            me = self.me
            send(self.src(plus(me)), self.dst(me), self.i, self.to(plus(me)))
            send(self.src(minus(me)), self.dst(me), self.i + 1, self.to(minus(me)))
            send(self.src(beyond(me)), self.via, self.i + 2, self.to(ahead(me)))

        def forward(self):
            arrive(self.via, self.i + 2)
            send(self.via, self.dst(behind(self.me)), self.i + 3, self.to(ahead(self.me)))

        def from_minus(self):
            arrive(self.dst(minus(self.me)), self.i)

        def from_plus(self):
            arrive(self.dst(plus(self.me)), self.i + 1)

        def from_beyond(self):
            arrive(self.dst(beyond(self.me)), self.i + 3)

        def finish(self):
            self.from_minus()
            self.from_plus()
            self.from_beyond()

    load_rho = pltpu.make_async_copy(density, out, local_sem.at[0])
    load_rho.start()

    barrier = pltpu.get_barrier_semaphore()

    def greet_pb(d, carry):
        pl.semaphore_signal(
            barrier, inc=1, device_id=((pb + d) % q_count, ga), device_id_type=MESH
        )
        return carry

    def greet_ga(d, carry):
        pl.semaphore_signal(
            barrier, inc=1, device_id=(pb, (ga + d) % g_count), device_id_type=MESH
        )
        return carry

    lax.fori_loop(1, q_count, greet_pb, 0)
    lax.fori_loop(1, g_count, greet_ga, 0)
    pl.semaphore_wait(barrier, q_count + g_count - 2)

    own_irr = NX * (y % 2)
    next_irr = NX * ((y + 1) % 2)
    next_x = Exchange(x, on_x, lambda t: irr.at[next_irr + t], lambda s: fwd.at[s], via_x.at[0])
    own_x = Exchange(x, on_x, lambda t: irr.at[own_irr + t], lambda s: held.at[y, s], via_x.at[1])
    next_x.start()
    keep = pltpu.make_async_copy(irr.at[own_irr + x], held.at[y, x], local_sem.at[1])
    keep.start()
    y_sem = sems(8)

    def to_neighbours(k, source, src):
        there = held.at[y, source]
        send(src, there, y_sem + k, on_y(up))
        send(src, there, y_sem + 4 + k, on_y(down))

    to_neighbours(0, x, irr.at[next_irr + x])

    def turn_of(j):
        sources = lax.broadcasted_iota(jnp.int32, (rows, rows), 0)
        sign = (1 - 2 * bits[pl.ds(j, 1), :]).astype(F32)
        return jnp.where(row_table[pl.ds(j, 1), :] == sources, sign, 0.0)

    load_rho.wait()
    rho_sem = sems(2 * g_count)

    def rho_copy(h, d):
        to = (ga + d) % g_count
        return copy(
            rho_tx.at[h, pl.ds(to * CAP, CAP)],
            rho_rx[h].at[pl.ds(ga * CAP, CAP)],
            rho_sem + h * g_count + d,
            (pb, to),
        )

    for h in parts:

        def make_turned(j, carry):
            value = jnp.dot(
                turn_of(j).astype(BF16),
                out[j, :, h * wide : (h + 1) * wide],
                preferred_element_type=F32,
            )
            res[h][j] = value.astype(BF16)
            return carry

        def rho_start(k, carry):
            d = (k + 2) % (g_count - 1) + 1
            to = (ga + d) % g_count
            for i in range(CAP):
                rho_tx[h, to * CAP + i] = res[h][block_of_slot[to * CAP + i]]
            rho_copy(h, d).start()
            return carry

        lax.fori_loop(0, q_count, make_turned, 0)
        lax.fori_loop(0, g_count - 1, rho_start, 0)
        for i in range(CAP):
            rho_rx[h][ga * CAP + i] = res[h][block_of_slot[ga * CAP + i]]

    load_d = pltpu.make_async_copy(drows, own_d, local_sem.at[3])
    load_d.start()

    own_x.start()
    next_x.from_minus()
    to_neighbours(1, minus(x), fwd.at[minus(x)])
    next_x.from_plus()
    to_neighbours(2, plus(x), fwd.at[plus(x)])
    next_x.forward()

    def make_turn_back(j, carry):
        turn_back[j] = turn_of(j).T.astype(BF16)
        return carry

    lax.fori_loop(0, q_count, make_turn_back, 0)
    next_x.from_beyond()
    to_neighbours(3, beyond(x), fwd.at[beyond(x)])
    own_x.forward()

    def group(h, row):
        return jnp.concatenate([rho_rx[h][held_slot[row * NX + i]] for i in range(NX)], axis=0).T

    def project(row, values, total, first):
        def one(n, carry):
            columns = pl.ds(pl.multiple_of(n * basis, basis), basis)
            block = held[row, :, :, columns].reshape(-1, basis)
            part = jnp.dot(values[...], block, preferred_element_type=F32)
            total[n] = part if first else total[n] + part
            return carry

        lax.fori_loop(0, g_count, one, 0)

    part_sem = sems(4)
    column_sem = sems(g_count)

    def column_copy(d):
        to = (ga + d) % g_count
        columns = pl.ds(pl.multiple_of(to * basis, basis), basis)
        return copy(dmat.at[:, :, columns], dcols.at[ga], column_sem + d, (pb, to))

    def column_start(d, carry):
        column_copy(d).start()
        return carry

    own_columns = pl.ds(pl.multiple_of(ga * basis, basis), basis)
    keep_cols = pltpu.make_async_copy(
        dmat.at[:, :, own_columns], dcols.at[ga], local_sem.at[4]
    )

    for h in parts:

        def rho_wait(d, carry):
            source = (ga + g_count - d) % g_count
            arrive(rho_rx[h].at[pl.ds(source * CAP, CAP)], rho_sem + h * g_count + d)
            return carry

        lax.fori_loop(1, g_count, rho_wait, 0)
        part_tx[h] = group(h, across)
        send(part_tx.at[h], part_rx.at[h], part_sem + h, on_y(across))

    lax.fori_loop(1, g_count, column_start, 0)
    keep_cols.start()

    class Reduce:
        def __init__(self, total, landing, outgoing, incoming):
            self.total, self.landing = total, landing
            self.outgoing, self.incoming = outgoing, incoming
            self.i = sems(2 * z_count)

        def to_core(self, k):
            return copy(
                self.total.at[k * NC + (1 - c)], self.landing.at[k], self.i + k, (pb, sibling)
            )

        def start(self):
            for k in range(z_count):
                self.to_core(k).start()

        def sent(self):
            for k in range(z_count):
                self.to_core(k).wait_send()

        def along_z(self):
            for d in (2, 1, 3):
                k = (z + d) % z_count
                arrive(self.landing.at[k], self.i + k)
                self.outgoing[d] = (self.total[k * NC + c] + self.landing[k]).astype(BF16)
                send(
                    self.outgoing.at[d],
                    self.incoming.at[d],
                    self.i + z_count + d,
                    (pb, k * NC + c),
                )
            arrive(self.landing.at[z], self.i + z)

        def finish(self):
            value = self.total[ga] + self.landing[z]
            for d in (1, 3, 2):
                arrive(self.incoming.at[d], self.i + z_count + d)
                value = value + self.incoming[d].astype(F32)
            return value

    reduce1 = [Reduce(acc.at[h], core_rx.at[h], sum_tx.at[h], sum_rx.at[h]) for h in parts]
    reduce2 = [Reduce(acc2.at[h], core_rx2.at[h], sum_tx2.at[h], sum_rx2.at[h]) for h in parts]

    own_x.finish()
    keep.wait()
    for h in parts:
        rho_group[...] = group(h, y)
        project(y, rho_group, acc.at[h], True)
        arrive(part_rx.at[h], part_sem + h)
        project(y, part_rx.at[h], acc2.at[h], True)
        reduce2[h].start()
    def column_wait(d, carry):
        arrive(dcols.at[(ga + g_count - d) % g_count], column_sem + d)
        return carry

    lax.fori_loop(1, g_count, column_wait, 0)
    keep_cols.wait()
    d1_sem, d2_sem = sems(q_count), sems(q_count)

    def spread_copy(d):
        to = (pb + d) % q_count
        return copy(dcols.at[to // 2, to % 2], spread.at[pb], d1_sem + d, (to, ga))

    def spread_start(d, carry):
        spread_copy(d).start()
        return carry

    lax.fori_loop(1, q_count, spread_start, 0)
    keep_d1 = pltpu.make_async_copy(dcols.at[pb // 2, pb % 2], spread.at[pb], local_sem.at[2])
    keep_d1.start()

    reduce2[0].along_z()
    for k, s in enumerate((x, minus(x), plus(x), beyond(x))):
        arrive(held.at[down, s], y_sem + k)
        arrive(held.at[up, s], y_sem + 4 + k)
    for h in parts:
        for row in (down, up):
            rho_group[...] = group(h, row)
            project(row, rho_group, acc.at[h], False)
        reduce1[h].start()
        if h == 0:
            reduce2[1].along_z()
    def spread_wait(d, carry):
        arrive(spread.at[(pb + q_count - d) % q_count], d1_sem + d)
        return carry

    lax.fori_loop(1, q_count, spread_wait, 0)
    keep_d1.wait()

    def choose(q, carry):
        chosen[q] = spread[minus_q[q]]
        return carry

    lax.fori_loop(0, q_count, choose, 0)

    def mate_copy(d):
        to = (pb + d) % q_count
        return copy(chosen.at[to], mate_cols.at[pb], d2_sem + d, (to, ga))

    def mate_start(d, carry):
        mate_copy(d).start()
        return carry

    lax.fori_loop(1, q_count, mate_start, 0)
    keep_d2 = pltpu.make_async_copy(chosen.at[pb], mate_cols.at[pb], local_sem.at[2])
    keep_d2.start()

    for h in parts:
        mate_sum[h, 0] = reduce2[h].finish().astype(BF16)
        send(mate_sum.at[h, 0], mate_sum.at[h, 1], part_sem + 2 + h, on_y(across))
        reduce1[h].along_z()

    class Gather:
        def __init__(self, ref, use):
            self.ref, self.use = ref, use
            self.i = sems(8)

        def start(self):
            mine = self.ref.at[ga]
            for d in (2, 1, 3):
                send(mine, mine, self.i + d, (pb, (z + d) % z_count * NC + c))
            send(mine, mine, self.i, (pb, sibling))

        def own(self):
            self.use(ga)

        def beside(self):
            arrive(self.ref.at[sibling], self.i)
            self.use(sibling)

        def along_z(self):
            for d in (1, 3, 2):
                source = (z + z_count - d) % z_count * NC + c
                there = self.ref.at[source]
                arrive(there, self.i + d)
                send(there, there, self.i + 4 + d, (pb, sibling))
                self.use(source)

        def rest(self):
            for d in (1, 3, 2):
                source = (z + z_count - d) % z_count * NC + (1 - c)
                arrive(self.ref.at[source], self.i + 4 + d)
                self.use(source)

    def apply(h):
        def use(n):
            columns = pl.ds(pl.multiple_of(n * basis, basis), basis)
            slab_sum[h] += jnp.dot(
                own_d[:, columns], coef[h, n], preferred_element_type=F32
            ) + jnp.dot(mate_t[:, columns], coef[h, n], preferred_element_type=F32)

        return use

    gather_coef = [Gather(coef.at[h], apply(h)) for h in parts]
    for h in parts:
        value = reduce1[h].finish()
        arrive(mate_sum.at[h, 1], part_sem + 2 + h)
        coef[h, ga] = (value + mate_sum[h, 1].astype(F32)).astype(BF16).T
        gather_coef[h].start()

    def mate_wait(d, carry):
        arrive(mate_cols.at[(pb + q_count - d) % q_count], d2_sem + d)
        return carry

    lax.fori_loop(1, q_count, mate_wait, 0)
    keep_d2.wait()
    load_d.wait()
    chunk = mate_cols.shape[1]

    def turn_columns(k, carry):
        mate_t[:, pl.ds(pl.multiple_of(k * chunk, chunk), chunk)] = mate_cols[k].T
        return carry

    lax.fori_loop(0, q_count, turn_columns, 0)
    slab_sum[...] = jnp.zeros_like(slab_sum)

    half = NX // 2

    def row_of(k):
        return (y + NX - 1 + k) % NX

    def expand(values, total, first_row, count):
        first = [True]

        def use(n):
            columns = pl.ds(pl.multiple_of(n * basis, basis), basis)
            fresh = first.pop() if first else False

            def one(k, carry):
                block = held[row_of(first_row + k), :, :, columns].reshape(-1, basis)
                value = jnp.dot(block, values[n], preferred_element_type=F32)
                value = value.reshape(half, -1, wide)
                place = pl.ds(k * half, half)
                total[place] = value if fresh else total[place] + value
                return carry

            lax.fori_loop(0, count, one, 0)

        return use

    mate_sem = sems(4)
    gather_own, gather_mate = [], []
    for h in parts:
        gather_own.append(
            Gather(screened.at[h], expand(screened.at[h], acc2.at[h], 0, NX - 1))
        )
        gather_mate.append(Gather(mate_scr.at[h], expand(mate_scr.at[h], acc.at[h], 1, 1)))
    for h in parts:
        gather_coef[h].own()
        gather_coef[h].beside()
    for h in parts:
        gather_coef[h].along_z()
        gather_coef[h].rest()
        screened[h, ga] = (0.5 * slab_sum[h] - coef[h, ga].astype(F32)).astype(BF16)
        send(screened.at[h, ga], mate_scr.at[h, ga], mate_sem + h, on_y(across))
        if h == 0:
            gather_own[h].start()
    for h in parts:
        reduce1[h].sent()
        reduce2[h].sent()
    gather_own[0].own()
    arrive(mate_scr.at[0, ga], mate_sem)
    gather_mate[0].start()

    def rho_sent(d, carry):
        for h in parts:
            rho_copy(h, d).wait_send()
        return carry

    lax.fori_loop(1, g_count, rho_sent, 0)
    back_sem = sems(2 * g_count)

    def back_copy(h, d):
        to = (ga + d) % g_count
        return copy(
            rho_tx.at[h, pl.ds(to * CAP, CAP)],
            back[h].at[pl.ds(ga * CAP, CAP)],
            back_sem + h * g_count + d,
            (pb, to),
        )

    for h in parts:
        if h:
            gather_own[h].own()
        gather_own[h].beside()
        gather_own[h].along_z()
        gather_mate[h].own()
        gather_mate[h].beside()
        gather_mate[h].along_z()
        if h == 0:
            gather_own[1].start()
            arrive(mate_scr.at[1, ga], mate_sem + 1)
            gather_mate[1].start()
        gather_mate[h].rest()
        mate_res[h] = (acc[h, :half] * ratio).astype(BF16).reshape(NX, rows, wide)
        send(mate_res.at[h], res[h].at[pl.ds(y * NX, NX)], mate_sem + 2 + h, on_y(across))
        gather_own[h].rest()

        def finish_rows(k, carry):
            value = (acc2[h, pl.ds(k * half, half)] * ratio).astype(BF16)
            res[h][pl.ds(row_of(k) * NX, NX)] = value.reshape(NX, rows, wide)
            return carry

        lax.fori_loop(0, NX - 1, finish_rows, 0)
        arrive(res[h].at[pl.ds(across * NX, NX)], mate_sem + 2 + h)

        def back_start(k, carry):
            d = (k + 2) % (g_count - 1) + 1
            to = (ga + d) % g_count
            for i in range(CAP):
                rho_tx[h, to * CAP + i] = res[h][held_of_slot[to * CAP + i]]
            back_copy(h, d).start()
            return carry

        lax.fori_loop(0, g_count - 1, back_start, 0)
        for i in range(CAP):
            back[h][ga * CAP + i] = res[h][held_of_slot[ga * CAP + i]]

    for h in parts:

        def back_wait(d, carry):
            source = (ga + g_count - d) % g_count
            arrive(back[h].at[pl.ds(source * CAP, CAP)], back_sem + h * g_count + d)
            return carry

        def unturn(j, carry):
            value = jnp.dot(turn_back[j], back[h][send_slot[j]], preferred_element_type=F32)
            out[j, :, h * wide : (h + 1) * wide] = value.astype(BF16)
            return carry

        lax.fori_loop(1, g_count, back_wait, 0)
        lax.fori_loop(0, q_count, unturn, 0)

    for one in started:
        one.wait_send()

    def drain_pb(d, carry):
        spread_copy(d).wait_send()
        mate_copy(d).wait_send()
        return carry

    def drain_ga(d, carry):
        column_copy(d).wait_send()
        for h in parts:
            back_copy(h, d).wait_send()
        return carry

    lax.fori_loop(1, q_count, drain_pb, 0)
    lax.fori_loop(1, g_count, drain_ga, 0)


def on_device(
    irr_vectors, inv_dielectric, pair_density, minus_q, sym_op, rot_blocks, rot_rows, phase_bits
):
    q_count = lax.axis_size("pb")
    g_count = lax.axis_size("ga")
    owner = lax.axis_index("pb")
    slab_index = lax.axis_index("ga")
    irr_count, block_rows, width = irr_vectors.shape
    density_width = pair_density.shape[2]
    blocks_all = q_count * g_count
    slab_rows = q_count * block_rows
    basis_rows = width // g_count
    slot_count = g_count * CAP
    ratio = math.sqrt(slab_rows * g_count / width)

    operation = lax.dynamic_index_in_dim(sym_op, owner, 0, keepdims=False)
    table = lax.dynamic_index_in_dim(rot_blocks, operation, 0, keepdims=False)
    places = jnp.arange(blocks_all, dtype=jnp.int32)
    source_ga = table % g_count
    earlier = (places[None, :] < places[:, None]) & (
        places[None, :] // q_count == places[:, None] // q_count
    )
    ranks = jnp.sum(
        (earlier & (source_ga[None, :] == source_ga[:, None])).astype(jnp.int32), axis=1
    )
    mine_source = lax.dynamic_slice_in_dim(table, slab_index * q_count, q_count)
    mine_rank = lax.dynamic_slice_in_dim(ranks, slab_index * q_count, q_count)
    send_slot = mine_source % g_count * CAP + mine_rank
    slots = jnp.arange(slot_count, dtype=jnp.int32)
    local = jnp.arange(q_count, dtype=jnp.int32)
    block_of_slot = jnp.sum(
        jnp.where(slots[:, None] == send_slot[None, :], local[None, :], 0), axis=1
    )
    senders = local * g_count + slab_index
    match = table[None, :] == senders[:, None]
    dest_block = jnp.sum(jnp.where(match, places[None, :], 0), axis=1)
    dest_rank = jnp.sum(jnp.where(match, ranks[None, :], 0), axis=1)
    held_slot = dest_block // q_count * CAP + dest_rank
    held_of_slot = jnp.sum(
        jnp.where(slots[:, None] == held_slot[None, :], local[None, :], 0), axis=1
    )

    row_table = lax.dynamic_slice_in_dim(
        lax.dynamic_index_in_dim(rot_rows, operation, 0, keepdims=False),
        slab_index * q_count,
        q_count,
    )
    bits = lax.dynamic_slice_in_dim(
        lax.dynamic_index_in_dim(phase_bits, operation, 0, keepdims=False),
        slab_index * slab_rows,
        slab_rows,
    ).reshape(q_count, block_rows)

    vmem = pltpu.VMEM
    dma = pltpu.SemaphoreType.DMA
    wide = density_width // 2
    slab = (wide, basis_rows)
    square = (basis_rows, wide)
    slots = (slot_count, block_rows, wide)
    chunk = width // q_count
    any_spec = pl.BlockSpec(memory_space=pl.ANY)
    smem_spec = pl.BlockSpec(memory_space=pltpu.SMEM)
    vmem_spec = pl.BlockSpec(memory_space=pltpu.VMEM)

    def run(*operands):
        return pl.pallas_call(
            lambda *refs: kernel(ratio, *refs),
            out_shape=jax.ShapeDtypeStruct((q_count, block_rows, density_width), BF16),
            in_specs=[any_spec] * 4 + [vmem_spec] * 2 + [smem_spec] * 5,
            out_specs=vmem_spec,
            scratch_shapes=[
                vmem((NX, NX, block_rows, width), BF16),
                vmem((NX, block_rows, width), BF16),
                vmem((2, block_rows, width), BF16),
                vmem((2, *slots), BF16),
                vmem(slots, BF16),
                vmem(slots, BF16),
                vmem((wide, NX * block_rows), BF16),
                vmem((2, wide, NX * block_rows), BF16),
                vmem((2, wide, NX * block_rows), BF16),
                vmem((2, g_count, *slab), F32),
                vmem((2, g_count, *slab), F32),
                vmem((2, g_count // NC, *slab), F32),
                vmem((2, g_count // NC, *slab), F32),
                vmem((2, g_count // NC, *slab), BF16),
                vmem((2, g_count // NC, *slab), BF16),
                vmem((2, g_count // NC, *slab), BF16),
                vmem((2, g_count // NC, *slab), BF16),
                vmem((2, 2, *slab), BF16),
                vmem((2, g_count, *square), BF16),
                vmem((2, *square), F32),
                vmem((basis_rows, width), BF16),
                vmem((q_count, chunk, basis_rows), BF16),
                vmem((q_count, chunk, basis_rows), BF16),
                vmem((g_count, 2, chunk, basis_rows), BF16),
                vmem((q_count, chunk, basis_rows), BF16),
                vmem((basis_rows, width), BF16),
                vmem((2, g_count, *square), BF16),
                vmem((2, g_count, *square), BF16),
                vmem((q_count, block_rows, wide), BF16),
                vmem((q_count, block_rows, wide), BF16),
                vmem((2, NX, block_rows, wide), BF16),
                vmem(slots, BF16),
                vmem(slots, BF16),
                vmem((q_count, block_rows, block_rows), BF16),
                dma((5,)),
                dma((SEMS,)),
                dma((SEMS,)),
            ],
            compiler_params=pltpu.CompilerParams(
                collective_id=0, has_side_effects=True, vmem_limit_bytes=62 * 1024 * 1024
            ),
        )(*operands)

    out = run(
        irr_vectors,
        inv_dielectric[0].reshape(2, chunk, width),
        inv_dielectric[0],
        pair_density[0].reshape(q_count, block_rows, density_width),
        row_table,
        bits,
        minus_q,
        block_of_slot,
        held_slot,
        held_of_slot,
        send_slot,
    )
    return out.reshape(1, slab_rows, density_width)


def solution(mesh):
    in_specs = (
        P(None, ("pb", "ga"), None),
        P("pb", "ga", None),
        P("pb", "ga", None),
        P(),
        P(),
        P(),
        P(),
        P(),
    )
    out_specs = P("pb", "ga", None)
    return jax.shard_map(
        on_device, mesh=mesh, in_specs=in_specs, out_specs=out_specs, check_vma=False
    )
```
